32 devices in a mesh: rows: 8 (over z, y), cols: 4 (over x, core).
Axes of the slice: x: 2, y: 2, z: 4, core: 2. Of those that a mesh axis runs over, the one named last changes fastest.
Arguments:
- inputs: bfloat16 [192, 180, 768], P('rows', 'cols'), may hold values from -6 to 6
- valid_mask: int32 [192, 180], P('rows', 'cols'), may hold values from 0 to 1, as said below
- cotangent: bfloat16 [192, 180, 768], P('rows', 'cols'), may hold values from -6 to 6
- first_gain: float32 [768], replicated, may hold values from 0.5 to 1.5
- first_shift: float32 [768], replicated, may hold values from -1.5 to 1.5
- mix_weight_a: bfloat16 [2, 8, 96, 96], replicated, may hold values from -0.4375 to 0.4375
- mix_bias_a: float32 [2, 768], replicated, may hold values from -0.1 to 0.1
- mix_weight_b: bfloat16 [2, 8, 96, 96], replicated, may hold values from -0.4375 to 0.4375
- mix_bias_b: float32 [2, 768], replicated, may hold values from -0.2 to 0.2
- second_gain: float32 [768], replicated, may hold values from 0.5 to 1.5
- second_shift: float32 [768], replicated, may hold values from -1.5 to 1.5
- expand_weight: bfloat16 [768, 3072], replicated, may hold values from -0.21875 to 0.21875
- expand_bias: float32 [3072], replicated, may hold values from -1.5 to 1.5
- reduce_weight: bfloat16 [3072, 768], replicated, may hold values from -0.109375 to 0.109375
- reduce_bias: float32 [768], replicated, may hold values from -1.5 to 1.5
Outputs:
- outputs: float32 [192, 180, 768], P('rows', 'cols')
- grad_inputs: float32 [192, 180, 768], P('rows', 'cols')
- grad_first_gain: float32 [768], replicated
- grad_first_shift: float32 [768], replicated
- grad_mix_weight_a: float32 [2, 8, 96, 96], replicated
- grad_mix_bias_a: float32 [2, 768], replicated
- grad_mix_weight_b: float32 [2, 8, 96, 96], replicated
- grad_mix_bias_b: float32 [2, 768], replicated
- grad_second_gain: float32 [768], replicated
- grad_second_shift: float32 [768], replicated
- grad_expand_weight: float32 [768, 3072], replicated
- grad_expand_bias: float32 [3072], replicated
- grad_reduce_weight: float32 [3072, 768], replicated
- grad_reduce_bias: float32 [768], replicated
The draws below stay inside these ranges and needn't reach their ends.
Inputs may be any that keep to these rules, and one draw needn't show every extreme that they name: `valid_mask`: 1 marks a patch that holds data; rows whose latitude within a snapshot is 90 or more are 0.
All inputs are finite; a program needn't handle non-finite values.
Results may differ from the reference program's by a relative error of at most 0.022.
Values may be sent and summed in bfloat16 or wider, within the bound.
No kernel may reach another device: no remote copies, remote signals or barrier semaphores. Data moves between devices by JAX's collectives and lax.ppermute only.
A program may use at most 256 MiB of HBM per device.

```python
import jax
import jax.numpy as jnp
from jax import lax

D = 768
HIDDEN_SIZE = 3072
BLOCKS = 8
BLOCK = 96
LAT = 96
VALID_LAT = 90
LON = 180
ROWS = 192
SNAPS = 2


def draw_valid_mask(key, part):
    key = jax.random.fold_in(key, 11)
    level_key, roll_key = jax.random.split(key)
    levels = jax.random.randint(level_key, (SNAPS, 1, 1), 0, 10)
    cutoff = levels * levels * levels // 2
    rolls = jax.random.randint(roll_key, (SNAPS, LAT, LON), 0, 1000)
    latitude = jnp.arange(LAT, dtype=jnp.int32)[None, :, None]
    valid = (rolls >= cutoff) & (latitude < VALID_LAT)
    return valid.astype(jnp.int32).reshape(ROWS, LON)


def level_of(key, extent, cuts, least, largest):
    level, own = 1.0, jax.random.fold_in(key, 6)
    for axis_at, parts in cuts:
        draws = jnp.exp(jax.random.uniform(jax.random.fold_in(own, axis_at), (parts,), jnp.float32, least / len(cuts), largest / len(cuts)))
        level = level * jnp.repeat(draws, extent[axis_at] // parts).reshape([-1 if axis == axis_at else 1 for axis in range(len(extent))])
    return level


def gaussian(rng, dims, deviation, reach, cuts=(), held_as=jnp.bfloat16):
    result = deviation * jax.random.normal(rng, dims, jnp.float32)
    if cuts:
        result = result * level_of(rng, dims, cuts, -0.22, 0.18)
    return jnp.clip(result, -reach, reach).astype(held_as)


def setup_inputs(seed: int = 0) -> dict:
    splits = jax.random.split(jax.random.key(seed), 16)
    inputs = gaussian(splits[0], (ROWS, LON, D), 1.0, 6.0, ((0, 8), (1, 4)))
    valid_mask = draw_valid_mask(jax.random.fold_in(splits[15], 71), 0)
    cotangent = gaussian(splits[2], (ROWS, LON, D), 1.0, 6.0, ((0, 8), (1, 4)))
    first_gain = jnp.clip(1.0 + 0.1 * jax.random.normal(splits[3], (D,), jnp.float32), 0.5, 1.5)
    first_shift = gaussian(splits[4], (D,), 0.3, 1.5, (), jnp.float32)
    mix_weight_a = gaussian(splits[5], (2, BLOCKS, BLOCK, BLOCK), (2 * BLOCK) ** -0.5, 0.4375)
    mix_bias_a = gaussian(splits[6], (2, D), 0.02, 0.1, (), jnp.float32)
    mix_weight_b = gaussian(splits[7], (2, BLOCKS, BLOCK, BLOCK), (2 * BLOCK) ** -0.5, 0.4375)
    mix_bias_b = gaussian(splits[8], (2, D), 0.04, 0.2, (), jnp.float32)
    second_gain = jnp.clip(1.0 + 0.1 * jax.random.normal(splits[9], (D,), jnp.float32), 0.5, 1.5)
    second_shift = gaussian(splits[10], (D,), 0.3, 1.5, (), jnp.float32)
    expand_weight = gaussian(splits[11], (D, HIDDEN_SIZE), D ** -0.5, 0.21875)
    expand_bias = gaussian(splits[12], (HIDDEN_SIZE,), 0.3, 1.5, (), jnp.float32)
    reduce_weight = gaussian(splits[13], (HIDDEN_SIZE, D), HIDDEN_SIZE ** -0.5, 0.109375)
    reduce_bias = gaussian(splits[14], (D,), 0.3, 1.5, (), jnp.float32)
    return {"inputs": inputs, "valid_mask": valid_mask, "cotangent": cotangent, "first_gain": first_gain, "first_shift": first_shift, "mix_weight_a": mix_weight_a, "mix_bias_a": mix_bias_a, "mix_weight_b": mix_weight_b, "mix_bias_b": mix_bias_b, "second_gain": second_gain, "second_shift": second_shift, "expand_weight": expand_weight, "expand_bias": expand_bias, "reduce_weight": reduce_weight, "reduce_bias": reduce_bias}


shrink_level = 0.01
shrink_soft = 0.1
norm_eps = 1e-05
best = lax.Precision.HIGHEST

@jax.custom_vjp
def low(v):
    return lax.optimization_barrier(v.astype(jnp.bfloat16)).astype(jnp.float32)

@jax.custom_vjp
def low_back(v):
    return v

def low_keep(v):
    return (low(v), None)

def low_pass(kept, grad):
    return (grad,)

def back_keep(v):
    return (v, None)

def back_low(kept, grad):
    return (low(grad),)
low.defvjp(low_keep, low_pass)
low_back.defvjp(back_keep, back_low)

def layer_norm(source, gain_in, shift_in):
    average = lax.optimization_barrier(jnp.mean(source, axis=-1, keepdims=True))
    centred = source - average
    spread = lax.optimization_barrier(jnp.mean(centred * centred, axis=-1, keepdims=True))
    return centred * lax.rsqrt(spread + norm_eps) * gain_in + shift_in

def block_layer(source_re, source_im, weight, bias_row):
    real_part = jnp.einsum('...bi,bio->...bo', source_re, weight[0], precision=best) - jnp.einsum('...bi,bio->...bo', source_im, weight[1], precision=best)
    imag_part = jnp.einsum('...bi,bio->...bo', source_im, weight[0], precision=best) + jnp.einsum('...bi,bio->...bo', source_re, weight[1], precision=best)
    return (real_part + bias_row[0], imag_part + bias_row[1])

def shrink(values):
    return values - shrink_level * jnp.tanh(values / shrink_soft)

def reference(inputs, valid_mask, cotangent, first_gain, first_shift, mix_weight_a, mix_bias_a, mix_weight_b, mix_bias_b, second_gain, second_shift, expand_weight, expand_bias, reduce_weight, reduce_bias):
    masked = valid_mask.astype(jnp.float32)[:, :, None]
    lon_modes = LON // 2 + 1
    block_size = D // BLOCKS

    def forward(fields, gain_one, shift_one, weight_a, bias_a, weight_b, bias_b, gain_two, shift_two, expand_w, expand_b, reduce_w, reduce_b):
        normed = low(masked * layer_norm(fields, gain_one, shift_one))
        spectral_in = low_back(normed).reshape(SNAPS, LAT, LON, D)
        spectrum = jnp.fft.rfft2(spectral_in, axes=(1, 2), norm='ortho')
        modes_re = low_back(low(jnp.real(spectrum))).reshape(SNAPS, LAT, lon_modes, BLOCKS, block_size)
        modes_im = low_back(low(jnp.imag(spectrum))).reshape(SNAPS, LAT, lon_modes, BLOCKS, block_size)
        pre_re, pre_im = block_layer(modes_re, modes_im, weight_a, bias_a.reshape(2, BLOCKS, block_size))
        hidden_re = low(jax.nn.gelu(low_back(pre_re)))
        hidden_im = low(jax.nn.gelu(low_back(pre_im)))
        second_re, second_im = block_layer(hidden_re, hidden_im, weight_b, bias_b.reshape(2, BLOCKS, block_size))
        second_re = low_back(second_re)
        second_im = low_back(second_im)
        shrunk_re = low_back(low(shrink(second_re)))
        shrunk_im = low_back(low(shrink(second_im)))
        joined = lax.complex(shrunk_re, shrunk_im).reshape(SNAPS, LAT, lon_modes, D)
        spatial = jnp.fft.irfft2(joined, s=(LAT, LON), axes=(1, 2), norm='ortho')
        spatial = low_back(low(spatial.reshape(ROWS, LON, D)))
        residual = fields + normed + masked * spatial
        tokens = low(layer_norm(residual, gain_two, shift_two)).reshape(ROWS * LON, D)
        pre_up = low_back(jnp.dot(tokens, expand_w, precision=best) + expand_b)
        active = low(jax.nn.gelu(pre_up))
        branch = jnp.dot(active, reduce_w, precision=best) + reduce_b
        return residual + branch.reshape(ROWS, LON, D)
    primals = (inputs, first_gain, first_shift, mix_weight_a, mix_bias_a, mix_weight_b, mix_bias_b, second_gain, second_shift, expand_weight, expand_bias, reduce_weight, reduce_bias)
    primals = tuple((member.astype(jnp.float32) for member in primals))
    outputs, pull = jax.vjp(forward, *primals)
    grads = pull(cotangent.astype(jnp.float32))
    return (outputs, grads[0], grads[1], grads[2], grads[3], grads[4], grads[5], grads[6], grads[7], grads[8], grads[9], grads[10], grads[11], grads[12])
```

```python
import math

import jax
import jax.numpy as jnp
import numpy as np
from jax import lax
from jax.experimental import pallas as pl
from jax.experimental.pallas import tpu as pltpu
from jax.sharding import PartitionSpec as P

BLOCKS = 8
LAT = 96
CORES = 2
PACK = 4
LANES = 128

shrink_level = 0.01
shrink_soft = 0.1
norm_eps = 1e-05
gelu_root = math.sqrt(2.0 / math.pi)
gelu_cube = 0.044715

BF = jnp.bfloat16
F32 = jnp.float32
AXES = ("rows", "cols")


def up_to(value, step):
    return (value + step - 1) // step * step


def params(limit=56):
    return pltpu.CompilerParams(vmem_limit_bytes=limit * 1024 * 1024)


def lon_table(lon_size, col_devs, cols_here, cols_pad, slots, slots_pad):
    modes = lon_size // 2 + 1
    table = np.zeros((CORES, 2, slots_pad, col_devs, cols_pad), np.float64)
    weights = np.zeros((CORES, slots_pad), np.float64)
    place = np.arange(lon_size).reshape(col_devs, cols_here)
    for half in range(CORES):
        for slot in range(slots):
            mode = half * slots + slot
            if mode >= modes:
                continue
            angle = (place * mode % lon_size) * (2.0 * math.pi / lon_size)
            table[half, 0, slot, :, :cols_here] = np.cos(angle) / math.sqrt(lon_size)
            edge = mode == 0 or 2 * mode == lon_size
            if not edge:
                table[half, 1, slot, :, :cols_here] = np.sin(angle) / math.sqrt(lon_size)
            weights[half, slot] = 1.0 if edge else 2.0
    weighted = table * weights[:, None, :, None, None]
    rows = 2 * slots_pad
    flat = [a.reshape(CORES, rows, col_devs * cols_pad) for a in (table, weighted)]
    return [
        np.stack([np.concatenate([a[h], a[1 - h]], 0) for h in range(CORES)]) for a in flat
    ]


def lat_table(rows_here, row_group):
    share = rows_here // CORES
    out = []
    for h in range(CORES):
        own = [
            rows_here * r + share * h + i for r in range(row_group) for i in range(share)
        ]
        other = [
            rows_here * r + share * (1 - h) + i for r in range(row_group) for i in range(share)
        ]
        angle = np.outer(np.arange(LAT), np.array(own + other)) % LAT * (2.0 * math.pi / LAT)
        cos, sin = np.cos(angle) / math.sqrt(LAT), np.sin(angle) / math.sqrt(LAT)
        out.append(np.block([[cos, -sin], [-sin, -cos]]))
    return np.stack(out)


def pack_lanes(tiles):
    a, b, c, d = tiles
    lane = lax.broadcasted_iota(jnp.int32, a.shape, a.ndim - 1)
    axis = a.ndim - 1
    b, c, d = pltpu.roll(b, 96, axis), pltpu.roll(c, 64, axis), pltpu.roll(d, 32, axis)
    return [
        jnp.where(lane < 96, a, b),
        jnp.where(lane < 64, b, c),
        jnp.where(lane < 32, c, d),
    ]


def unpack_lanes(tiles):
    a, b, c = tiles
    lane = lax.broadcasted_iota(jnp.int32, a.shape, a.ndim - 1)
    axis = a.ndim - 1
    return [
        a,
        pltpu.roll(jnp.where(lane >= 96, a, b), 32, axis),
        pltpu.roll(jnp.where(lane >= 64, b, c), 64, axis),
        pltpu.roll(c, 96, axis),
    ]


def tiles_of(value):
    return [value[:, LANES * i : LANES * (i + 1)] for i in range(value.shape[1] // LANES)]


def split_blocks(value):
    tiles = tiles_of(value)
    out = []
    for i in range(0, len(tiles), 3):
        out += unpack_lanes(tiles[i : i + 3])
    return out


def join_blocks(tiles):
    out = []
    for i in range(0, len(tiles), 4):
        out += pack_lanes(tiles[i : i + 4])
    return jnp.concatenate(out, axis=1)


def pad_rows(value, rows):
    return jnp.concatenate(
        [value, jnp.zeros((rows - value.shape[0], value.shape[1]), value.dtype)], axis=0
    )


def store_packed(ref, half, per_lat):
    split = [split_blocks(v) for v in per_lat]
    for q in range(BLOCKS):
        packed = pack_lanes([split[j][q] for j in range(PACK)])
        ref[q, half, 0] = jnp.concatenate(packed, axis=1).astype(ref.dtype)


def load_packed(ref, half):
    by_lat = [[] for _ in range(PACK)]
    for q in range(BLOCKS):
        parts = unpack_lanes(tiles_of(ref[q, half, 0].astype(F32)))
        for j in range(PACK):
            by_lat[j].append(parts[j])
    return [join_blocks(tiles) for tiles in by_lat]


def stats(x):
    average = jnp.mean(x, axis=-1, keepdims=True)
    centred = x - average
    spread = jnp.mean(centred * centred, axis=-1, keepdims=True)
    inv = lax.rsqrt(spread + norm_eps)
    return centred * inv, inv


def norm_back(grad, xhat, inv, gain):
    scaled = grad * gain
    m1 = jnp.mean(scaled, axis=-1, keepdims=True)
    m2 = jnp.mean(scaled * xhat, axis=-1, keepdims=True)
    return inv * (scaled - m1 - xhat * m2)


def first_kernel(x_ref, mask_ref, gain_ref, shift_ref, normed_ref, out_ref):
    rows = normed_ref.shape[3]
    for half in range(CORES):
        lats = []
        for j in range(PACK):
            x = pad_rows(x_ref[half, 0, j].astype(F32), rows)
            xhat, _ = stats(x)
            y = mask_ref[half, 0, j] * (xhat * gain_ref[...] + shift_ref[...])
            normed_ref[half, 0, j] = y.astype(BF)
            lats.append(y)
        store_packed(out_ref, half, lats)


def second_kernel(
    x_ref, normed_ref, mask_ref, cot_ref, got_ref, gain_ref, shift_ref, resid_ref, tok_ref, cot_out
):
    rows = normed_ref.shape[3]
    for half in range(CORES):
        spatial = load_packed(got_ref, half)
        for j in range(PACK):
            x = pad_rows(x_ref[half, 0, j].astype(F32), rows)
            resid = x + normed_ref[half, 0, j].astype(F32) + mask_ref[half, 0, j] * spatial[j]
            resid_ref[half, 0, j] = resid
            xhat, _ = stats(resid)
            tok_ref[half, 0, j] = (xhat * gain_ref[...] + shift_ref[...]).astype(BF)
            cot_out[half, 0, j] = pad_rows(cot_ref[half, 0, j].astype(F32), rows).astype(BF)


def third_kernel(
    resid_ref, branch_ref, gtok_ref, cot_ref, mask_ref, gain_ref, bias_ref,
    out_ref, gresid_ref, send_ref, ggain_ref, gshift_ref, gbias_ref,
):
    @pl.when(pl.program_id(0) == 0)
    def _():
        ggain_ref[...] = jnp.zeros_like(ggain_ref)
        gshift_ref[...] = jnp.zeros_like(gshift_ref)
        gbias_ref[...] = jnp.zeros_like(gbias_ref)

    here = out_ref.shape[3]
    for half in range(CORES):
        lats = []
        for j in range(PACK):
            resid = resid_ref[half, 0, j]
            out_ref[half, 0, j] = (resid + branch_ref[half, 0, j] + bias_ref[...])[:here]
            xhat, inv = stats(resid)
            gtok = gtok_ref[half, 0, j]
            cot = cot_ref[half, 0, j].astype(F32)
            ggain_ref[...] += jnp.sum(gtok * xhat, axis=0, keepdims=True)
            gshift_ref[...] += jnp.sum(gtok, axis=0, keepdims=True)
            gbias_ref[...] += jnp.sum(cot, axis=0, keepdims=True)
            gres = cot + norm_back(gtok, xhat, inv, gain_ref[...])
            gresid_ref[half, 0, j] = gres
            lats.append(mask_ref[half, 0, j] * gres)
        store_packed(send_ref, half, lats)


def last_kernel(
    x_ref, gresid_ref, mask_ref, got_ref, gain_ref, out_ref, ggain_ref, gshift_ref
):
    @pl.when(pl.program_id(0) == 0)
    def _():
        ggain_ref[...] = jnp.zeros_like(ggain_ref)
        gshift_ref[...] = jnp.zeros_like(gshift_ref)

    here = out_ref.shape[3]
    rows = gresid_ref.shape[3]
    for half in range(CORES):
        got = load_packed(got_ref, half)
        for j in range(PACK):
            x = pad_rows(x_ref[half, 0, j].astype(F32), rows)
            xhat, inv = stats(x)
            gres = gresid_ref[half, 0, j]
            grad = mask_ref[half, 0, j] * (gres + got[j])
            ggain_ref[...] += jnp.sum(grad * xhat, axis=0, keepdims=True)
            gshift_ref[...] += jnp.sum(grad, axis=0, keepdims=True)
            out_ref[half, 0, j] = (gres + norm_back(grad, xhat, inv, gain_ref[...]))[:here]


def lon_kernel(col_devs, row_group, x_ref, table_ref, own_ref, other_ref, turn_ref):
    groups = x_ref.shape[1]
    rows = table_ref.shape[0]
    lats = own_ref.shape[1]
    slots = own_ref.shape[0]
    for r in range(row_group):
        for g in range(groups):
            cells = jnp.concatenate(
                [x_ref[r * col_devs + c, g] for c in range(col_devs)], axis=0
            )
            modes = jnp.dot(table_ref[...], cells, preferred_element_type=F32)
            for j, tile in enumerate(unpack_lanes(tiles_of(modes))):
                at = (r * groups + g) * PACK + j
                turn_ref[pl.ds(at, rows, stride=lats), :] = tile

    @pl.loop(0, slots)
    def _(s):
        own_ref[s] = turn_ref[pl.ds(pl.multiple_of(s * lats, 8), lats), :].astype(BF)
        other_ref[s] = turn_ref[
            pl.ds(pl.multiple_of((s + slots) * lats, 8), lats), :
        ].astype(BF)


def lon_back_kernel(col_devs, row_group, own_ref, other_ref, table_ref, out_ref):
    groups = out_ref.shape[1]
    cols = out_ref.shape[2]
    for r in range(row_group):
        for g in range(groups):
            tiles = []
            for j in range(0, PACK, 2):
                pair = []
                for k in range(2):
                    at = (r * groups + g) * PACK + j + k
                    pair.append(jnp.concatenate([own_ref[at], other_ref[at]], axis=0))
                cells = jnp.dot(
                    table_ref[...], jnp.concatenate(pair, axis=1), preferred_element_type=F32
                )
                tiles += tiles_of(cells)
            packed = jnp.concatenate(pack_lanes(tiles), axis=1).astype(BF)
            for c in range(col_devs):
                out_ref[r * col_devs + c, g] = packed[c * cols : (c + 1) * cols]


def gelu_parts(v):
    squash = jnp.tanh(gelu_root * (v + gelu_cube * (v * v * v)))
    return squash


def gelu(v):
    return 0.5 * v * (1.0 + gelu_parts(v))


def gelu_slope(v, squash):
    inner = gelu_root * (1.0 + 3.0 * gelu_cube * (v * v))
    return 0.5 * (1.0 + squash) + 0.5 * v * (1.0 - squash * squash) * inner


def latitudes(own_ref, other_ref, slot, half_slots):
    return jnp.concatenate(
        [own_ref[slot], other_ref[slot], own_ref[slot + half_slots], other_ref[slot + half_slots]],
        axis=0,
    )


def turn_out(turn_ref, value, slot, lats, rows, half_slots):
    for part in range(2):
        for dest in range(2):
            piece = value[(2 * part + dest) * lats : (2 * part + dest + 1) * lats]
            start = dest * lats * rows + part * half_slots + slot
            turn_ref[pl.ds(start, lats, stride=rows), :] = piece


def drain(turn_ref, own_ref, other_ref):
    lats, rows = own_ref.shape[0], own_ref.shape[1]

    @pl.loop(0, lats)
    def _(at):
        own_ref[at] = turn_ref[pl.ds(pl.multiple_of(at * rows, 8), rows), :].astype(BF)
        other_ref[at] = turn_ref[
            pl.ds(pl.multiple_of((at + lats) * rows, 8), rows), :
        ].astype(BF)


def mix_kernel(
    own_ref, other_ref, lat_ref, back_ref, wa_ref, ba_ref, wb_ref, bb_ref,
    own_out, other_out, modes_out, turn_ref,
):
    half_slots = own_ref.shape[0] // 2
    lats = own_ref.shape[1]

    @pl.loop(0, half_slots // 2)
    def _(step):
        slot = 2 * step
        cells = jnp.concatenate(
            [latitudes(own_ref, other_ref, slot + k, half_slots) for k in range(2)], axis=1
        )
        full = jnp.dot(lat_ref[...], cells, preferred_element_type=F32).astype(BF)
        real, imag = full[:LAT], full[LAT:]
        modes = jnp.concatenate(
            [
                jnp.concatenate([real[:, :LANES], imag[:, :LANES]], axis=1),
                jnp.concatenate([real[:, LANES:], imag[:, LANES:]], axis=1),
            ],
            axis=0,
        )
        modes_out[step] = modes
        pre_a = jnp.dot(modes, wa_ref[...], preferred_element_type=F32) + ba_ref[...]
        hidden = gelu(pre_a).astype(BF)
        pre_b = jnp.dot(hidden, wb_ref[...], preferred_element_type=F32) + bb_ref[...]
        shrunk = (pre_b - shrink_level * jnp.tanh(pre_b * (1.0 / shrink_soft))).astype(BF)
        mixed = jnp.concatenate(
            [
                jnp.concatenate([shrunk[:LAT, :LANES], shrunk[LAT:, :LANES]], axis=1),
                jnp.concatenate([shrunk[:LAT, LANES:], shrunk[LAT:, LANES:]], axis=1),
            ],
            axis=0,
        )
        back = jnp.dot(back_ref[...], mixed, preferred_element_type=F32)
        for k in range(2):
            turn_out(
                turn_ref, back[:, k * LANES : (k + 1) * LANES], slot + k, lats,
                2 * half_slots, half_slots,
            )

    drain(turn_ref, own_out, other_out)


def mix_back_kernel(
    own_ref, other_ref, modes_ref, lat_ref, back_ref, wa_ref, ba_ref, wb_ref, bb_ref,
    own_out, other_out, gwa_ref, gba_ref, gwb_ref, gbb_ref, turn_ref,
):
    half_slots = own_ref.shape[0] // 2
    lats = own_ref.shape[1]
    for ref in (gwa_ref, gba_ref, gwb_ref, gbb_ref):
        ref[...] = jnp.zeros_like(ref)
    outer = (((0,), (0,)), ((), ()))
    across = (((1,), (1,)), ((), ()))

    @pl.loop(0, half_slots // 2)
    def _(step):
        slot = 2 * step
        cells = jnp.concatenate(
            [latitudes(own_ref, other_ref, slot + k, half_slots) for k in range(2)], axis=1
        )
        full = jnp.dot(lat_ref[...], cells, preferred_element_type=F32)
        real, imag = full[:LAT], full[LAT:]
        grad = jnp.concatenate(
            [
                jnp.concatenate([real[:, :LANES], imag[:, :LANES]], axis=1),
                jnp.concatenate([real[:, LANES:], imag[:, LANES:]], axis=1),
            ],
            axis=0,
        )
        modes = modes_ref[step]
        pre_a = jnp.dot(modes, wa_ref[...], preferred_element_type=F32) + ba_ref[...]
        squash_a = gelu_parts(pre_a)
        hidden = (0.5 * pre_a * (1.0 + squash_a)).astype(BF)
        pre_b = jnp.dot(hidden, wb_ref[...], preferred_element_type=F32) + bb_ref[...]
        squash_b = jnp.tanh(pre_b * (1.0 / shrink_soft))
        factor = 1.0 - shrink_level / shrink_soft * (1.0 - squash_b * squash_b)
        grad_b = factor * grad
        gbb_ref[...] += jnp.sum(grad_b, axis=0, keepdims=True)
        grad_b = grad_b.astype(BF)
        grad_hidden = lax.dot_general(grad_b, wb_ref[...], across, preferred_element_type=F32)
        gwb_ref[...] += lax.dot_general(hidden, grad_b, outer, preferred_element_type=F32)
        grad_a = gelu_slope(pre_a, squash_a) * grad_hidden
        gba_ref[...] += jnp.sum(grad_a, axis=0, keepdims=True)
        grad_a = grad_a.astype(BF)
        grad_modes = lax.dot_general(
            grad_a, wa_ref[...], across, preferred_element_type=F32
        ).astype(BF)
        gwa_ref[...] += lax.dot_general(modes, grad_a, outer, preferred_element_type=F32)
        mixed = jnp.concatenate(
            [
                jnp.concatenate([grad_modes[:LAT, :LANES], grad_modes[LAT:, :LANES]], axis=1),
                jnp.concatenate([grad_modes[:LAT, LANES:], grad_modes[LAT:, LANES:]], axis=1),
            ],
            axis=0,
        )
        back = jnp.dot(back_ref[...], mixed, preferred_element_type=F32)
        for k in range(2):
            turn_out(
                turn_ref, back[:, k * LANES : (k + 1) * LANES], slot + k, lats,
                2 * half_slots, half_slots,
            )

    drain(turn_ref, own_out, other_out)


def per_device(
    inputs, valid_mask, cotangent, first_gain, first_shift, mix_weight_a, mix_bias_a,
    mix_weight_b, mix_bias_b, second_gain, second_shift, expand_weight, expand_bias,
    reduce_weight, reduce_bias,
):
    row_devs = lax.axis_size("rows")
    col_devs = lax.axis_size("cols")
    rows_here, cols_here, channels = inputs.shape
    block = channels // BLOCKS
    lon_size = cols_here * col_devs
    cols_pad = up_to(cols_here, 16)
    row_group = LAT // rows_here
    members = row_group * col_devs
    share = rows_here // CORES
    groups = share // PACK
    slots = (lon_size // 2 + 2) // 2
    slots_pad = up_to(slots, 16)
    lats = share * row_group
    half_rows = 2 * slots_pad
    all_rows = CORES * half_rows
    assert members == CORES * BLOCKS and block * PACK == 3 * LANES
    assert col_devs * cols_pad == all_rows and CORES * lats == LAT

    row_at, col_at = lax.axis_index("rows"), lax.axis_index("cols")
    core = col_at % CORES
    mine = (row_at % row_group) * (col_devs // CORES) + col_at // CORES

    def pick(table):
        return lax.dynamic_index_in_dim(jnp.asarray(table, BF), core, 0, keepdims=False)

    plain_np, weighted_np = lon_table(
        lon_size, col_devs, cols_here, cols_pad, slots, slots_pad
    )
    lat_np = lat_table(rows_here, row_group)
    lon_fwd, lon_wfwd = pick(plain_np), pick(weighted_np)
    lon_inv, lon_winv = (
        pick(np.swapaxes(plain_np, 1, 2)), pick(np.swapaxes(weighted_np, 1, 2))
    )
    lat_fwd, lat_inv = pick(lat_np), pick(np.swapaxes(lat_np, 1, 2))

    snap_groups = [
        [(s * row_group + r) * col_devs + c for r in range(row_group) for c in range(col_devs)]
        for s in range(row_devs // row_group)
    ]
    core_pairs = [
        (r * col_devs + c, r * col_devs + c ^ 1) for r in range(row_devs) for c in range(col_devs)
    ]

    def exchange(x):
        return lax.all_to_all(x, AXES, 0, 0, axis_index_groups=snap_groups, tiled=True)

    def swap(x):
        return lax.ppermute(x, AXES, core_pairs)

    def fold(x):
        return x.reshape((CORES, groups, PACK) + x.shape[1:])

    def row(v):
        return v.reshape(1, -1)

    mask = jnp.pad(
        valid_mask.astype(F32), ((0, 0), (0, cols_pad - cols_here))
    )[:, :, None]
    mask = fold(mask)
    x5, cot5 = fold(inputs), fold(cotangent)

    def lat_spec(cols, width):
        return pl.BlockSpec((CORES, 1, PACK, cols, width), lambda i: (0, i, 0, 0, 0))

    packed_spec = pl.BlockSpec(
        (BLOCKS, CORES, 1, cols_pad, 3 * LANES), lambda i: (0, 0, i, 0, 0)
    )
    row_spec = pl.BlockSpec((1, channels), lambda i: (0, 0))
    here_spec, pad_spec, mask_spec = (
        lat_spec(cols_here, channels), lat_spec(cols_pad, channels), lat_spec(cols_pad, 1)
    )
    packed_shape = (BLOCKS, CORES, groups, cols_pad, 3 * LANES)
    flat_shape = (members, groups, cols_pad, 3 * LANES)
    pad_shape = (CORES, groups, PACK, cols_pad, channels)
    here_shape = (CORES, groups, PACK, cols_here, channels)

    def shape(s, d):
        return jax.ShapeDtypeStruct(s, d)

    def lon_forward(cells, table):
        return pl.pallas_call(
            lambda *refs: lon_kernel(col_devs, row_group, *refs),
            out_shape=[shape((half_rows, lats, LANES), BF)] * 2,
            scratch_shapes=[pltpu.VMEM((all_rows * lats, LANES), F32)],
            compiler_params=params(),
            name="lon_forward",
        )(cells.reshape(flat_shape), table)

    def lon_backward(own, other, table):
        return pl.pallas_call(
            lambda *refs: lon_back_kernel(col_devs, row_group, *refs),
            out_shape=shape(flat_shape, BF),
            compiler_params=params(),
            name="lon_backward",
        )(own, other, table)

    def big_weight(w):
        w = lax.dynamic_index_in_dim(w, mine, 1, keepdims=False)
        gap = LANES - block
        w = jnp.pad(w, ((0, 0), (0, gap), (0, gap)))
        return jnp.concatenate(
            [jnp.concatenate([w[0], w[1]], 1), jnp.concatenate([-w[1], w[0]], 1)], 0
        )

    def big_bias(b):
        b = lax.dynamic_index_in_dim(b.reshape(2, BLOCKS, block), mine, 1, keepdims=False)
        return jnp.pad(b, ((0, 0), (0, LANES - block))).reshape(1, 2 * LANES)

    wa, wb = big_weight(mix_weight_a), big_weight(mix_weight_b)
    ba, bb = big_bias(mix_bias_a), big_bias(mix_bias_b)

    normed, send = pl.pallas_call(
        first_kernel,
        grid=(groups,),
        in_specs=[here_spec, mask_spec, row_spec, row_spec],
        out_specs=[pad_spec, packed_spec],
        out_shape=[shape(pad_shape, BF), shape(packed_shape, BF)],
        compiler_params=params(),
        name="first_norm",
    )(x5, mask, row(first_gain), row(first_shift))
    cells = exchange(send.reshape(flat_shape))

    own, other = lon_forward(cells, lon_fwd)
    other = swap(other)
    turn_scratch = [pltpu.VMEM((2 * lats * half_rows, LANES), F32)]
    lat_out = [shape((lats, half_rows, LANES), BF)] * 2
    own, other, modes = pl.pallas_call(
        mix_kernel,
        out_shape=lat_out + [shape((slots_pad // 2, 2 * LAT, 2 * LANES), BF)],
        scratch_shapes=turn_scratch,
        compiler_params=params(),
        name="mix",
    )(own, other, lat_fwd, lat_inv, wa, ba, wb, bb)
    other = swap(other)
    got = exchange(lon_backward(own, other, lon_winv))

    resid, tokens, cot_pad = pl.pallas_call(
        second_kernel,
        grid=(groups,),
        in_specs=[here_spec, pad_spec, mask_spec, here_spec, packed_spec, row_spec, row_spec],
        out_specs=[pad_spec, pad_spec, pad_spec],
        out_shape=[shape(pad_shape, F32), shape(pad_shape, BF), shape(pad_shape, BF)],
        compiler_params=params(),
        name="second_norm",
    )(x5, normed, mask, cot5, got.reshape(packed_shape), row(second_gain), row(second_shift))
    tokens2 = tokens.reshape(-1, channels)
    cot2 = cot_pad.reshape(-1, channels)
    pre_up = jnp.dot(tokens2, expand_weight, preferred_element_type=F32) + expand_bias
    squash = gelu_parts(pre_up)
    active = (0.5 * pre_up * (1.0 + squash)).astype(BF)
    branch = jnp.dot(active, reduce_weight, preferred_element_type=F32)
    outer = (((0,), (0,)), ((), ()))
    across = (((1,), (1,)), ((), ()))
    grad_reduce = lax.dot_general(active, cot2, outer, preferred_element_type=F32)
    grad_active = lax.dot_general(cot2, reduce_weight, across, preferred_element_type=F32)
    grad_pre = (gelu_slope(pre_up, squash) * grad_active).astype(BF)
    grad_expand = lax.dot_general(tokens2, grad_pre, outer, preferred_element_type=F32)
    grad_expand_bias = jnp.sum(grad_pre.astype(F32), axis=0)
    grad_tokens = lax.dot_general(grad_pre, expand_weight, across, preferred_element_type=F32)

    one_row = shape((1, channels), F32)
    outputs, grad_resid, send, g_gain2, g_shift2, g_rbias = pl.pallas_call(
        third_kernel,
        grid=(groups,),
        in_specs=[pad_spec, pad_spec, pad_spec, pad_spec, mask_spec, row_spec, row_spec],
        out_specs=[here_spec, pad_spec, packed_spec, row_spec, row_spec, row_spec],
        out_shape=[shape(here_shape, F32), shape(pad_shape, F32), shape(packed_shape, BF)]
        + [one_row] * 3,
        compiler_params=params(),
        name="second_back",
    )(
        resid, branch.reshape(pad_shape), grad_tokens.reshape(pad_shape), cot_pad, mask,
        row(second_gain), row(reduce_bias),
    )
    cells = exchange(send.reshape(flat_shape))

    own, other = lon_forward(cells, lon_wfwd)
    other = swap(other)
    square = shape((2 * LANES, 2 * LANES), F32)
    line = shape((1, 2 * LANES), F32)
    own, other, g_wa, g_ba, g_wb, g_bb = pl.pallas_call(
        mix_back_kernel,
        out_shape=lat_out + [square, line, square, line],
        scratch_shapes=turn_scratch,
        compiler_params=params(),
        name="mix_back",
    )(own, other, modes, lat_fwd, lat_inv, wa, ba, wb, bb)
    other = swap(other)
    got = exchange(lon_backward(own, other, lon_inv))

    grad_inputs, g_gain1, g_shift1 = pl.pallas_call(
        last_kernel,
        grid=(groups,),
        in_specs=[here_spec, pad_spec, mask_spec, packed_spec, row_spec],
        out_specs=[here_spec, row_spec, row_spec],
        out_shape=[shape(here_shape, F32)] + [one_row] * 2,
        compiler_params=params(),
        name="first_back",
    )(x5, grad_resid, mask, got.reshape(packed_shape), row(first_gain))

    def small_weight(g):
        rr, ri = g[:block, :block], g[:block, LANES : LANES + block]
        ir, ii = g[LANES : LANES + block, :block], g[LANES : LANES + block, LANES : LANES + block]
        pair = jnp.stack([rr + ii, ri - ir])[:, None]
        return lax.dynamic_update_slice(
            jnp.zeros((2, BLOCKS, block, block), F32), pair, (0, mine, 0, 0)
        )

    def small_bias(g):
        pair = g.reshape(2, 1, LANES)[:, :, :block]
        full = lax.dynamic_update_slice(jnp.zeros((2, BLOCKS, block), F32), pair, (0, mine, 0))
        return full.reshape(2, channels)

    big = lax.psum((grad_expand.astype(BF), grad_reduce.astype(BF)), AXES)
    g_expand, g_reduce = big[0].astype(F32), big[1].astype(F32)
    (g_gain1, g_shift1, g_wa, g_ba, g_wb, g_bb, g_gain2, g_shift2, g_ebias, g_rbias) = lax.psum(
        (
            g_gain1, g_shift1, small_weight(g_wa), small_bias(g_ba), small_weight(g_wb),
            small_bias(g_bb), g_gain2, g_shift2, grad_expand_bias, g_rbias,
        ),
        AXES,
    )

    def flat(v):
        return v.reshape(-1)

    return (
        outputs.reshape(inputs.shape), grad_inputs.reshape(inputs.shape),
        flat(g_gain1), flat(g_shift1), g_wa, g_ba, g_wb, g_bb, flat(g_gain2), flat(g_shift2),
        g_expand, g_ebias, g_reduce, flat(g_rbias),
    )


def solution(mesh):
    grid = P("rows", "cols", None)
    placed = (grid, P("rows", "cols"), grid) + (P(),) * 12
    return jax.shard_map(
        per_device,
        mesh=mesh,
        in_specs=placed,
        out_specs=(grid, grid) + (P(),) * 12,
        check_vma=False,
    )
```

```python
import math

import jax
import jax.numpy as jnp
import numpy as np
from jax import lax
from jax.experimental import pallas as pl
from jax.experimental.pallas import tpu as pltpu
from jax.sharding import PartitionSpec as P

BLOCKS = 8
LAT = 96
CORES = 2
PACK = 4
LANES = 128

shrink_level = 0.01
shrink_soft = 0.1
norm_eps = 1e-05
gelu_root = math.sqrt(2.0 / math.pi)
gelu_cube = 0.044715

BF = jnp.bfloat16
F32 = jnp.float32
AXES = ("rows", "cols")


def up_to(value, step):
    return (value + step - 1) // step * step


def call(kernel, args, out_shape, us, after=(), in_specs=None, prefetch=(), vmem=12, **kw):
    outs = out_shape if isinstance(out_shape, (list, tuple)) else [out_shape]
    lead, n_in, n_after = len(prefetch), len(args), len(after)

    def body(*refs):
        kernel(*refs[: lead + n_in], *refs[lead + n_in + n_after :])

    grid = kw.pop("grid", (1,))
    whole = lambda x: pl.BlockSpec(x.shape, lambda *_, n=len(x.shape): (0,) * n)
    specs = list(in_specs) if in_specs is not None else [whole(a) for a in args]
    specs += [pl.BlockSpec(memory_space=pl.ANY)] * n_after
    out_specs = kw.pop("out_specs", None) or [whole(o) for o in outs]
    got = pl.pallas_call(
        body,
        grid_spec=pltpu.PrefetchScalarGridSpec(
            num_scalar_prefetch=lead,
            grid=grid,
            in_specs=specs,
            out_specs=out_specs,
            scratch_shapes=kw.pop("scratch_shapes", ()),
        ),
        out_shape=outs,
        compiler_params=pltpu.CompilerParams(vmem_limit_bytes=vmem * 1024 * 1024),
        cost_estimate=pl.CostEstimate(
            flops=0, bytes_accessed=int(us * 1e5), transcendentals=0
        ),
        **kw,
    )(*prefetch, *args, *after)
    return list(got) if isinstance(out_shape, (list, tuple)) else got[0]


SPLIT = 3


def lon_table(lon_size, col_devs, cols_here, cols_pad, slots, slots_pad):
    modes = lon_size // 2 + 1
    table = np.zeros((CORES, 2, slots_pad, col_devs, cols_pad), np.float64)
    weights = np.zeros((CORES, slots_pad), np.float64)
    place = np.arange(lon_size).reshape(col_devs, cols_here)
    for half in range(CORES):
        for slot in range(slots):
            mode = half * slots + slot
            if mode >= modes:
                continue
            angle = (place * mode % lon_size) * (2.0 * math.pi / lon_size)
            table[half, 0, slot, :, :cols_here] = np.cos(angle) / math.sqrt(lon_size)
            edge = mode == 0 or 2 * mode == lon_size
            if not edge:
                table[half, 1, slot, :, :cols_here] = np.sin(angle) / math.sqrt(lon_size)
            weights[half, slot] = 1.0 if edge else 2.0
    weighted = table * weights[:, None, :, None, None]
    rows = 2 * slots_pad
    flat = [
        a.reshape(CORES, 2, SPLIT, slots_pad // SPLIT, col_devs, cols_pad)
        .swapaxes(1, 2)
        .reshape(CORES, rows, col_devs * cols_pad)
        for a in (table, weighted)
    ]
    return [
        np.stack([np.concatenate([a[h], a[1 - h]], 0) for h in range(CORES)]) for a in flat
    ]


def lat_table(rows_here, row_group):
    share = rows_here // CORES
    out = []
    for h in range(CORES):
        own = [
            rows_here * r + share * h + i for r in range(row_group) for i in range(share)
        ]
        other = [
            rows_here * r + share * (1 - h) + i for r in range(row_group) for i in range(share)
        ]
        angle = np.outer(np.arange(LAT), np.array(own + other)) % LAT * (2.0 * math.pi / LAT)
        cos, sin = np.cos(angle) / math.sqrt(LAT), np.sin(angle) / math.sqrt(LAT)
        out.append(np.block([[cos, -sin], [-sin, -cos]]))
    return np.stack(out)


def pack_lanes(tiles):
    a, b, c, d = tiles
    lane = lax.broadcasted_iota(jnp.int32, a.shape, a.ndim - 1)
    axis = a.ndim - 1
    b, c, d = pltpu.roll(b, 96, axis), pltpu.roll(c, 64, axis), pltpu.roll(d, 32, axis)
    return [
        jnp.where(lane < 96, a, b),
        jnp.where(lane < 64, b, c),
        jnp.where(lane < 32, c, d),
    ]


def unpack_lanes(tiles):
    a, b, c = tiles
    lane = lax.broadcasted_iota(jnp.int32, a.shape, a.ndim - 1)
    axis = a.ndim - 1
    return [
        a,
        pltpu.roll(jnp.where(lane >= 96, a, b), 32, axis),
        pltpu.roll(jnp.where(lane >= 64, b, c), 64, axis),
        pltpu.roll(c, 96, axis),
    ]


def tiles_of(value):
    return [value[:, LANES * i : LANES * (i + 1)] for i in range(value.shape[1] // LANES)]


def split_blocks(value):
    tiles = tiles_of(value)
    out = []
    for i in range(0, len(tiles), 3):
        out += unpack_lanes(tiles[i : i + 3])
    return out


def join_blocks(tiles):
    out = []
    for i in range(0, len(tiles), 4):
        out += pack_lanes(tiles[i : i + 4])
    return jnp.concatenate(out, axis=1)


def pad_rows(value, rows):
    return jnp.concatenate(
        [value, jnp.zeros((rows - value.shape[0], value.shape[1]), value.dtype)], axis=0
    )


def store_packed(ref, half, per_lat):
    split = [split_blocks(v) for v in per_lat]
    for q in range(BLOCKS):
        packed = pack_lanes([split[j][q] for j in range(PACK)])
        ref[q, half, 0] = jnp.concatenate(packed, axis=1).astype(ref.dtype)


def load_packed(ref, half):
    by_lat = [[] for _ in range(PACK)]
    for q in range(BLOCKS):
        parts = unpack_lanes(tiles_of(ref[q, half, 0].astype(F32)))
        for j in range(PACK):
            by_lat[j].append(parts[j])
    return [join_blocks(tiles) for tiles in by_lat]


def stats(x):
    average = jnp.mean(x, axis=-1, keepdims=True)
    centred = x - average
    spread = jnp.mean(centred * centred, axis=-1, keepdims=True)
    inv = lax.rsqrt(spread + norm_eps)
    return centred * inv, inv


def norm_back(grad, xhat, inv, gain):
    scaled = grad * gain
    m1 = jnp.mean(scaled, axis=-1, keepdims=True)
    m2 = jnp.mean(scaled * xhat, axis=-1, keepdims=True)
    return inv * (scaled - m1 - xhat * m2)


def first_kernel(x_ref, mask_ref, gain_ref, shift_ref, normed_ref, out_ref):
    rows = normed_ref.shape[3]
    for half in range(CORES):
        lats = []
        for j in range(PACK):
            x = pad_rows(x_ref[half, 0, j].astype(F32), rows)
            xhat, _ = stats(x)
            y = mask_ref[half, 0, j] * (xhat * gain_ref[...] + shift_ref[...])
            normed_ref[half, 0, j] = y.astype(BF)
            lats.append(y)
        store_packed(out_ref, half, lats)


def second_kernel(
    x_ref, normed_ref, mask_ref, cot_ref, got_ref, gain_ref, shift_ref, resid_ref, tok_ref, cot_out
):
    rows = normed_ref.shape[3]
    for half in range(CORES):
        spatial = load_packed(got_ref, half)
        for j in range(PACK):
            x = pad_rows(x_ref[half, 0, j].astype(F32), rows)
            resid = x + normed_ref[half, 0, j].astype(F32) + mask_ref[half, 0, j] * spatial[j]
            resid_ref[half, 0, j] = resid
            xhat, _ = stats(resid)
            tok_ref[half, 0, j] = (xhat * gain_ref[...] + shift_ref[...]).astype(BF)
            cot_out[half, 0, j] = pad_rows(cot_ref[half, 0, j].astype(F32), rows).astype(BF)


def third_kernel(
    resid_ref, gtok_ref, cot_ref, mask_ref, gain_ref,
    gresid_ref, send_ref, ggain_ref, gshift_ref, gbias_ref,
):
    @pl.when(pl.program_id(0) == 0)
    def _():
        ggain_ref[...] = jnp.zeros_like(ggain_ref)
        gshift_ref[...] = jnp.zeros_like(gshift_ref)
        gbias_ref[...] = jnp.zeros_like(gbias_ref)

    for half in range(CORES):
        lats = []
        for j in range(PACK):
            xhat, inv = stats(resid_ref[half, 0, j])
            gtok = gtok_ref[half, 0, j]
            cot = cot_ref[half, 0, j].astype(F32)
            ggain_ref[...] += jnp.sum(gtok * xhat, axis=0, keepdims=True)
            gshift_ref[...] += jnp.sum(gtok, axis=0, keepdims=True)
            gbias_ref[...] += jnp.sum(cot, axis=0, keepdims=True)
            gres = cot + norm_back(gtok, xhat, inv, gain_ref[...])
            gresid_ref[half, 0, j] = gres
            lats.append(mask_ref[half, 0, j] * gres)
        store_packed(send_ref, half, lats)


def last_kernel(
    x_ref, gresid_ref, mask_ref, got_ref, gain_ref, out_ref, ggain_ref, gshift_ref
):
    @pl.when(pl.program_id(0) == 0)
    def _():
        ggain_ref[...] = jnp.zeros_like(ggain_ref)
        gshift_ref[...] = jnp.zeros_like(gshift_ref)

    here = out_ref.shape[3]
    rows = gresid_ref.shape[3]
    for half in range(CORES):
        got = load_packed(got_ref, half)
        for j in range(PACK):
            x = pad_rows(x_ref[half, 0, j].astype(F32), rows)
            xhat, inv = stats(x)
            gres = gresid_ref[half, 0, j]
            grad = mask_ref[half, 0, j] * (gres + got[j])
            ggain_ref[...] += jnp.sum(grad * xhat, axis=0, keepdims=True)
            gshift_ref[...] += jnp.sum(grad, axis=0, keepdims=True)
            out_ref[half, 0, j] = (gres + norm_back(grad, xhat, inv, gain_ref[...]))[:here]


OUTER = (((0,), (0,)), ((), ()))
ACROSS = (((1,), (1,)), ((), ()))


def chain_kernel(
    tok_ref, cot_ref, up_ref, bias_ref, down_ref, act_ref, gpre_ref, gtok_ref, gbias_ref
):
    @pl.when(pl.program_id(0) == 0)
    def _():
        gtok_ref[...] = jnp.zeros_like(gtok_ref)

    pre = jnp.dot(tok_ref[...], up_ref[...], preferred_element_type=F32) + bias_ref[...]
    squash = gelu_parts(pre)
    act_ref[...] = (0.5 * pre * (1.0 + squash)).astype(BF)
    gact = lax.dot_general(cot_ref[...], down_ref[...], ACROSS, preferred_element_type=F32)
    gpre = gelu_slope(pre, squash) * gact
    gbias_ref[...] = jnp.sum(gpre, axis=0, keepdims=True)
    gpre = gpre.astype(BF)
    gpre_ref[...] = gpre
    gtok_ref[...] += lax.dot_general(gpre, up_ref[...], ACROSS, preferred_element_type=F32)


def split_store(value, tiles, sent_ref, kept_ref):
    @pl.when(pl.program_id(0) < tiles)
    def _():
        sent_ref[...] = value

    @pl.when(pl.program_id(0) >= tiles)
    def _():
        kept_ref[...] = value


def weight_grad_kernel(core_ref, act_ref, cot_ref, sent_ref, kept_ref):
    value = lax.dot_general(act_ref[...], cot_ref[...], OUTER, preferred_element_type=F32)
    split_store(value.astype(BF), pl.num_programs(0) // 2, sent_ref, kept_ref)


def branch_kernel(act_ref, down_ref, resid_ref, bias_ref, out_ref):
    cols, here = resid_ref.shape[3], out_ref.shape[3]
    rows = CORES * PACK * cols
    act = act_ref[...].reshape(rows, act_ref.shape[-1])
    branch = jnp.dot(act, down_ref[...], preferred_element_type=F32) + bias_ref[...]
    for half in range(CORES):
        for j in range(PACK):
            at = (half * PACK + j) * cols
            out_ref[half, 0, j] = (resid_ref[half, 0, j] + branch[at : at + cols])[:here]


def plus(left, right):
    return (left.astype(F32) + right.astype(F32)).astype(BF)


def halve_first_kernel(bits_ref, *refs):
    count = len(refs) // 6
    for p in range(count):
        a, b, c, d = refs[4 * p : 4 * p + 4]
        low, high = plus(a[...], b[...]), plus(c[...], d[...])
        first = bits_ref[p] == 0
        refs[4 * count + 2 * p][...] = jnp.where(first, low, high)
        refs[4 * count + 2 * p + 1][...] = jnp.where(first, high, low)


def halve_kernel(bits_ref, *refs):
    count = len(refs) // 6
    for k in range(2 * count):
        refs[4 * count + k][...] = plus(refs[2 * k][...], refs[2 * k + 1][...])


def join_kernel(count, *refs):
    for p in range(count):
        n = refs[2 * p].shape[0]
        value = plus(refs[2 * p][...], refs[2 * p + 1][...])
        for out in refs[-2:]:
            out[p * n : (p + 1) * n] = value


def part_kernel(kept, got, *outs):
    n, count = outs[0].shape[0], len(outs) // 2
    for p in range(count):
        rows = slice(p * n, (p + 1) * n)
        value = plus(kept[rows], got[rows])
        outs[p][...] = value
        outs[count + p][...] = value


def add_kernel(left, right, *outs):
    value = left[...].astype(F32) + right[...].astype(F32)
    for out in outs:
        out[...] = value.astype(out.dtype)


def tail_kernel(*refs):
    for out in refs[-2:]:
        at = 0
        for ref in refs[:-2]:
            out[:, at : at + ref.shape[1]] = ref[...]
            at += ref.shape[1]


def merge_kernel(count, single, bits_ref, *refs):
    outs = refs[2 * count :]
    for p in range(count):
        own, got = refs[2 * p], refs[2 * p + 1]
        n = own.shape[0]
        for out in (outs[p::count] if not single else [o.at[p] for o in outs]):
            out[pl.ds(pl.multiple_of(bits_ref[p] * n, 16), n), :] = own[...]
            out[pl.ds(pl.multiple_of((1 - bits_ref[p]) * n, 16), n), :] = got[...]


def widen_kernel(core_ref, reduce_ref, expand_ref, *refs):
    reduce_out, expand_out = refs[-2:]
    reduce_out[...] = reduce_ref[...].astype(F32)
    expand_out[...] = expand_ref[...].astype(F32).T


def collect_kernel(block, *refs):
    n = (len(refs) - 1) // SPLIT
    out = refs[-1]
    out[...] = jnp.zeros_like(out)
    for i in range(n // 2):
        g = sum(refs[n * k + 2 * i][...] for k in range(SPLIT))
        line = sum(refs[n * k + 2 * i + 1][...] for k in range(SPLIT))
        top, low = g[:block], g[LANES : LANES + block]
        at = 2 * i * block
        out[at : at + block] = top[:, :LANES] + low[:, LANES:]
        out[at + block : at + 2 * block] = top[:, LANES:] - low[:, :LANES]
        base = n * block + 2 * i
        out[base : base + 1] = line[:, :LANES]
        out[base + 1 : base + 2] = line[:, LANES:]


def spread_kernel(block, x_ref, wa_ref, wb_ref, ba_ref, bb_ref):
    for i, (w, b) in enumerate(((wa_ref, ba_ref), (wb_ref, bb_ref))):
        for part in range(2):
            row = 4 * block + 2 * i + part
            tiles = []
            for q in range(BLOCKS):
                at = (2 * i + part) * block
                w[part, q] = x_ref[q, at : at + block, :block].astype(F32)
                tail = x_ref[q, 4 * block :, :].astype(F32)
                tiles.append(tail[2 * i + part : 2 * i + part + 1])
            b[part : part + 1, :] = join_blocks(tiles)


def lon_kernel(col_devs, row_group, x_ref, table_ref, own_ref, other_ref, turn_ref):
    groups = x_ref.shape[1]
    rows = table_ref.shape[0]
    lats = own_ref.shape[1]
    slots = own_ref.shape[0]
    for r in range(row_group):
        for g in range(groups):
            cells = jnp.concatenate(
                [x_ref[r * col_devs + c, g] for c in range(col_devs)], axis=0
            )
            modes = jnp.dot(table_ref[...], cells, preferred_element_type=F32)
            for j, tile in enumerate(unpack_lanes(tiles_of(modes))):
                at = (r * groups + g) * PACK + j
                turn_ref[pl.ds(at, rows, stride=lats), :] = tile

    @pl.loop(0, slots)
    def _(s):
        own_ref[s] = turn_ref[pl.ds(pl.multiple_of(s * lats, 8), lats), :].astype(BF)
        other_ref[s] = turn_ref[
            pl.ds(pl.multiple_of((s + slots) * lats, 8), lats), :
        ].astype(BF)


def lon_back_kernel(col_devs, row_group, pieces, table_ref, *refs):
    out_ref = refs[pieces]
    groups = out_ref.shape[1]
    cols = out_ref.shape[2]
    for r in range(row_group):
        for g in range(groups):
            tiles = []
            for j in range(0, PACK, 2):
                pair = []
                for k in range(2):
                    at = (r * groups + g) * PACK + j + k
                    pair.append(jnp.concatenate([r_[at] for r_ in refs[:pieces]], axis=0))
                cells = jnp.dot(
                    table_ref[...], jnp.concatenate(pair, axis=1), preferred_element_type=F32
                )
                tiles += tiles_of(cells)
            packed = jnp.concatenate(pack_lanes(tiles), axis=1).astype(BF)
            for c in range(col_devs):
                out_ref[r * col_devs + c, g] = packed[c * cols : (c + 1) * cols]


def gelu_parts(v):
    squash = jnp.tanh(gelu_root * (v + gelu_cube * (v * v * v)))
    return squash


def gelu(v):
    return 0.5 * v * (1.0 + gelu_parts(v))


def gelu_slope(v, squash):
    inner = gelu_root * (1.0 + 3.0 * gelu_cube * (v * v))
    return 0.5 * (1.0 + squash) + 0.5 * v * (1.0 - squash * squash) * inner


def latitudes(own_ref, other_ref, row, run):
    return jnp.concatenate(
        [own_ref[row], other_ref[row], own_ref[row + run], other_ref[row + run]], axis=0
    )


def turn_out(turn_ref, value, row, lats, rows, run):
    for part in range(2):
        for dest in range(2):
            piece = value[(2 * part + dest) * lats : (2 * part + dest + 1) * lats]
            start = dest * lats * rows + part * run + row
            turn_ref[pl.ds(start, lats, stride=rows), :] = piece


def drain(turn_ref, own_ref, other_ref):
    lats, rows = own_ref.shape[0], own_ref.shape[1]

    @pl.loop(0, lats)
    def _(at):
        own_ref[at] = turn_ref[pl.ds(pl.multiple_of(at * rows, 8), rows), :].astype(BF)
        other_ref[at] = turn_ref[
            pl.ds(pl.multiple_of((at + lats) * rows, 8), rows), :
        ].astype(BF)


def mix_kernel(
    own_ref, other_ref, lat_ref, back_ref, wa_ref, ba_ref, wb_ref, bb_ref,
    own_out, other_out, modes_out, turn_ref,
):
    lats, rows = own_ref.shape[1], own_ref.shape[0]
    run = rows // 2 // SPLIT

    @pl.loop(0, rows // 4)
    def _(step):
        slot = 2 * step
        row = slot + slot // run * run
        cells = jnp.concatenate(
            [latitudes(own_ref, other_ref, row + k, run) for k in range(2)], axis=1
        )
        full = jnp.dot(lat_ref[...], cells, preferred_element_type=F32).astype(BF)
        real, imag = full[:LAT], full[LAT:]
        modes = jnp.concatenate(
            [
                jnp.concatenate([real[:, :LANES], imag[:, :LANES]], axis=1),
                jnp.concatenate([real[:, LANES:], imag[:, LANES:]], axis=1),
            ],
            axis=0,
        )
        modes_out[step] = modes
        pre_a = jnp.dot(modes, wa_ref[...], preferred_element_type=F32) + ba_ref[...]
        hidden = gelu(pre_a).astype(BF)
        pre_b = jnp.dot(hidden, wb_ref[...], preferred_element_type=F32) + bb_ref[...]
        shrunk = (pre_b - shrink_level * jnp.tanh(pre_b * (1.0 / shrink_soft))).astype(BF)
        mixed = jnp.concatenate(
            [
                jnp.concatenate([shrunk[:LAT, :LANES], shrunk[LAT:, :LANES]], axis=1),
                jnp.concatenate([shrunk[:LAT, LANES:], shrunk[LAT:, LANES:]], axis=1),
            ],
            axis=0,
        )
        back = jnp.dot(back_ref[...], mixed, preferred_element_type=F32)
        for k in range(2):
            turn_out(turn_ref, back[:, k * LANES : (k + 1) * LANES], row + k, lats, rows, run)

    drain(turn_ref, own_out, other_out)


def mix_back_kernel(
    own_ref, other_ref, modes_ref, lat_ref, back_ref, wa_ref, ba_ref, wb_ref, bb_ref,
    own_out, other_out, gwa_ref, gba_ref, gwb_ref, gbb_ref, turn_ref,
):
    lats, rows = own_ref.shape[1], own_ref.shape[0]
    run = rows // 2
    for ref in (gwa_ref, gba_ref, gwb_ref, gbb_ref):
        ref[...] = jnp.zeros_like(ref)

    @pl.loop(0, run // 2)
    def _(step):
        row = 2 * step
        cells = jnp.concatenate(
            [latitudes(own_ref, other_ref, row + k, run) for k in range(2)], axis=1
        )
        full = jnp.dot(lat_ref[...], cells, preferred_element_type=F32)
        real, imag = full[:LAT], full[LAT:]
        grad = jnp.concatenate(
            [
                jnp.concatenate([real[:, :LANES], imag[:, :LANES]], axis=1),
                jnp.concatenate([real[:, LANES:], imag[:, LANES:]], axis=1),
            ],
            axis=0,
        )
        modes = modes_ref[step]
        pre_a = jnp.dot(modes, wa_ref[...], preferred_element_type=F32) + ba_ref[...]
        squash_a = gelu_parts(pre_a)
        hidden = (0.5 * pre_a * (1.0 + squash_a)).astype(BF)
        pre_b = jnp.dot(hidden, wb_ref[...], preferred_element_type=F32) + bb_ref[...]
        squash_b = jnp.tanh(pre_b * (1.0 / shrink_soft))
        factor = 1.0 - shrink_level / shrink_soft * (1.0 - squash_b * squash_b)
        grad_b = factor * grad
        gbb_ref[...] += jnp.sum(grad_b, axis=0, keepdims=True)
        grad_b = grad_b.astype(BF)
        grad_hidden = lax.dot_general(grad_b, wb_ref[...], ACROSS, preferred_element_type=F32)
        gwb_ref[...] += lax.dot_general(hidden, grad_b, OUTER, preferred_element_type=F32)
        grad_a = gelu_slope(pre_a, squash_a) * grad_hidden
        gba_ref[...] += jnp.sum(grad_a, axis=0, keepdims=True)
        grad_a = grad_a.astype(BF)
        grad_modes = lax.dot_general(
            grad_a, wa_ref[...], ACROSS, preferred_element_type=F32
        ).astype(BF)
        gwa_ref[...] += lax.dot_general(modes, grad_a, OUTER, preferred_element_type=F32)
        mixed = jnp.concatenate(
            [
                jnp.concatenate([grad_modes[:LAT, :LANES], grad_modes[LAT:, :LANES]], axis=1),
                jnp.concatenate([grad_modes[:LAT, LANES:], grad_modes[LAT:, LANES:]], axis=1),
            ],
            axis=0,
        )
        back = jnp.dot(back_ref[...], mixed, preferred_element_type=F32)
        for k in range(2):
            turn_out(turn_ref, back[:, k * LANES : (k + 1) * LANES], row + k, lats, rows, run)

    drain(turn_ref, own_out, other_out)


def per_device(
    inputs, valid_mask, cotangent, first_gain, first_shift, mix_weight_a, mix_bias_a,
    mix_weight_b, mix_bias_b, second_gain, second_shift, expand_weight, expand_bias,
    reduce_weight, reduce_bias,
):
    row_devs = lax.axis_size("rows")
    col_devs = lax.axis_size("cols")
    rows_here, cols_here, channels = inputs.shape
    block = channels // BLOCKS
    lon_size = cols_here * col_devs
    cols_pad = up_to(cols_here, 16)
    row_group = LAT // rows_here
    members = row_group * col_devs
    share = rows_here // CORES
    groups = share // PACK
    slots = (lon_size // 2 + 2) // 2
    slots_pad = up_to(slots, 16)
    lats = share * row_group
    half_rows = 2 * slots_pad
    all_rows = CORES * half_rows
    assert members == CORES * BLOCKS and block * PACK == 3 * LANES
    assert col_devs * cols_pad == all_rows and CORES * lats == LAT

    row_at, col_at = lax.axis_index("rows"), lax.axis_index("cols")
    core = col_at % CORES
    mine = (row_at % row_group) * (col_devs // CORES) + col_at // CORES

    def pick(table):
        return lax.dynamic_index_in_dim(jnp.asarray(table, BF), core, 0, keepdims=False)

    plain_np, weighted_np = lon_table(
        lon_size, col_devs, cols_here, cols_pad, slots, slots_pad
    )
    lat_np = lat_table(rows_here, row_group)
    lon_fwd, lon_wfwd = pick(plain_np), pick(weighted_np)
    lon_inv, lon_winv = (
        pick(np.swapaxes(plain_np, 1, 2)), pick(np.swapaxes(weighted_np, 1, 2))
    )
    lat_fwd, lat_inv = pick(lat_np), pick(np.swapaxes(lat_np, 1, 2))

    snap_groups = [
        [(s * row_group + r) * col_devs + c for r in range(row_group) for c in range(col_devs)]
        for s in range(row_devs // row_group)
    ]
    core_pairs = [
        (r * col_devs + c, r * col_devs + c ^ 1) for r in range(row_devs) for c in range(col_devs)
    ]

    def exchange(x):
        return lax.all_to_all(x, AXES, 0, 0, axis_index_groups=snap_groups, tiled=True)

    def swap(x):
        return lax.ppermute(x, AXES, core_pairs)

    def fold(x):
        return x.reshape((CORES, groups, PACK) + x.shape[1:])

    def row(v):
        return v.reshape(1, -1)

    mask = jnp.pad(
        valid_mask.astype(F32), ((0, 0), (0, cols_pad - cols_here))
    )[:, :, None]
    mask = fold(mask)
    x5, cot5 = fold(inputs), fold(cotangent)

    def lat_spec(cols, width):
        return pl.BlockSpec((CORES, 1, PACK, cols, width), lambda i: (0, i, 0, 0, 0))

    packed_spec = pl.BlockSpec(
        (BLOCKS, CORES, 1, cols_pad, 3 * LANES), lambda i: (0, 0, i, 0, 0)
    )
    row_spec = pl.BlockSpec((1, channels), lambda i: (0, 0))
    here_spec, pad_spec, mask_spec = (
        lat_spec(cols_here, channels), lat_spec(cols_pad, channels), lat_spec(cols_pad, 1)
    )
    packed_shape = (BLOCKS, CORES, groups, cols_pad, 3 * LANES)
    flat_shape = (members, groups, cols_pad, 3 * LANES)
    pad_shape = (CORES, groups, PACK, cols_pad, channels)
    here_shape = (CORES, groups, PACK, cols_here, channels)

    def shape(s, d):
        return jax.ShapeDtypeStruct(s, d)

    index = row_at * col_devs + col_at
    devices = row_devs * col_devs
    all_bits = [2**k for k in range(16) if 2**k < devices]
    cube, outer_bits = all_bits[1:4], all_bits[4:]
    core_line = core.astype(jnp.int32).reshape(1)

    def bit(mask_bit):
        return (index // mask_bit) % 2

    def partner(x, flip):
        return lax.ppermute(x, AXES, [(d, d ^ flip) for d in range(devices)])


    orders = [[cube[(p + k) % 3] for k in range(3)] for p in range(3)]

    def bits(level):
        return jnp.stack([bit(o[level]) for o in orders]).astype(jnp.int32)

    def zipped(kept, got):
        return [x for pair in zip(kept, got) for x in pair]

    def merge(own, got, which, single, after):
        n, (r, c) = len(own), own[0].shape
        out = [shape((n, 2 * r, c), BF)] * 2 if single else [shape((2 * r, c), BF)] * (2 * n)
        return call(
            lambda *refs: merge_kernel(n, single, *refs), zipped(own, got), out, 2.0,
            after=after, prefetch=[which], vmem=34 if single else 12, name="merge",
        )

    class Sum:
        def __init__(self, kept, got):
            self.kept, self.got, self.level = kept, got, 0

        def send(self, arrays):
            self.got = [partner(x, o[self.level]) for x, o in zip(arrays, orders)]

        def halve(self, after=()):
            first, n = self.level == 0, len(orders)
            rows, wide = self.kept[0].shape
            half = rows // n if first else rows // 2
            tiles = 2 if first else 1
            t = half // tiles
            args, specs = [], []
            if first:
                for chunk in range(2 * n):
                    grad, at = divmod(chunk, n)
                    args += [self.kept[grad], self.got[grad]]
                    specs += [pl.BlockSpec((t, wide), lambda i, b, at=at: (at * tiles + i, 0))] * 2
            else:
                for p in range(n):
                    stay = lambda i, b, p=p: (b[p] * tiles + i, 0)
                    leave = lambda i, b, p=p: ((1 - b[p]) * tiles + i, 0)
                    args += [self.kept[p], self.got[p]] * 2
                    specs += [pl.BlockSpec((t, wide), m) for m in (stay, stay, leave, leave)]
            res = call(
                halve_first_kernel if first else halve_kernel,
                args, [shape((half, wide), BF)] * (2 * n), 3.0,
                after=after, prefetch=[bits(self.level)], grid=(tiles,), in_specs=specs,
                out_specs=[pl.BlockSpec((t, wide), lambda i, b: (i, 0))] * (2 * n), vmem=20 if first else 12, name="halve",
            )
            self.kept = res[0::2]
            self.send(res[1::2])
            self.level += 1
            return self.kept[0]

        def join(self, after=()):
            n, (r, c) = len(orders), self.kept[0].shape
            self.kept, sent = call(
                lambda *refs: join_kernel(n, *refs), zipped(self.kept, self.got),
                [shape((n * r, c), BF)] * 2, 1.5, after=after, name="join",
            )
            self.got = partner(sent, outer_bits[0])
            for m in outer_bits[1:]:
                self.kept, sent = add(self.kept, self.got, BF)
                self.got = partner(sent, m)
            return self.kept

        def part(self, after=()):
            n, (r, c) = len(orders), self.kept.shape
            res = call(
                part_kernel, [self.kept, self.got], [shape((r // n, c), BF)] * (2 * n), 1.5,
                after=after, name="part",
            )
            self.kept = res[:n]
            self.level = len(cube) - 1
            self.send(res[n:])
            return self.kept[0]

        def double(self, after=()):
            n, (r, c), single = len(orders), self.kept[0].shape, self.level == 0
            res = merge(self.kept, self.got, bits(self.level), single, after)
            self.level -= 1
            if not single:
                self.kept = res[:n]
                self.send(res[n:])
                return self.kept[0]
            self.kept, sent = (x.reshape(2 * n * r, c) for x in res)
            self.got = partner(sent, 1)
            return self.kept

        def widen(self):
            (rows, c), t = self.kept.shape, 256
            steps = rows // 2 // t
            full = [shape((rows, c), F32), shape((c, rows), F32)]
            done = []
            for k, x in enumerate((self.kept, self.got)):
                at = lambda i, h, k=k: jnp.where(h[0] == 0, k, 1 - k) * steps + i
                done = call(
                    widen_kernel, [x, x] + done, full, 5.0, prefetch=[core_line], grid=(steps,),
                    in_specs=[
                        pl.BlockSpec((t, c), lambda i, h: (i, 0)),
                        pl.BlockSpec((t, c), lambda i, h: (steps + i, 0)),
                    ] + [pl.BlockSpec(memory_space=pl.ANY)] * len(done),
                    out_specs=[
                        pl.BlockSpec((t, c), lambda i, h, at=at: (at(i, h), 0)),
                        pl.BlockSpec((c, t), lambda i, h, at=at: (0, at(i, h))),
                    ],
                    input_output_aliases={3: 0, 4: 1} if done else {}, name="widen",
                )
            return done

    def add(x, y, dtype, after=()):
        return call(add_kernel, [x, y], [shape(x.shape, dtype)] * 2, 1.0, after=after, name="add")

    class Modes:
        def __init__(self, x):
            self.flips = [1] + outer_bits
            self.doubles = list(cube)
            self.x, self.got = x, partner(x, 1)

        def step(self, after=()):
            if self.flips:
                self.flips.pop(0)
                left = self.flips or self.doubles
                self.x, sent = add(self.x, self.got, BF, after)
            else:
                m = self.doubles.pop(0)
                left = self.doubles
                which = bit(m).astype(jnp.int32).reshape(1)
                self.x, sent = merge([self.x], [self.got], which, False, after)
            if left:
                self.got = partner(sent, left[0])
            return self.x

    class Tail:
        def __init__(self, x):
            self.bits = list(all_bits)
            self.x, self.got = x[0], partner(x[1], self.bits[0])

        def step(self, after=()):
            self.x, sent = add(self.x, self.got, F32, after)
            self.bits.pop(0)
            if self.bits:
                self.got = partner(sent, self.bits[0])
            return self.x


    def lon_forward(cells, table, after=()):
        return call(
            lambda *refs: lon_kernel(col_devs, row_group, *refs),
            [cells.reshape(flat_shape), table],
            [shape((half_rows, lats, LANES), BF)] * 2, 5.5, after=after,
            scratch_shapes=[pltpu.VMEM((all_rows * lats, LANES), F32)],
            vmem=24, name="lon_forward",
        )

    def lon_backward(pieces, table, after=()):
        return call(
            lambda *refs: lon_back_kernel(
                col_devs, row_group, len(pieces), refs[len(pieces)], *refs[: len(pieces)], refs[-1]
            ),
            [*pieces, table], shape(flat_shape, BF), 3.5, after=after, vmem=16, name="lon_backward",
        )

    def big_weight(w):
        w = lax.dynamic_index_in_dim(w, mine, 1, keepdims=False)
        gap = LANES - block
        w = jnp.pad(w, ((0, 0), (0, gap), (0, gap)))
        return jnp.concatenate(
            [jnp.concatenate([w[0], w[1]], 1), jnp.concatenate([-w[1], w[0]], 1)], 0
        )

    def big_bias(b):
        b = lax.dynamic_index_in_dim(b.reshape(2, BLOCKS, block), mine, 1, keepdims=False)
        return jnp.pad(b, ((0, 0), (0, LANES - block))).reshape(1, 2 * LANES)

    wa, wb = big_weight(mix_weight_a), big_weight(mix_weight_b)
    ba, bb = big_bias(mix_bias_a), big_bias(mix_bias_b)

    normed, send = call(
        first_kernel, [x5, mask, row(first_gain), row(first_shift)],
        [shape(pad_shape, BF), shape(packed_shape, BF)], 6.0,
        grid=(groups,), in_specs=[here_spec, mask_spec, row_spec, row_spec],
        out_specs=[pad_spec, packed_spec], vmem=16, name="first_norm",
    )
    cells = exchange(send.reshape(flat_shape))

    own, other = lon_forward(cells, lon_fwd)
    other = swap(other)
    own, other, modes = call(
        mix_kernel, [own, other, lat_fwd, lat_inv, wa, ba, wb, bb],
        [shape((lats, half_rows, LANES), BF)] * 2
        + [shape((slots_pad // 2, 2 * LAT, 2 * LANES), BF)], 22.0,
        scratch_shapes=[pltpu.VMEM((2 * lats * half_rows, LANES), F32)], vmem=32, name="mix",
    )
    other = swap(other)
    got = exchange(lon_backward([own, other], lon_winv))

    resid, tokens, cot_pad = call(
        second_kernel,
        [x5, normed, mask, cot5, got.reshape(packed_shape), row(second_gain), row(second_shift)],
        [shape(pad_shape, F32), shape(pad_shape, BF), shape(pad_shape, BF)], 8.5,
        grid=(groups,),
        in_specs=[here_spec, pad_spec, mask_spec, here_spec, packed_spec, row_spec, row_spec],
        out_specs=[pad_spec, pad_spec, pad_spec], vmem=20, name="second_norm",
    )
    tokens2, cot2 = tokens.reshape(-1, channels), cot_pad.reshape(-1, channels)
    count, hidden = tokens2.shape[0], expand_weight.shape[1]
    tile = hidden // 6
    all_tok = pl.BlockSpec((count, channels), lambda i: (0, 0))
    by_col = lambda n: pl.BlockSpec((n, tile), lambda i: (0, i))
    by_row = pl.BlockSpec((tile, channels), lambda i: (i, 0))
    act, gpre, gtok, g_ebias = call(
        chain_kernel,
        [tokens2, cot2, expand_weight, row(expand_bias), reduce_weight],
        [
            shape((count, hidden), BF), shape((count, hidden), BF),
            shape((count, channels), F32), shape((1, hidden), F32),
        ],
        25.0, grid=(6,),
        in_specs=[all_tok, all_tok, by_col(channels), by_col(1), by_row],
        out_specs=[by_col(count), by_col(count), all_tok, by_col(1)], vmem=46, name="mlp_chain",
    )

    halves = 3

    def tile_of(i, c):
        return jnp.where(i < halves, (1 - c[0]) * halves + i, c[0] * halves + i - halves)

    def sent_at(i):
        return jnp.minimum(i, halves - 1)

    def kept_at(i):
        return jnp.maximum(i - halves, 0)

    all_tok_p = pl.BlockSpec((count, channels), lambda i, c: (0, 0))
    hid_tile = pl.BlockSpec((count, tile), lambda i, c: (0, tile_of(i, c)))

    def weight_grad(left, right, after, name):
        return call(
            weight_grad_kernel, [left, right], [shape((halves * tile, channels), BF)] * 2, 10.0,
            after=after, prefetch=[core_line], grid=(6,), in_specs=[hid_tile, all_tok_p],
            out_specs=[
                pl.BlockSpec((tile, channels), lambda i, c: (sent_at(i), 0)),
                pl.BlockSpec((tile, channels), lambda i, c: (kept_at(i), 0)),
            ],
            vmem=20, name=name,
        )

    sent_r, kept_r = weight_grad(act, cot2, [], "reduce_grad")
    got_r = partner(sent_r, 1)
    sent_e, kept_e = weight_grad(gpre, tokens2, [kept_r], "expand_grad")
    sums = Sum([kept_r, kept_e], [got_r, partner(sent_e, 1)])

    one_row = shape((1, channels), F32)
    grad_resid, send, g_gain2, g_shift2, g_rbias = call(
        third_kernel,
        [resid, gtok.reshape(pad_shape), cot_pad, mask, row(second_gain)],
        [shape(pad_shape, F32), shape(packed_shape, BF)] + [one_row] * 3, 9.0, after=[kept_e],
        grid=(groups,), in_specs=[pad_spec, pad_spec, pad_spec, mask_spec, row_spec],
        out_specs=[pad_spec, packed_spec, row_spec, row_spec, row_spec], vmem=20, name="second_back",
    )
    cells = exchange(send.reshape(flat_shape))

    token = sums.halve(after=[send])
    own, other = lon_forward(cells, lon_wfwd, after=[token])
    other = swap(other)
    token = sums.halve(after=[own])
    square = shape((2 * LANES, 2 * LANES), F32)
    line = shape((1, 2 * LANES), F32)
    run = half_rows // SPLIT
    pieces, grads = [], []
    for k in range(SPLIT):
        here = pl.BlockSpec((run, lats, LANES), lambda i, k=k: (k, 0, 0))
        steps = modes.shape[0] // SPLIT
        const = lambda x: pl.BlockSpec(x.shape, lambda i: (0, 0))
        o, t, *g = call(
            mix_back_kernel, [own, other, modes, lat_fwd, lat_inv, wa, ba, wb, bb],
            [shape((lats, run, LANES), BF)] * 2 + [square, line, square, line], 13.0,
            after=[token],
            in_specs=[
                here, here, pl.BlockSpec((steps,) + modes.shape[1:], lambda i, k=k: (k, 0, 0)),
            ] + [const(x) for x in (lat_fwd, lat_inv, wa, ba, wb, bb)],
            scratch_shapes=[pltpu.VMEM((2 * lats * run, LANES), F32)], name="mix_back",
        )
        pieces.append((o, swap(t)))
        grads.append(g)
        if k < SPLIT - 1:
            token = sums.halve(after=[o]) if k == 0 else sums.join(after=[o])
    outputs = call(
        branch_kernel,
        [act.reshape(CORES, groups, PACK, cols_pad, hidden), reduce_weight, resid, row(reduce_bias)],
        shape(here_shape, F32), 10.0, after=[o], grid=(groups,),
        in_specs=[
            lat_spec(cols_pad, hidden), pl.BlockSpec((hidden, channels), lambda i: (0, 0)),
            pad_spec, row_spec,
        ],
        out_specs=[here_spec], vmem=26, name="branch",
    )

    modes_sum = Modes(
        call(
            lambda *refs: collect_kernel(block, *refs), sum(grads, []),
            shape((up_to(4 * block + 4, 16), LANES), F32), 1.5, after=[outputs], name="collect",
        )
    )
    token = sums.part(after=[modes_sum.x])
    send = lon_backward(
        [p[0] for p in pieces] + [p[1] for p in pieces], lon_inv, after=[token]
    )
    got = exchange(send)
    token = modes_sum.step(after=[send])
    token = sums.double(after=[token])
    token = sums.double(after=[token])

    grad_inputs, g_gain1, g_shift1 = call(
        last_kernel, [x5, grad_resid, mask, got.reshape(packed_shape), row(first_gain)],
        [shape(here_shape, F32)] + [one_row] * 2, 9.0, after=[token],
        grid=(groups,), in_specs=[here_spec, pad_spec, mask_spec, packed_spec, row_spec],
        out_specs=[here_spec, row_spec, row_spec], vmem=20, name="first_back",
    )
    tail_sum = Tail(
        call(
            tail_kernel, [g_gain1, g_shift1, g_gain2, g_shift2, g_rbias, g_ebias],
            [shape((1, 5 * channels + hidden), F32)] * 2, 1.0, name="tail",
        )
    )
    token = modes_sum.step(after=[tail_sum.x])
    token = tail_sum.step(after=[token])
    token = modes_sum.step(after=[token])
    token = sums.double(after=[token])
    token = tail_sum.step(after=[token])
    token = modes_sum.step(after=[token])
    token = tail_sum.step(after=[token])
    token = modes_sum.step(after=[token])
    while modes_sum.flips or modes_sum.doubles:
        token = modes_sum.step(after=[token])
    while tail_sum.bits:
        token = tail_sum.step(after=[token])
    g_reduce, g_expand = sums.widen()
    spread = modes_sum.x.reshape(BLOCKS, -1, LANES)
    weight_out, bias_out = shape(mix_weight_a.shape, F32), shape(mix_bias_a.shape, F32)
    g_wa, g_wb, g_ba, g_bb = call(
        lambda *refs: spread_kernel(block, *refs), [spread],
        [weight_out, weight_out, bias_out, bias_out], 3.0, name="spread",
    )

    tail = tail_sum.x
    g_gain1, g_shift1, g_gain2, g_shift2, g_rbias = (
        tail[0, k * channels : (k + 1) * channels] for k in range(5)
    )
    g_ebias = tail[0, 5 * channels :]

    def flat(v):
        return v.reshape(-1)

    return (
        outputs.reshape(inputs.shape), grad_inputs.reshape(inputs.shape),
        flat(g_gain1), flat(g_shift1), g_wa, g_ba, g_wb, g_bb, flat(g_gain2), flat(g_shift2),
        g_expand, g_ebias, g_reduce, flat(g_rbias),
    )


def solution(mesh):
    grid = P("rows", "cols", None)
    placed = (grid, P("rows", "cols"), grid) + (P(),) * 12
    return jax.shard_map(
        per_device,
        mesh=mesh,
        in_specs=placed,
        out_specs=(grid, grid) + (P(),) * 12,
        check_vma=False,
    )
```

```python
import math

import jax
import jax.numpy as jnp
import numpy as np
from jax import lax
from jax.experimental import pallas as pl
from jax.experimental.pallas import tpu as pltpu
from jax.sharding import PartitionSpec as P

BLOCKS = 8
LAT = 96
CORES = 2
PACK = 4
LANES = 128

shrink_level = 0.01
shrink_soft = 0.1
norm_eps = 1e-05
gelu_root = math.sqrt(2.0 / math.pi)
gelu_cube = 0.044715

BF = jnp.bfloat16
F32 = jnp.float32
AXES = ("rows", "cols")


def up_to(value, step):
    return (value + step - 1) // step * step


def call(kernel, args, out_shape, us, after=(), in_specs=None, prefetch=(), vmem=12, **kw):
    outs = out_shape if isinstance(out_shape, (list, tuple)) else [out_shape]
    lead, n_in, n_after = len(prefetch), len(args), len(after)

    def body(*refs):
        kernel(*refs[: lead + n_in], *refs[lead + n_in + n_after :])

    grid = kw.pop("grid", (1,))
    whole = lambda x: pl.BlockSpec(x.shape, lambda *_, n=len(x.shape): (0,) * n)
    specs = list(in_specs) if in_specs is not None else [whole(a) for a in args]
    specs += [pl.BlockSpec(memory_space=pl.ANY)] * n_after
    out_specs = kw.pop("out_specs", None) or [whole(o) for o in outs]
    got = pl.pallas_call(
        body,
        grid_spec=pltpu.PrefetchScalarGridSpec(
            num_scalar_prefetch=lead,
            grid=grid,
            in_specs=specs,
            out_specs=out_specs,
            scratch_shapes=kw.pop("scratch_shapes", ()),
        ),
        out_shape=outs,
        compiler_params=pltpu.CompilerParams(vmem_limit_bytes=vmem * 1024 * 1024),
        cost_estimate=pl.CostEstimate(
            flops=0, bytes_accessed=int(us * 1e5), transcendentals=0
        ),
        **kw,
    )(*prefetch, *args, *after)
    return list(got) if isinstance(out_shape, (list, tuple)) else got[0]


SPLIT = 3


def lon_table(lon_size, col_devs, cols_here, cols_pad, slots, slots_pad):
    modes = lon_size // 2 + 1
    table = np.zeros((CORES, 2, slots_pad, col_devs, cols_pad), np.float64)
    weights = np.zeros((CORES, slots_pad), np.float64)
    place = np.arange(lon_size).reshape(col_devs, cols_here)
    for half in range(CORES):
        for slot in range(slots):
            mode = half * slots + slot
            if mode >= modes:
                continue
            angle = (place * mode % lon_size) * (2.0 * math.pi / lon_size)
            table[half, 0, slot, :, :cols_here] = np.cos(angle) / math.sqrt(lon_size)
            edge = mode == 0 or 2 * mode == lon_size
            if not edge:
                table[half, 1, slot, :, :cols_here] = np.sin(angle) / math.sqrt(lon_size)
            weights[half, slot] = 1.0 if edge else 2.0
    weighted = table * weights[:, None, :, None, None]
    rows = 2 * slots_pad
    flat = [
        a.reshape(CORES, 2, SPLIT, slots_pad // SPLIT, col_devs, cols_pad)
        .swapaxes(1, 2)
        .reshape(CORES, rows, col_devs * cols_pad)
        for a in (table, weighted)
    ]
    return [
        np.stack([np.concatenate([a[h], a[1 - h]], 0) for h in range(CORES)]) for a in flat
    ]


def lat_table(rows_here, row_group):
    share = rows_here // CORES
    out = []
    for h in range(CORES):
        own = [
            rows_here * r + share * h + i for r in range(row_group) for i in range(share)
        ]
        other = [
            rows_here * r + share * (1 - h) + i for r in range(row_group) for i in range(share)
        ]
        angle = np.outer(np.arange(LAT), np.array(own + other)) % LAT * (2.0 * math.pi / LAT)
        cos, sin = np.cos(angle) / math.sqrt(LAT), np.sin(angle) / math.sqrt(LAT)
        out.append(np.block([[cos, -sin], [-sin, -cos]]))
    return np.stack(out)


def pack_lanes(tiles):
    a, b, c, d = tiles
    lane = lax.broadcasted_iota(jnp.int32, a.shape, a.ndim - 1)
    axis = a.ndim - 1
    b, c, d = pltpu.roll(b, 96, axis), pltpu.roll(c, 64, axis), pltpu.roll(d, 32, axis)
    return [
        jnp.where(lane < 96, a, b),
        jnp.where(lane < 64, b, c),
        jnp.where(lane < 32, c, d),
    ]


def unpack_lanes(tiles):
    a, b, c = tiles
    lane = lax.broadcasted_iota(jnp.int32, a.shape, a.ndim - 1)
    axis = a.ndim - 1
    return [
        a,
        pltpu.roll(jnp.where(lane >= 96, a, b), 32, axis),
        pltpu.roll(jnp.where(lane >= 64, b, c), 64, axis),
        pltpu.roll(c, 96, axis),
    ]


def tiles_of(value):
    return [value[:, LANES * i : LANES * (i + 1)] for i in range(value.shape[1] // LANES)]


def split_blocks(value):
    tiles = tiles_of(value)
    out = []
    for i in range(0, len(tiles), 3):
        out += unpack_lanes(tiles[i : i + 3])
    return out


def join_blocks(tiles):
    out = []
    for i in range(0, len(tiles), 4):
        out += pack_lanes(tiles[i : i + 4])
    return jnp.concatenate(out, axis=1)


def pad_rows(value, rows):
    return jnp.concatenate(
        [value, jnp.zeros((rows - value.shape[0], value.shape[1]), value.dtype)], axis=0
    )


def store_packed(ref, half, per_lat):
    split = [split_blocks(v) for v in per_lat]
    for q in range(BLOCKS):
        packed = pack_lanes([split[j][q] for j in range(PACK)])
        ref[q, half, 0] = jnp.concatenate(packed, axis=1).astype(ref.dtype)


def load_packed(ref, half):
    by_lat = [[] for _ in range(PACK)]
    for q in range(BLOCKS):
        parts = unpack_lanes(tiles_of(ref[q, half, 0].astype(F32)))
        for j in range(PACK):
            by_lat[j].append(parts[j])
    return [join_blocks(tiles) for tiles in by_lat]


def stats(x):
    average = jnp.mean(x, axis=-1, keepdims=True)
    centred = x - average
    spread = jnp.mean(centred * centred, axis=-1, keepdims=True)
    inv = lax.rsqrt(spread + norm_eps)
    return centred * inv, inv


def norm_back(grad, xhat, inv, gain):
    scaled = grad * gain
    m1 = jnp.mean(scaled, axis=-1, keepdims=True)
    m2 = jnp.mean(scaled * xhat, axis=-1, keepdims=True)
    return inv * (scaled - m1 - xhat * m2)


def first_kernel(x_ref, mask_ref, gain_ref, shift_ref, normed_ref, out_ref):
    rows = normed_ref.shape[3]
    for half in range(CORES):
        lats = []
        for j in range(PACK):
            x = pad_rows(x_ref[half, 0, j].astype(F32), rows)
            xhat, _ = stats(x)
            y = mask_ref[half, 0, j] * (xhat * gain_ref[...] + shift_ref[...])
            normed_ref[half, 0, j] = y.astype(BF)
            lats.append(y)
        store_packed(out_ref, half, lats)


def second_kernel(
    x_ref, normed_ref, mask_ref, cot_ref, got_ref, gain_ref, shift_ref, resid_ref, tok_ref, cot_out
):
    rows = normed_ref.shape[3]
    for half in range(CORES):
        spatial = load_packed(got_ref, half)
        for j in range(PACK):
            x = pad_rows(x_ref[half, 0, j].astype(F32), rows)
            resid = x + normed_ref[half, 0, j].astype(F32) + mask_ref[half, 0, j] * spatial[j]
            resid_ref[half, 0, j] = resid
            xhat, _ = stats(resid)
            tok_ref[half, 0, j] = (xhat * gain_ref[...] + shift_ref[...]).astype(BF)
            cot_out[half, 0, j] = pad_rows(cot_ref[half, 0, j].astype(F32), rows).astype(BF)


def third_kernel(
    resid_ref, gtok_ref, cot_ref, mask_ref, gain_ref,
    gresid_ref, send_ref, ggain_ref, gshift_ref, gbias_ref,
):
    @pl.when(pl.program_id(0) == 0)
    def _():
        ggain_ref[...] = jnp.zeros_like(ggain_ref)
        gshift_ref[...] = jnp.zeros_like(gshift_ref)
        gbias_ref[...] = jnp.zeros_like(gbias_ref)

    for half in range(CORES):
        lats = []
        for j in range(PACK):
            xhat, inv = stats(resid_ref[half, 0, j])
            gtok = gtok_ref[half, 0, j]
            cot = cot_ref[half, 0, j].astype(F32)
            ggain_ref[...] += jnp.sum(gtok * xhat, axis=0, keepdims=True)
            gshift_ref[...] += jnp.sum(gtok, axis=0, keepdims=True)
            gbias_ref[...] += jnp.sum(cot, axis=0, keepdims=True)
            gres = cot + norm_back(gtok, xhat, inv, gain_ref[...])
            gresid_ref[half, 0, j] = gres
            lats.append(mask_ref[half, 0, j] * gres)
        store_packed(send_ref, half, lats)


def store_lat(out_ref, half, j, rows_here, value):
    at = half * (rows_here // CORES) + pl.program_id(0) * PACK + j
    out_ref[:, at, :] = value[: out_ref.shape[0]]


def last_kernel(
    rows_here, x_ref, gresid_ref, mask_ref, got_ref, gain_ref, out_ref, ggain_ref, gshift_ref
):
    @pl.when(pl.program_id(0) == 0)
    def _():
        ggain_ref[...] = jnp.zeros_like(ggain_ref)
        gshift_ref[...] = jnp.zeros_like(gshift_ref)

    rows = gresid_ref.shape[3]
    for half in range(CORES):
        got = load_packed(got_ref, half)
        for j in range(PACK):
            x = pad_rows(x_ref[half, 0, j].astype(F32), rows)
            xhat, inv = stats(x)
            gres = gresid_ref[half, 0, j]
            grad = mask_ref[half, 0, j] * (gres + got[j])
            ggain_ref[...] += jnp.sum(grad * xhat, axis=0, keepdims=True)
            gshift_ref[...] += jnp.sum(grad, axis=0, keepdims=True)
            store_lat(
                out_ref, half, j, rows_here, gres + norm_back(grad, xhat, inv, gain_ref[...])
            )


OUTER = (((0,), (0,)), ((), ()))
ACROSS = (((1,), (1,)), ((), ()))


def chain_kernel(
    tok_ref, cot_ref, up_ref, bias_ref, down_ref, act_ref, gpre_ref, gtok_ref, gbias_ref
):
    @pl.when(pl.program_id(0) == 0)
    def _():
        gtok_ref[...] = jnp.zeros_like(gtok_ref)

    pre = jnp.dot(tok_ref[...], up_ref[...], preferred_element_type=F32) + bias_ref[...]
    squash = gelu_parts(pre)
    act_ref[...] = (0.5 * pre * (1.0 + squash)).astype(BF)
    gact = lax.dot_general(cot_ref[...], down_ref[...], ACROSS, preferred_element_type=F32)
    gpre = gelu_slope(pre, squash) * gact
    gbias_ref[...] = jnp.sum(gpre, axis=0, keepdims=True)
    gpre = gpre.astype(BF)
    gpre_ref[...] = gpre
    gtok_ref[...] += lax.dot_general(gpre, up_ref[...], ACROSS, preferred_element_type=F32)


def weight_grad_kernel(core_ref, left_ref, right_ref, out_ref):
    out_ref[...] = lax.dot_general(
        left_ref[...], right_ref[...], OUTER, preferred_element_type=F32
    ).astype(BF)


def branch_kernel(rows_here, act_ref, down_ref, resid_ref, bias_ref, out_ref):
    cols = resid_ref.shape[3]
    rows = CORES * PACK * cols
    act = act_ref[...].reshape(rows, act_ref.shape[-1])
    branch = jnp.dot(act, down_ref[...], preferred_element_type=F32) + bias_ref[...]
    for half in range(CORES):
        for j in range(PACK):
            at = (half * PACK + j) * cols
            store_lat(
                out_ref, half, j, rows_here, resid_ref[half, 0, j] + branch[at : at + cols]
            )


def plus(left, right):
    return (left.astype(F32) + right.astype(F32)).astype(BF)


def halve_first_kernel(bits_ref, *refs):
    count = len(refs) // 6
    for p in range(count):
        a, b, c, d = refs[4 * p : 4 * p + 4]
        low, high = plus(a[...], b[...]), plus(c[...], d[...])
        first = bits_ref[p] == 0
        refs[4 * count + 2 * p][...] = jnp.where(first, low, high)
        refs[4 * count + 2 * p + 1][...] = jnp.where(first, high, low)


def halve_kernel(bits_ref, *refs):
    count = len(refs) // 6
    for k in range(2 * count):
        refs[4 * count + k][...] = plus(refs[2 * k][...], refs[2 * k + 1][...])


def join_kernel(count, *refs):
    stay, got = refs[count : count + 2]
    for p in range(count):
        n, m = refs[p].shape[0], stay.shape[0] // count
        value = refs[p][...]
        rows = slice(p * m, (p + 1) * m)
        extra = (stay[rows] + got[rows]).astype(BF)
        for out in refs[-2:]:
            out[p * (n + m) : p * (n + m) + n] = value
            out[p * (n + m) + n : (p + 1) * (n + m)] = extra


def settle_kernel(count, *refs):
    for p in range(count):
        refs[2 * count + p][...] = plus(refs[2 * p][...], refs[2 * p + 1][...])


def part_kernel(kept, got, *outs):
    n, count = outs[0].shape[0], len(outs) // 2
    for p in range(count):
        rows = slice(p * n, (p + 1) * n)
        value = plus(kept[rows], got[rows])
        outs[p][...] = value
        outs[count + p][...] = value


def add_kernel(left, right, *outs):
    value = left[...].astype(F32) + right[...].astype(F32)
    for out in outs:
        out[...] = value.astype(out.dtype)


def tail_kernel(*refs):
    for out in refs[-2:]:
        at = 0
        for ref in refs[:-2]:
            out[:, at : at + ref.shape[1]] = ref[...]
            at += ref.shape[1]


def merge_kernel(count, single, bits_ref, *refs):
    outs = refs[2 * count :]
    for p in range(count):
        own, got = refs[2 * p], refs[2 * p + 1]
        n = own.shape[0]
        for out in (outs[p::count] if not single else [o.at[p] for o in outs]):
            out[pl.ds(pl.multiple_of(bits_ref[p] * n, 16), n), :] = own[...]
            out[pl.ds(pl.multiple_of((1 - bits_ref[p]) * n, 16), n), :] = got[...]


def widen_kernel(core_ref, reduce_ref, expand_ref, *refs):
    reduce_out, expand_out, extra_r, extra_e = refs[-4:]
    n = reduce_out.shape[0] // 2
    for k in range(2):
        at = k * (n + EXTRA)
        reduce_out[k * n : (k + 1) * n] = reduce_ref[at : at + n].astype(F32)
        expand_out[:, k * n : (k + 1) * n] = expand_ref[at : at + n].astype(F32).T
        extra_r[k] = reduce_ref[at + n : at + n + EXTRA]
        extra_e[k] = expand_ref[at + n : at + n + EXTRA]


EXTRA = 16


def collect_kernel(block, core_ref, grad_ref, *refs):
    wide = 2 * LANES
    halves, lines = [], []
    for i in range(2):
        g = grad_ref[i * wide : (i + 1) * wide]
        at = 2 * wide + 8 * i
        line = jnp.sum(grad_ref[at : at + 8], axis=0, keepdims=True)
        top, low = g[:block], g[LANES : LANES + block]
        halves.append([top[:, :LANES] + low[:, LANES:], top[:, LANES:] - low[:, :LANES]])
        lines += [line[:, :LANES], line[:, LANES:]]
    rows = lax.broadcasted_iota(jnp.int32, (EXTRA, LANES), 0)
    bias = sum(jnp.where(rows == k, line, 0.0) for k, line in enumerate(lines))
    first = core_ref[0] == 0
    for k, out in enumerate(refs[-2:]):
        own = first if k == 0 else jnp.logical_not(first)
        out[...] = jnp.zeros_like(out)
        for p in range(2):
            value = jnp.where(own, halves[0][p], halves[1][p])
            for t in range(block // EXTRA):
                at = slice(t * LANES, (t + 1) * LANES)
                out[p * EXTRA : (p + 1) * EXTRA, at] = value[t * EXTRA : (t + 1) * EXTRA]
        out[2 * EXTRA : 3 * EXTRA, :LANES] = jnp.where(own, bias, 0.0)


def spread_kernel(block, core_ref, *refs):
    own, got = refs[:2], refs[2:4]
    wa_ref, wb_ref, ba_ref, bb_ref = refs[4:]
    first = core_ref[0] == 0
    per = own[0].shape[0]
    biases = [[] for _ in range(4)]
    for q in range(BLOCKS):
        for half in range(CORES):
            for p in range(3):
                if half == 1 and p == 2:
                    continue
                k = sum(((q >> ((p + j) % 3)) & 1) << (2 - j) for j in range(3))
                at = p * BLOCKS + k
                mine, other = (r[at // per][at % per].astype(F32) for r in (own, got))
                value = jnp.where(first, mine, other) if half == 0 else jnp.where(first, other, mine)
                if p == 2:
                    for i in range(4):
                        biases[i].append(value[i : i + 1, :LANES])
                    continue
                out = wb_ref if half else wa_ref
                for t in range(block // EXTRA):
                    out[p, q, t * EXTRA : (t + 1) * EXTRA, :] = value[
                        :, t * LANES : t * LANES + block
                    ]
    for i in range(4):
        (bb_ref if i > 1 else ba_ref)[i % 2 : i % 2 + 1, :] = join_blocks(biases[i])


def lon_kernel(col_devs, row_group, x_ref, table_ref, own_ref, other_ref, turn_ref):
    groups = x_ref.shape[1]
    rows = table_ref.shape[0]
    lats = own_ref.shape[1]
    slots = own_ref.shape[0]
    for r in range(row_group):
        for g in range(groups):
            cells = jnp.concatenate(
                [x_ref[r * col_devs + c, g] for c in range(col_devs)], axis=0
            )
            modes = jnp.dot(table_ref[...], cells, preferred_element_type=F32)
            for j, tile in enumerate(unpack_lanes(tiles_of(modes))):
                at = (r * groups + g) * PACK + j
                turn_ref[pl.ds(at, rows, stride=lats), :] = tile

    @pl.loop(0, slots)
    def _(s):
        own_ref[s] = turn_ref[pl.ds(pl.multiple_of(s * lats, 8), lats), :].astype(BF)
        other_ref[s] = turn_ref[
            pl.ds(pl.multiple_of((s + slots) * lats, 8), lats), :
        ].astype(BF)


def lon_back_kernel(col_devs, row_group, pieces, table_ref, *refs):
    out_ref = refs[pieces]
    groups = out_ref.shape[1]
    cols = out_ref.shape[2]
    for r in range(row_group):
        for g in range(groups):
            tiles = []
            for j in range(0, PACK, 2):
                pair = []
                for k in range(2):
                    at = (r * groups + g) * PACK + j + k
                    pair.append(jnp.concatenate([r_[at] for r_ in refs[:pieces]], axis=0))
                cells = jnp.dot(
                    table_ref[...], jnp.concatenate(pair, axis=1), preferred_element_type=F32
                )
                tiles += tiles_of(cells)
            packed = jnp.concatenate(pack_lanes(tiles), axis=1).astype(BF)
            for c in range(col_devs):
                out_ref[r * col_devs + c, g] = packed[c * cols : (c + 1) * cols]


def gelu_parts(v):
    squash = jnp.tanh(gelu_root * (v + gelu_cube * (v * v * v)))
    return squash


def gelu(v):
    return 0.5 * v * (1.0 + gelu_parts(v))


def gelu_slope(v, squash):
    inner = gelu_root * (1.0 + 3.0 * gelu_cube * (v * v))
    return 0.5 * (1.0 + squash) + 0.5 * v * (1.0 - squash * squash) * inner


def latitudes(own_ref, other_ref, row, run):
    return jnp.concatenate(
        [own_ref[row], other_ref[row], own_ref[row + run], other_ref[row + run]], axis=0
    )


def turn_out(turn_ref, value, row, lats, rows, run):
    for part in range(2):
        for dest in range(2):
            piece = value[(2 * part + dest) * lats : (2 * part + dest + 1) * lats]
            start = dest * lats * rows + part * run + row
            turn_ref[pl.ds(start, lats, stride=rows), :] = piece


def drain(turn_ref, own_ref, other_ref):
    lats, rows = own_ref.shape[0], own_ref.shape[1]

    @pl.loop(0, lats)
    def _(at):
        own_ref[at] = turn_ref[pl.ds(pl.multiple_of(at * rows, 8), rows), :].astype(BF)
        other_ref[at] = turn_ref[
            pl.ds(pl.multiple_of((at + lats) * rows, 8), rows), :
        ].astype(BF)


def mix_kernel(
    own_ref, other_ref, lat_ref, back_ref, wa_ref, ba_ref, wb_ref, bb_ref,
    own_out, other_out, modes_out, turn_ref,
):
    lats, rows = own_ref.shape[1], own_ref.shape[0]
    run = rows // 2 // SPLIT

    @pl.loop(0, rows // 4)
    def _(step):
        slot = 2 * step
        row = slot + slot // run * run
        cells = jnp.concatenate(
            [latitudes(own_ref, other_ref, row + k, run) for k in range(2)], axis=1
        )
        full = jnp.dot(lat_ref[...], cells, preferred_element_type=F32).astype(BF)
        real, imag = full[:LAT], full[LAT:]
        modes = jnp.concatenate(
            [
                jnp.concatenate([real[:, :LANES], imag[:, :LANES]], axis=1),
                jnp.concatenate([real[:, LANES:], imag[:, LANES:]], axis=1),
            ],
            axis=0,
        )
        modes_out[step] = modes
        pre_a = jnp.dot(modes, wa_ref[...], preferred_element_type=F32) + ba_ref[...]
        hidden = gelu(pre_a).astype(BF)
        pre_b = jnp.dot(hidden, wb_ref[...], preferred_element_type=F32) + bb_ref[...]
        shrunk = (pre_b - shrink_level * jnp.tanh(pre_b * (1.0 / shrink_soft))).astype(BF)
        mixed = jnp.concatenate(
            [
                jnp.concatenate([shrunk[:LAT, :LANES], shrunk[LAT:, :LANES]], axis=1),
                jnp.concatenate([shrunk[:LAT, LANES:], shrunk[LAT:, LANES:]], axis=1),
            ],
            axis=0,
        )
        back = jnp.dot(back_ref[...], mixed, preferred_element_type=F32)
        for k in range(2):
            turn_out(turn_ref, back[:, k * LANES : (k + 1) * LANES], row + k, lats, rows, run)

    drain(turn_ref, own_out, other_out)


def row_sums(value):
    return jnp.sum(value.reshape(-1, 8, value.shape[1]), axis=0)


def mix_back_kernel(
    own_ref, other_ref, modes_ref, lat_ref, back_ref, wa_ref, ba_ref, wb_ref, bb_ref,
    *refs,
):
    own_out, other_out, grad_ref, turn_ref = refs[-4:]
    lats, rows = own_ref.shape[1], own_ref.shape[0]
    run = rows // 2
    grad_ref[...] = refs[0][...] if len(refs) > 4 else jnp.zeros_like(grad_ref)
    wide = wa_ref.shape[0]
    gwa_ref, gwb_ref = grad_ref.at[:wide], grad_ref.at[wide : 2 * wide]
    gba_ref, gbb_ref = grad_ref.at[2 * wide : 2 * wide + 8], grad_ref.at[2 * wide + 8 :]

    @pl.loop(0, run // 2)
    def _(step):
        row = 2 * step
        cells = jnp.concatenate(
            [latitudes(own_ref, other_ref, row + k, run) for k in range(2)], axis=1
        )
        full = jnp.dot(lat_ref[...], cells, preferred_element_type=F32)
        real, imag = full[:LAT], full[LAT:]
        grad = jnp.concatenate(
            [
                jnp.concatenate([real[:, :LANES], imag[:, :LANES]], axis=1),
                jnp.concatenate([real[:, LANES:], imag[:, LANES:]], axis=1),
            ],
            axis=0,
        )
        modes = modes_ref[step]
        pre_a = jnp.dot(modes, wa_ref[...], preferred_element_type=F32) + ba_ref[...]
        squash_a = gelu_parts(pre_a)
        hidden = (0.5 * pre_a * (1.0 + squash_a)).astype(BF)
        pre_b = jnp.dot(hidden, wb_ref[...], preferred_element_type=F32) + bb_ref[...]
        squash_b = jnp.tanh(pre_b * (1.0 / shrink_soft))
        factor = 1.0 - shrink_level / shrink_soft * (1.0 - squash_b * squash_b)
        grad_b = factor * grad
        gbb_ref[...] += row_sums(grad_b)
        grad_b = grad_b.astype(BF)
        grad_hidden = lax.dot_general(grad_b, wb_ref[...], ACROSS, preferred_element_type=F32)
        gwb_ref[...] += lax.dot_general(hidden, grad_b, OUTER, preferred_element_type=F32)
        grad_a = gelu_slope(pre_a, squash_a) * grad_hidden
        gba_ref[...] += row_sums(grad_a)
        grad_a = grad_a.astype(BF)
        grad_modes = lax.dot_general(
            grad_a, wa_ref[...], ACROSS, preferred_element_type=F32
        ).astype(BF)
        gwa_ref[...] += lax.dot_general(modes, grad_a, OUTER, preferred_element_type=F32)
        mixed = jnp.concatenate(
            [
                jnp.concatenate([grad_modes[:LAT, :LANES], grad_modes[LAT:, :LANES]], axis=1),
                jnp.concatenate([grad_modes[:LAT, LANES:], grad_modes[LAT:, LANES:]], axis=1),
            ],
            axis=0,
        )
        back = jnp.dot(back_ref[...], mixed, preferred_element_type=F32)
        for k in range(2):
            turn_out(turn_ref, back[:, k * LANES : (k + 1) * LANES], row + k, lats, rows, run)

    drain(turn_ref, own_out, other_out)


def per_device(
    inputs, valid_mask, cotangent, first_gain, first_shift, mix_weight_a, mix_bias_a,
    mix_weight_b, mix_bias_b, second_gain, second_shift, expand_weight, expand_bias,
    reduce_weight, reduce_bias,
):
    row_devs = lax.axis_size("rows")
    col_devs = lax.axis_size("cols")
    rows_here, cols_here, channels = inputs.shape
    block = channels // BLOCKS
    lon_size = cols_here * col_devs
    cols_pad = up_to(cols_here, 16)
    row_group = LAT // rows_here
    members = row_group * col_devs
    share = rows_here // CORES
    groups = share // PACK
    slots = (lon_size // 2 + 2) // 2
    slots_pad = up_to(slots, 16)
    lats = share * row_group
    half_rows = 2 * slots_pad
    all_rows = CORES * half_rows
    assert members == CORES * BLOCKS and block * PACK == 3 * LANES
    assert col_devs * cols_pad == all_rows and CORES * lats == LAT

    row_at, col_at = lax.axis_index("rows"), lax.axis_index("cols")
    core = col_at % CORES
    mine = (row_at % row_group) * (col_devs // CORES) + col_at // CORES

    def pick(table):
        return lax.dynamic_index_in_dim(jnp.asarray(table, BF), core, 0, keepdims=False)

    plain_np, weighted_np = lon_table(
        lon_size, col_devs, cols_here, cols_pad, slots, slots_pad
    )
    lat_np = lat_table(rows_here, row_group)
    lon_fwd, lon_wfwd = pick(plain_np), pick(weighted_np)
    lon_inv, lon_winv = (
        pick(np.swapaxes(plain_np, 1, 2)), pick(np.swapaxes(weighted_np, 1, 2))
    )
    lat_fwd, lat_inv = pick(lat_np), pick(np.swapaxes(lat_np, 1, 2))

    snap_groups = [
        [(s * row_group + r) * col_devs + c for r in range(row_group) for c in range(col_devs)]
        for s in range(row_devs // row_group)
    ]
    core_pairs = [
        (r * col_devs + c, r * col_devs + c ^ 1) for r in range(row_devs) for c in range(col_devs)
    ]

    def exchange(x):
        return lax.all_to_all(x, AXES, 0, 0, axis_index_groups=snap_groups, tiled=True)

    def swap(x):
        return lax.ppermute(x, AXES, core_pairs)

    def fold(x):
        return x.reshape((CORES, groups, PACK) + x.shape[1:])

    def row(v):
        return v.reshape(1, -1)

    mask = jnp.pad(
        valid_mask.astype(F32), ((0, 0), (0, cols_pad - cols_here))
    )[:, :, None]
    mask = fold(mask)
    x5, cot5 = fold(inputs), fold(cotangent)

    def lat_spec(cols, width):
        return pl.BlockSpec((CORES, 1, PACK, cols, width), lambda i: (0, i, 0, 0, 0))

    packed_spec = pl.BlockSpec(
        (BLOCKS, CORES, 1, cols_pad, 3 * LANES), lambda i: (0, 0, i, 0, 0)
    )
    row_spec = pl.BlockSpec((1, channels), lambda i: (0, 0))
    here_spec, pad_spec, mask_spec = (
        lat_spec(cols_here, channels), lat_spec(cols_pad, channels), lat_spec(cols_pad, 1)
    )
    packed_shape = (BLOCKS, CORES, groups, cols_pad, 3 * LANES)
    flat_shape = (members, groups, cols_pad, 3 * LANES)
    pad_shape = (CORES, groups, PACK, cols_pad, channels)
    here_shape = (CORES, groups, PACK, cols_here, channels)

    def shape(s, d):
        return jax.ShapeDtypeStruct(s, d)

    index = row_at * col_devs + col_at
    devices = row_devs * col_devs
    all_bits = [2**k for k in range(16) if 2**k < devices]
    cube, outer_bits = all_bits[1:4], all_bits[4:]
    core_line = core.astype(jnp.int32).reshape(1)

    def bit(mask_bit):
        return (index // mask_bit) % 2

    def partner(x, flip):
        return lax.ppermute(x, AXES, [(d, d ^ flip) for d in range(devices)])


    orders = [[cube[(p + k) % 3] for k in range(3)] for p in range(3)]

    def bits(level):
        return jnp.stack([bit(o[level]) for o in orders]).astype(jnp.int32)

    def zipped(kept, got):
        return [x for pair in zip(kept, got) for x in pair]

    def merge(own, got, which, single, after):
        n, (r, c) = len(own), own[0].shape
        out = [shape((n, 2 * r, c), BF)] * 2 if single else [shape((2 * r, c), BF)] * (2 * n)
        return call(
            lambda *refs: merge_kernel(n, single, *refs), zipped(own, got), out, 2.0,
            after=after, prefetch=[which], vmem=34 if single else 12, name="merge",
        )

    class Sum:
        def __init__(self, kept, got):
            self.kept, self.got, self.level = kept, got, 0

        def send(self, arrays):
            self.got = [partner(x, o[self.level]) for x, o in zip(arrays, orders)]

        def halve(self, after=()):
            first, n = self.level == 0, len(orders)
            rows, wide = self.kept[0].shape
            half = rows // n if first else rows // 2
            tiles = 2 if first else 1
            t = half // tiles
            args, specs = [], []
            if first:
                for chunk in range(2 * n):
                    grad, at = divmod(chunk, n)
                    args += [self.kept[grad], self.got[grad]]
                    specs += [pl.BlockSpec((t, wide), lambda i, b, at=at: (at * tiles + i, 0))] * 2
            else:
                for p in range(n):
                    stay = lambda i, b, p=p: (b[p] * tiles + i, 0)
                    leave = lambda i, b, p=p: ((1 - b[p]) * tiles + i, 0)
                    args += [self.kept[p], self.got[p]] * 2
                    specs += [pl.BlockSpec((t, wide), m) for m in (stay, stay, leave, leave)]
            res = call(
                halve_first_kernel if first else halve_kernel,
                args, [shape((half, wide), BF)] * (2 * n), 3.0,
                after=after, prefetch=[bits(self.level)], grid=(tiles,), in_specs=specs,
                out_specs=[pl.BlockSpec((t, wide), lambda i, b: (i, 0))] * (2 * n), vmem=20 if first else 12, name="halve",
            )
            self.kept = res[0::2]
            self.send(res[1::2])
            self.level += 1
            return self.kept[0]

        def settle(self, after=()):
            n = len(orders)
            self.kept = call(
                lambda *refs: settle_kernel(n, *refs), zipped(self.kept, self.got),
                [shape(x.shape, BF) for x in self.kept], 1.0, after=after, name="settle",
            )
            return self.kept[0]

        def join(self, stay, got, after=()):
            n, (r, c) = len(orders), self.kept[0].shape
            self.kept, sent = call(
                lambda *refs: join_kernel(n, *refs), self.kept + [stay, got],
                [shape((n * (r + EXTRA), c), BF)] * 2, 1.5, after=after, name="join",
            )
            self.got = partner(sent, outer_bits[0])
            for m in outer_bits[1:]:
                self.kept, sent = add(self.kept, self.got, BF)
                self.got = partner(sent, m)
            return self.kept

        def part(self, after=()):
            n, (r, c) = len(orders), self.kept.shape
            res = call(
                part_kernel, [self.kept, self.got], [shape((r // n, c), BF)] * (2 * n), 1.5,
                after=after, name="part",
            )
            self.kept = res[:n]
            self.level = len(cube) - 1
            self.send(res[n:])
            return self.kept[0]

        def double(self, after=()):
            n, (r, c), single = len(orders), self.kept[0].shape, self.level == 0
            res = merge(self.kept, self.got, bits(self.level), single, after)
            self.level -= 1
            if not single:
                self.kept = res[:n]
                self.send(res[n:])
                return self.kept[0]
            self.kept, sent = (x.reshape(2 * n * r, c) for x in res)
            self.got = partner(sent, 1)
            return self.kept

        def widen(self, done, after=()):
            rows, c = self.kept.shape
            chunk = rows // (len(orders) * BLOCKS)
            t = 2 * (chunk - EXTRA)
            steps = rows // chunk // 4
            full_rows = CORES * steps * t
            x = self.got if done else self.kept
            full = [shape((full_rows, c), F32), shape((c, full_rows), F32)]
            extra = [shape((2 * steps, EXTRA, c), BF)] * 2
            at = lambda i, h: (1 - h[0] if done else h[0]) * steps + i
            return call(
                widen_kernel, [x, x] + done[:2], full + extra, 5.0, after=after,
                prefetch=[core_line], grid=(steps,),
                in_specs=[
                    pl.BlockSpec((2 * chunk, c), lambda i, h: (i, 0)),
                    pl.BlockSpec((2 * chunk, c), lambda i, h: (steps + i, 0)),
                ] + [pl.BlockSpec(memory_space=pl.ANY)] * len(done[:2]),
                out_specs=[
                    pl.BlockSpec((t, c), lambda i, h: (at(i, h), 0)),
                    pl.BlockSpec((c, t), lambda i, h: (0, at(i, h))),
                ] + [pl.BlockSpec((2, EXTRA, c), lambda i, h: (i, 0, 0))] * 2,
                input_output_aliases={3: 0, 4: 1} if done else {}, name="widen",
            )

    def add(x, y, dtype, after=()):
        return call(add_kernel, [x, y], [shape(x.shape, dtype)] * 2, 1.0, after=after, name="add")

    class Tail:
        def __init__(self, x):
            self.bits = list(all_bits)
            self.x, self.got = x[0], partner(x[1], self.bits[0])

        def step(self, after=()):
            self.x, sent = add(self.x, self.got, F32, after)
            self.bits.pop(0)
            if self.bits:
                self.got = partner(sent, self.bits[0])
            return self.x


    turned_shape = shape((cols_here, rows_here, channels), F32)
    turned_spec = pl.BlockSpec(turned_shape.shape, lambda i: (0, 0, 0))

    def turn_back(x):
        return x.swapaxes(0, 1)

    def lon_forward(cells, table, after=()):
        return call(
            lambda *refs: lon_kernel(col_devs, row_group, *refs),
            [cells.reshape(flat_shape), table],
            [shape((half_rows, lats, LANES), BF)] * 2, 5.5, after=after,
            scratch_shapes=[pltpu.VMEM((all_rows * lats, LANES), F32)],
            vmem=24, name="lon_forward",
        )

    def lon_backward(pieces, table, after=()):
        return call(
            lambda *refs: lon_back_kernel(
                col_devs, row_group, len(pieces), refs[len(pieces)], *refs[: len(pieces)], refs[-1]
            ),
            [*pieces, table], shape(flat_shape, BF), 3.5, after=after, vmem=16, name="lon_backward",
        )

    def big_weight(w):
        w = lax.dynamic_index_in_dim(w, mine, 1, keepdims=False)
        gap = LANES - block
        w = jnp.pad(w, ((0, 0), (0, gap), (0, gap)))
        return jnp.concatenate(
            [jnp.concatenate([w[0], w[1]], 1), jnp.concatenate([-w[1], w[0]], 1)], 0
        )

    def big_bias(b):
        b = lax.dynamic_index_in_dim(b.reshape(2, BLOCKS, block), mine, 1, keepdims=False)
        return jnp.pad(b, ((0, 0), (0, LANES - block))).reshape(1, 2 * LANES)

    wa, wb = big_weight(mix_weight_a), big_weight(mix_weight_b)
    ba, bb = big_bias(mix_bias_a), big_bias(mix_bias_b)

    normed, send = call(
        first_kernel, [x5, mask, row(first_gain), row(first_shift)],
        [shape(pad_shape, BF), shape(packed_shape, BF)], 6.0,
        grid=(groups,), in_specs=[here_spec, mask_spec, row_spec, row_spec],
        out_specs=[pad_spec, packed_spec], vmem=16, name="first_norm",
    )
    cells = exchange(send.reshape(flat_shape))

    own, other = lon_forward(cells, lon_fwd)
    other = swap(other)
    own, other, modes = call(
        mix_kernel, [own, other, lat_fwd, lat_inv, wa, ba, wb, bb],
        [shape((lats, half_rows, LANES), BF)] * 2
        + [shape((slots_pad // 2, 2 * LAT, 2 * LANES), BF)], 22.0,
        scratch_shapes=[pltpu.VMEM((2 * lats * half_rows, LANES), F32)], vmem=32, name="mix",
    )
    other = swap(other)
    got = exchange(lon_backward([own, other], lon_winv))

    resid, tokens, cot_pad = call(
        second_kernel,
        [x5, normed, mask, cot5, got.reshape(packed_shape), row(second_gain), row(second_shift)],
        [shape(pad_shape, F32), shape(pad_shape, BF), shape(pad_shape, BF)], 8.5,
        grid=(groups,),
        in_specs=[here_spec, pad_spec, mask_spec, here_spec, packed_spec, row_spec, row_spec],
        out_specs=[pad_spec, pad_spec, pad_spec], vmem=20, name="second_norm",
    )
    tokens2, cot2 = tokens.reshape(-1, channels), cot_pad.reshape(-1, channels)
    count, hidden = tokens2.shape[0], expand_weight.shape[1]
    tile = hidden // 6
    all_tok = pl.BlockSpec((count, channels), lambda i: (0, 0))
    by_col = lambda n: pl.BlockSpec((n, tile), lambda i: (0, i))
    by_row = pl.BlockSpec((tile, channels), lambda i: (i, 0))
    act, gpre, gtok, g_ebias = call(
        chain_kernel,
        [tokens2, cot2, expand_weight, row(expand_bias), reduce_weight],
        [
            shape((count, hidden), BF), shape((count, hidden), BF),
            shape((count, channels), F32), shape((1, hidden), F32),
        ],
        25.0, grid=(6,),
        in_specs=[all_tok, all_tok, by_col(channels), by_col(1), by_row],
        out_specs=[by_col(count), by_col(count), all_tok, by_col(1)], vmem=46, name="mlp_chain",
    )

    halves = 3
    assert halves * CORES * tile == hidden

    def weight_grad(left, right, own, after, name):
        at = lambda i, c: (c[0] if own else 1 - c[0]) * halves + i
        return call(
            weight_grad_kernel, [left, right], shape((halves * tile, channels), BF), 5.0,
            after=after, prefetch=[core_line], grid=(halves,),
            in_specs=[
                pl.BlockSpec((count, tile), lambda i, c: (0, at(i, c))),
                pl.BlockSpec((count, channels), lambda i, c: (0, 0)),
            ],
            out_specs=[pl.BlockSpec((tile, channels), lambda i, c: (i, 0))], vmem=20, name=name,
        )

    one_row = shape((1, channels), F32)
    grad_resid, send, g_gain2, g_shift2, g_rbias = call(
        third_kernel,
        [resid, gtok.reshape(pad_shape), cot_pad, mask, row(second_gain)],
        [shape(pad_shape, F32), shape(packed_shape, BF)] + [one_row] * 3, 9.0,
        grid=(groups,), in_specs=[pad_spec, pad_spec, pad_spec, mask_spec, row_spec],
        out_specs=[pad_spec, packed_spec, row_spec, row_spec, row_spec], vmem=20, name="second_back",
    )
    cells = exchange(send.reshape(flat_shape))

    sent_r = weight_grad(act, cot2, False, [send], "reduce_grad")
    sent_e = weight_grad(gpre, tokens2, False, [sent_r], "expand_grad")
    kept_r = weight_grad(act, cot2, True, [sent_e], "reduce_grad")
    kept_e = weight_grad(gpre, tokens2, True, [kept_r], "expand_grad")
    sums = Sum([kept_r, kept_e], [partner(sent_r, 1), partner(sent_e, 1)])

    own, other = lon_forward(cells, lon_wfwd, after=[kept_e])
    other = swap(other)
    token = sums.halve(after=[own])
    run = half_rows // SPLIT
    pieces, grads = [], []
    grad_shape = shape((4 * LANES + 16, 2 * LANES), F32)
    for k in range(SPLIT):
        here = pl.BlockSpec((run, lats, LANES), lambda i, k=k: (k, 0, 0))
        steps = modes.shape[0] // SPLIT
        const = lambda x: pl.BlockSpec(x.shape, lambda i: (0, 0))
        o, t, g = call(
            mix_back_kernel, [own, other, modes, lat_fwd, lat_inv, wa, ba, wb, bb] + grads,
            [shape((lats, run, LANES), BF)] * 2 + [grad_shape], 13.0,
            after=[token],
            in_specs=[
                here, here, pl.BlockSpec((steps,) + modes.shape[1:], lambda i, k=k: (k, 0, 0)),
            ] + [const(x) for x in (lat_fwd, lat_inv, wa, ba, wb, bb, *grads)],
            scratch_shapes=[pltpu.VMEM((2 * lats * run, LANES), F32)], name="mix_back",
        )
        pieces.append((o, swap(t)))
        grads = [g]
        token = sums.halve(after=[o]) if k < SPLIT - 1 else o
    token = sums.settle(after=[o])
    send = lon_backward(
        [p[0] for p in pieces] + [p[1] for p in pieces], lon_inv, after=[token]
    )
    got = exchange(send)
    stay, leave = call(
        lambda *refs: collect_kernel(block, *refs), grads,
        [shape((3 * EXTRA, channels), F32)] * 2, 1.5, after=[send], prefetch=[core_line],
        name="collect",
    )
    token = sums.join(stay, partner(leave, 1))

    grad_inputs, g_gain1, g_shift1 = call(
        lambda *refs: last_kernel(rows_here, *refs), [x5, grad_resid, mask, got.reshape(packed_shape), row(first_gain)],
        [turned_shape] + [one_row] * 2, 9.0, after=[token],
        grid=(groups,), in_specs=[here_spec, pad_spec, mask_spec, packed_spec, row_spec],
        out_specs=[turned_spec, row_spec, row_spec], vmem=28, name="first_back",
    )
    tail_sum = Tail(
        call(
            tail_kernel, [g_gain1, g_shift1, g_gain2, g_shift2, g_rbias, g_ebias],
            [shape((1, 5 * channels + hidden), F32)] * 2, 1.0, name="tail",
        )
    )
    token = sums.part(after=[tail_sum.x])
    token = tail_sum.step(after=[token])
    token = sums.double(after=[token])
    token = tail_sum.step(after=[token])
    token = sums.double(after=[token])
    outputs = call(
        lambda *refs: branch_kernel(rows_here, *refs),
        [act.reshape(CORES, groups, PACK, cols_pad, hidden), reduce_weight, resid, row(reduce_bias)],
        turned_shape, 10.0, after=[token], grid=(groups,),
        in_specs=[
            lat_spec(cols_pad, hidden), pl.BlockSpec((hidden, channels), lambda i: (0, 0)),
            pad_spec, row_spec,
        ],
        out_specs=[turned_spec], vmem=32, name="branch",
    )

    token = tail_sum.step(after=[outputs])
    token = sums.double(after=[token])
    token = tail_sum.step(after=[token])
    own_done = sums.widen([], after=[token])
    token = own_done[0]
    while tail_sum.bits:
        token = tail_sum.step(after=[token])
    g_reduce, g_expand, *got_extra = sums.widen(own_done, after=[token])
    weight_out, bias_out = shape(mix_weight_a.shape, F32), shape(mix_bias_a.shape, F32)
    g_wa, g_wb, g_ba, g_bb = call(
        lambda *refs: spread_kernel(block, *refs), own_done[2:] + got_extra,
        [weight_out, weight_out, bias_out, bias_out], 3.0, prefetch=[core_line], name="spread",
    )

    tail = tail_sum.x
    g_gain1, g_shift1, g_gain2, g_shift2, g_rbias = (
        tail[0, k * channels : (k + 1) * channels] for k in range(5)
    )
    g_ebias = tail[0, 5 * channels :]

    def flat(v):
        return v.reshape(-1)

    return (
        turn_back(outputs), turn_back(grad_inputs),
        flat(g_gain1), flat(g_shift1), g_wa, g_ba, g_wb, g_bb, flat(g_gain2), flat(g_shift2),
        g_expand, g_ebias, g_reduce, flat(g_rbias),
    )


def solution(mesh):
    grid = P("rows", "cols", None)
    placed = (grid, P("rows", "cols"), grid) + (P(),) * 12
    return jax.shard_map(
        per_device,
        mesh=mesh,
        in_specs=placed,
        out_specs=(grid, grid) + (P(),) * 12,
        check_vma=False,
    )
```

```python
import math

import jax
import jax.numpy as jnp
import numpy as np
from jax import lax
from jax.experimental import pallas as pl
from jax.experimental.pallas import tpu as pltpu
from jax.sharding import PartitionSpec as P

BLOCKS = 8
LAT = 96
CORES = 2
PACK = 4
LANES = 128

shrink_level = 0.01
shrink_soft = 0.1
norm_eps = 1e-05
gelu_root = math.sqrt(2.0 / math.pi)
gelu_cube = 0.044715

BF = jnp.bfloat16
F32 = jnp.float32
AXES = ("rows", "cols")


def up_to(value, step):
    return (value + step - 1) // step * step


def call(kernel, args, out_shape, us, after=(), in_specs=None, prefetch=(), vmem=12, **kw):
    outs = out_shape if isinstance(out_shape, (list, tuple)) else [out_shape]
    lead, n_in, n_after = len(prefetch), len(args), len(after)

    def body(*refs):
        kernel(*refs[: lead + n_in], *refs[lead + n_in + n_after :])

    grid = kw.pop("grid", (1,))
    whole = lambda x: pl.BlockSpec(x.shape, lambda *_, n=len(x.shape): (0,) * n)
    specs = list(in_specs) if in_specs is not None else [whole(a) for a in args]
    specs += [pl.BlockSpec(memory_space=pl.ANY)] * n_after
    out_specs = kw.pop("out_specs", None) or [whole(o) for o in outs]
    got = pl.pallas_call(
        body,
        grid_spec=pltpu.PrefetchScalarGridSpec(
            num_scalar_prefetch=lead,
            grid=grid,
            in_specs=specs,
            out_specs=out_specs,
            scratch_shapes=kw.pop("scratch_shapes", ()),
        ),
        out_shape=outs,
        compiler_params=pltpu.CompilerParams(vmem_limit_bytes=vmem * 1024 * 1024),
        cost_estimate=pl.CostEstimate(
            flops=0, bytes_accessed=int(us * 1e5), transcendentals=0
        ),
        **kw,
    )(*prefetch, *args, *after)
    return list(got) if isinstance(out_shape, (list, tuple)) else got[0]


SPLIT = 2
UNROLL = 2


def lon_table(lon_size, col_devs, cols_here, cols_pad, slots, slots_pad):
    modes = lon_size // 2 + 1
    table = np.zeros((CORES, 2, slots_pad, col_devs, cols_pad), np.float64)
    weights = np.zeros((CORES, slots_pad), np.float64)
    place = np.arange(lon_size).reshape(col_devs, cols_here)
    for half in range(CORES):
        for slot in range(slots):
            mode = half * slots + slot
            if mode >= modes:
                continue
            angle = (place * mode % lon_size) * (2.0 * math.pi / lon_size)
            table[half, 0, slot, :, :cols_here] = np.cos(angle) / math.sqrt(lon_size)
            edge = mode == 0 or 2 * mode == lon_size
            if not edge:
                table[half, 1, slot, :, :cols_here] = np.sin(angle) / math.sqrt(lon_size)
            weights[half, slot] = 1.0 if edge else 2.0
    weighted = table * weights[:, None, :, None, None]
    rows = 2 * slots_pad
    flat = [
        a.reshape(CORES, 2, SPLIT, slots_pad // SPLIT, col_devs, cols_pad)
        .swapaxes(1, 2)
        .reshape(CORES, rows, col_devs * cols_pad)
        for a in (table, weighted)
    ]
    return [
        np.stack([np.concatenate([a[h], a[1 - h]], 0) for h in range(CORES)]) for a in flat
    ]


def lat_table(rows_here, row_group):
    share = rows_here // CORES
    out = []
    for h in range(CORES):
        own = [
            rows_here * r + share * h + i for r in range(row_group) for i in range(share)
        ]
        other = [
            rows_here * r + share * (1 - h) + i for r in range(row_group) for i in range(share)
        ]
        angle = np.outer(np.arange(LAT), np.array(own + other)) % LAT * (2.0 * math.pi / LAT)
        cos, sin = np.cos(angle) / math.sqrt(LAT), np.sin(angle) / math.sqrt(LAT)
        out.append(np.block([[cos, -sin], [-sin, -cos]]))
    return np.stack(out)


def pack_lanes(tiles):
    a, b, c, d = tiles
    lane = lax.broadcasted_iota(jnp.int32, a.shape, a.ndim - 1)
    axis = a.ndim - 1
    b, c, d = pltpu.roll(b, 96, axis), pltpu.roll(c, 64, axis), pltpu.roll(d, 32, axis)
    return [
        jnp.where(lane < 96, a, b),
        jnp.where(lane < 64, b, c),
        jnp.where(lane < 32, c, d),
    ]


def unpack_lanes(tiles):
    a, b, c = tiles
    lane = lax.broadcasted_iota(jnp.int32, a.shape, a.ndim - 1)
    axis = a.ndim - 1
    return [
        a,
        pltpu.roll(jnp.where(lane >= 96, a, b), 32, axis),
        pltpu.roll(jnp.where(lane >= 64, b, c), 64, axis),
        pltpu.roll(c, 96, axis),
    ]


def tiles_of(value):
    return [value[:, LANES * i : LANES * (i + 1)] for i in range(value.shape[1] // LANES)]


def split_blocks(value):
    tiles = tiles_of(value)
    out = []
    for i in range(0, len(tiles), 3):
        out += unpack_lanes(tiles[i : i + 3])
    return out


def join_blocks(tiles):
    out = []
    for i in range(0, len(tiles), 4):
        out += pack_lanes(tiles[i : i + 4])
    return jnp.concatenate(out, axis=1)


def pad_rows(value, rows):
    return jnp.concatenate(
        [value, jnp.zeros((rows - value.shape[0], value.shape[1]), value.dtype)], axis=0
    )


def store_packed(ref, half, per_lat):
    split = [split_blocks(v) for v in per_lat]
    for q in range(BLOCKS):
        packed = pack_lanes([split[j][q] for j in range(PACK)])
        ref[q, half, 0] = jnp.concatenate(packed, axis=1).astype(ref.dtype)


def load_packed(ref, half):
    by_lat = [[] for _ in range(PACK)]
    for q in range(BLOCKS):
        parts = unpack_lanes(tiles_of(ref[q, half, 0].astype(F32)))
        for j in range(PACK):
            by_lat[j].append(parts[j])
    return [join_blocks(tiles) for tiles in by_lat]


def stats(x):
    average = jnp.mean(x, axis=-1, keepdims=True)
    centred = x - average
    spread = jnp.mean(centred * centred, axis=-1, keepdims=True)
    inv = lax.rsqrt(spread + norm_eps)
    return centred * inv, inv


def norm_back(grad, xhat, inv, gain):
    scaled = grad * gain
    m1 = jnp.mean(scaled, axis=-1, keepdims=True)
    m2 = jnp.mean(scaled * xhat, axis=-1, keepdims=True)
    return inv * (scaled - m1 - xhat * m2)


def mask_column(mask_ref, lat, rows):
    line = mask_ref[pl.ds(lat, 1), :].astype(F32)
    shape = (rows, line.shape[1])
    row, col = (lax.broadcasted_iota(jnp.int32, shape, k) for k in range(2))
    return jnp.sum(jnp.where(row == col, line, 0.0), axis=1, keepdims=True)


def first_kernel(x_ref, mask_ref, gain_ref, shift_ref, normed_ref, out_ref):
    rows = normed_ref.shape[3]
    half, first = 0, pl.program_id(0) * PACK
    lats = []
    for j in range(PACK):
        x = pad_rows(x_ref[half, 0, j].astype(F32), rows)
        xhat, _ = stats(x)
        y = mask_column(mask_ref, first + j, rows) * (xhat * gain_ref[...] + shift_ref[...])
        normed_ref[half, 0, j] = y.astype(BF)
        lats.append(y)
    store_packed(out_ref, half, lats)


def second_kernel(
    x_ref, normed_ref, mask_ref, cot_ref, got_ref, gain_ref, shift_ref, resid_ref, tok_ref, cot_out
):
    rows = normed_ref.shape[3]
    half, first = 0, pl.program_id(0) * PACK
    spatial = load_packed(got_ref, half)
    for j in range(PACK):
        x = pad_rows(x_ref[half, 0, j].astype(F32), rows)
        resid = x + normed_ref[half, 0, j].astype(F32)
        resid = resid + mask_column(mask_ref, first + j, rows) * spatial[j]
        resid_ref[half, 0, j] = resid
        xhat, _ = stats(resid)
        tok_ref[half, 0, j] = (xhat * gain_ref[...] + shift_ref[...]).astype(BF)
        cot_out[half, 0, j] = pad_rows(cot_ref[half, 0, j].astype(F32), rows).astype(BF)


def third_kernel(
    resid_ref, gtok_ref, cot_ref, mask_ref, gain_ref,
    gresid_ref, send_ref, ggain_ref, gshift_ref, gbias_ref,
):
    @pl.when(pl.program_id(0) == 0)
    def _():
        ggain_ref[...] = jnp.zeros_like(ggain_ref)
        gshift_ref[...] = jnp.zeros_like(gshift_ref)
        gbias_ref[...] = jnp.zeros_like(gbias_ref)

    half, first = 0, pl.program_id(0) * PACK
    lats = []
    for j in range(PACK):
        xhat, inv = stats(resid_ref[half, 0, j])
        gtok = gtok_ref[half, 0, j]
        cot = cot_ref[half, 0, j].astype(F32)
        ggain_ref[...] += jnp.sum(gtok * xhat, axis=0, keepdims=True)
        gshift_ref[...] += jnp.sum(gtok, axis=0, keepdims=True)
        gbias_ref[...] += jnp.sum(cot, axis=0, keepdims=True)
        gres = cot + norm_back(gtok, xhat, inv, gain_ref[...])
        gresid_ref[half, 0, j] = gres
        lats.append(mask_column(mask_ref, first + j, gres.shape[0]) * gres)
    store_packed(send_ref, half, lats)


def store_lat(out_ref, lat, value):
    out_ref[:, lat, :] = value[: out_ref.shape[0]]


def last_kernel(
    x_ref, gresid_ref, mask_ref, got_ref, gain_ref, out_ref, ggain_ref, gshift_ref
):
    @pl.when(pl.program_id(0) == 0)
    def _():
        ggain_ref[...] = jnp.zeros_like(ggain_ref)
        gshift_ref[...] = jnp.zeros_like(gshift_ref)

    rows = gresid_ref.shape[3]
    half, first = 0, pl.program_id(0) * PACK
    got = load_packed(got_ref, half)
    for j in range(PACK):
        x = pad_rows(x_ref[half, 0, j].astype(F32), rows)
        xhat, inv = stats(x)
        gres = gresid_ref[half, 0, j]
        grad = mask_column(mask_ref, first + j, rows) * (gres + got[j])
        ggain_ref[...] += jnp.sum(grad * xhat, axis=0, keepdims=True)
        gshift_ref[...] += jnp.sum(grad, axis=0, keepdims=True)
        store_lat(out_ref, first + j, gres + norm_back(grad, xhat, inv, gain_ref[...]))


OUTER = (((0,), (0,)), ((), ()))
ACROSS = (((1,), (1,)), ((), ()))


def chain_kernel(
    tok_ref, cot_ref, up_ref, bias_ref, down_ref, act_ref, gpre_ref, gtok_ref, gbias_ref
):
    @pl.when(pl.program_id(0) == 0)
    def _():
        gtok_ref[...] = jnp.zeros_like(gtok_ref)

    pre = jnp.dot(tok_ref[...], up_ref[...], preferred_element_type=F32) + bias_ref[...]
    squash = gelu_parts(pre)
    act_ref[...] = (0.5 * pre * (1.0 + squash)).astype(BF)
    gact = lax.dot_general(cot_ref[...], down_ref[...], ACROSS, preferred_element_type=F32)
    gpre = gelu_slope(pre, squash) * gact
    gbias_ref[...] = jnp.sum(gpre, axis=0, keepdims=True)
    gpre = gpre.astype(BF)
    gpre_ref[...] = gpre
    gtok_ref[...] += lax.dot_general(gpre, up_ref[...], ACROSS, preferred_element_type=F32)


def weight_grad_kernel(core_ref, left_ref, right_ref, out_ref):
    out_ref[...] = lax.dot_general(
        left_ref[...], right_ref[...], OUTER, preferred_element_type=F32
    ).astype(BF)


def branch_kernel(act_ref, down_ref, resid_ref, bias_ref, out_ref):
    cols = resid_ref.shape[3]
    rows = CORES * PACK * cols
    act = act_ref[...].reshape(rows, act_ref.shape[-1])
    branch = jnp.dot(act, down_ref[...], preferred_element_type=F32) + bias_ref[...]
    for half in range(CORES):
        for j in range(PACK):
            at = (half * PACK + j) * cols
            lat = (half * pl.num_programs(0) + pl.program_id(0)) * PACK + j
            store_lat(out_ref, lat, resid_ref[half, 0, j] + branch[at : at + cols])


def plus(left, right):
    return (left.astype(F32) + right.astype(F32)).astype(BF)


def halve_first_kernel(bits_ref, *refs):
    count = len(refs) // 6
    for p in range(count):
        a, b, c, d = refs[4 * p : 4 * p + 4]
        low, high = plus(a[...], b[...]), plus(c[...], d[...])
        first = bits_ref[p] == 0
        refs[4 * count + 2 * p][...] = jnp.where(first, low, high)
        refs[4 * count + 2 * p + 1][...] = jnp.where(first, high, low)


def halve_kernel(bits_ref, *refs):
    count = len(refs) // 6
    for k in range(2 * count):
        refs[4 * count + k][...] = plus(refs[2 * k][...], refs[2 * k + 1][...])


def join_kernel(count, *refs):
    stay, got = refs[count : count + 2]
    for p in range(count):
        n, m = refs[p].shape[0], stay.shape[0] // count
        value = refs[p][...]
        rows = slice(p * m, (p + 1) * m)
        extra = (stay[rows] + got[rows]).astype(BF)
        for out in refs[-2:]:
            out[p * (n + m) : p * (n + m) + n] = value
            out[p * (n + m) + n : (p + 1) * (n + m)] = extra


def settle_kernel(count, *refs):
    for p in range(count):
        refs[2 * count + p][...] = plus(refs[2 * p][...], refs[2 * p + 1][...])


def touch_kernel(out):
    out[...] = jnp.zeros_like(out)


def part_kernel(kept, got, *outs):
    n, count = outs[0].shape[0], len(outs) // 2
    for p in range(count):
        rows = slice(p * n, (p + 1) * n)
        value = plus(kept[rows], got[rows])
        outs[p][...] = value
        outs[count + p][...] = value


def add_kernel(left, right, *outs):
    value = left[...].astype(F32) + right[...].astype(F32)
    for out in outs:
        out[...] = value.astype(out.dtype)


def tail_kernel(*refs):
    for out in refs[-2:]:
        at = 0
        for ref in refs[:-2]:
            out[:, at : at + ref.shape[1]] = ref[...]
            at += ref.shape[1]


def merge_kernel(count, single, bits_ref, *refs):
    outs = refs[2 * count :]
    for p in range(count):
        own, got = refs[2 * p], refs[2 * p + 1]
        n = own.shape[0]
        for out in (outs[p::count] if not single else [o.at[p] for o in outs]):
            out[pl.ds(pl.multiple_of(bits_ref[p] * n, 16), n), :] = own[...]
            out[pl.ds(pl.multiple_of((1 - bits_ref[p]) * n, 16), n), :] = got[...]


def widen_kernel(core_ref, reduce_ref, expand_ref, *refs):
    reduce_out, expand_out, extra_r, extra_e = refs[-4:]
    n = reduce_out.shape[0] // 2
    for k in range(2):
        at = k * (n + EXTRA)
        reduce_out[k * n : (k + 1) * n] = reduce_ref[at : at + n].astype(F32)
        expand_out[:, k * n : (k + 1) * n] = expand_ref[at : at + n].astype(F32).T
        extra_r[k] = reduce_ref[at + n : at + n + EXTRA]
        extra_e[k] = expand_ref[at + n : at + n + EXTRA]


EXTRA = 16


def collect_kernel(block, core_ref, grad_ref, *refs):
    wide = 2 * LANES
    halves, lines = [], []
    for i in range(2):
        g = grad_ref[i * wide : (i + 1) * wide]
        at = 2 * wide + 8 * i
        line = jnp.sum(grad_ref[at : at + 8], axis=0, keepdims=True)
        top, low = g[:block], g[LANES : LANES + block]
        halves.append([top[:, :LANES] + low[:, LANES:], top[:, LANES:] - low[:, :LANES]])
        lines += [line[:, :LANES], line[:, LANES:]]
    rows = lax.broadcasted_iota(jnp.int32, (EXTRA, LANES), 0)
    bias = sum(jnp.where(rows == k, line, 0.0) for k, line in enumerate(lines))
    first = core_ref[0] == 0
    for k, out in enumerate(refs[-2:]):
        own = first if k == 0 else jnp.logical_not(first)
        out[...] = jnp.zeros_like(out)
        for p in range(2):
            value = jnp.where(own, halves[0][p], halves[1][p])
            for t in range(block // EXTRA):
                at = slice(t * LANES, (t + 1) * LANES)
                out[p * EXTRA : (p + 1) * EXTRA, at] = value[t * EXTRA : (t + 1) * EXTRA]
        out[2 * EXTRA : 3 * EXTRA, :LANES] = jnp.where(own, bias, 0.0)


def spread_kernel(block, core_ref, *refs):
    own, got = refs[:2], refs[2:4]
    wa_ref, wb_ref, ba_ref, bb_ref = refs[4:]
    first = core_ref[0] == 0
    per = own[0].shape[0]
    biases = [[] for _ in range(4)]
    for q in range(BLOCKS):
        for half in range(CORES):
            for p in range(3):
                if half == 1 and p == 2:
                    continue
                k = sum(((q >> ((p + j) % 3)) & 1) << (2 - j) for j in range(3))
                at = p * BLOCKS + k
                mine, other = (r[at // per][at % per].astype(F32) for r in (own, got))
                value = jnp.where(first, mine, other) if half == 0 else jnp.where(first, other, mine)
                if p == 2:
                    for i in range(4):
                        biases[i].append(value[i : i + 1, :LANES])
                    continue
                out = wb_ref if half else wa_ref
                for t in range(block // EXTRA):
                    out[p, q, t * EXTRA : (t + 1) * EXTRA, :] = value[
                        :, t * LANES : t * LANES + block
                    ]
    for i in range(4):
        (bb_ref if i > 1 else ba_ref)[i % 2 : i % 2 + 1, :] = join_blocks(biases[i])


def lon_kernel(col_devs, row_group, x_ref, table_ref, own_ref, other_ref, turn_ref):
    groups = x_ref.shape[1]
    rows = table_ref.shape[0]
    lats = own_ref.shape[1]
    slots = own_ref.shape[0]
    for r in range(row_group):
        for g in range(groups):
            cells = jnp.concatenate(
                [x_ref[r * col_devs + c, g] for c in range(col_devs)], axis=0
            )
            modes = jnp.dot(table_ref[...], cells, preferred_element_type=F32)
            for j, tile in enumerate(unpack_lanes(tiles_of(modes))):
                at = (r * groups + g) * PACK + j
                turn_ref[pl.ds(at, rows, stride=lats), :] = tile

    @pl.loop(0, slots)
    def _(s):
        own_ref[s] = turn_ref[pl.ds(pl.multiple_of(s * lats, 8), lats), :].astype(BF)
        other_ref[s] = turn_ref[
            pl.ds(pl.multiple_of((s + slots) * lats, 8), lats), :
        ].astype(BF)


def lon_back_kernel(col_devs, row_group, pieces, table_ref, *refs):
    out_ref = refs[pieces]
    groups = out_ref.shape[1]
    cols = out_ref.shape[2]
    for r in range(row_group):
        for g in range(groups):
            tiles = []
            for j in range(0, PACK, 2):
                pair = []
                for k in range(2):
                    at = (r * groups + g) * PACK + j + k
                    pair.append(jnp.concatenate([r_[at] for r_ in refs[:pieces]], axis=0))
                cells = jnp.dot(
                    table_ref[...], jnp.concatenate(pair, axis=1), preferred_element_type=F32
                )
                tiles += tiles_of(cells)
            packed = jnp.concatenate(pack_lanes(tiles), axis=1).astype(BF)
            for c in range(col_devs):
                out_ref[r * col_devs + c, g] = packed[c * cols : (c + 1) * cols]


def gelu_parts(v):
    squash = jnp.tanh(gelu_root * (v + gelu_cube * (v * v * v)))
    return squash


def gelu(v):
    return 0.5 * v * (1.0 + gelu_parts(v))


def gelu_slope(v, squash):
    inner = gelu_root * (1.0 + 3.0 * gelu_cube * (v * v))
    return 0.5 * (1.0 + squash) + 0.5 * v * (1.0 - squash * squash) * inner


def latitudes(own_ref, other_ref, row, run):
    return jnp.concatenate(
        [own_ref[row], other_ref[row], own_ref[row + run], other_ref[row + run]], axis=0
    )


def turn_out(turn_ref, value, row, lats, rows, run):
    for part in range(2):
        for dest in range(2):
            piece = value[(2 * part + dest) * lats : (2 * part + dest + 1) * lats]
            start = dest * lats * rows + part * run + row
            turn_ref[pl.ds(start, lats, stride=rows), :] = piece


def drain(turn_ref, own_ref, other_ref):
    lats, rows = own_ref.shape[0], own_ref.shape[1]

    @pl.loop(0, lats)
    def _(at):
        own_ref[at] = turn_ref[pl.ds(pl.multiple_of(at * rows, 8), rows), :].astype(BF)
        other_ref[at] = turn_ref[
            pl.ds(pl.multiple_of((at + lats) * rows, 8), rows), :
        ].astype(BF)


def mix_kernel(
    own_ref, other_ref, lat_ref, back_ref, wa_ref, ba_ref, wb_ref, bb_ref,
    own_out, other_out, modes_out, turn_ref,
):
    lats, rows = own_ref.shape[1], own_ref.shape[0]
    run = rows // 2 // SPLIT

    @pl.loop(0, rows // 4, unroll=UNROLL)
    def _(step):
        slot = 2 * step
        row = slot + slot // run * run
        cells = jnp.concatenate(
            [latitudes(own_ref, other_ref, row + k, run) for k in range(2)], axis=1
        )
        full = jnp.dot(lat_ref[...], cells, preferred_element_type=F32).astype(BF)
        real, imag = full[:LAT], full[LAT:]
        modes = jnp.concatenate(
            [
                jnp.concatenate([real[:, :LANES], imag[:, :LANES]], axis=1),
                jnp.concatenate([real[:, LANES:], imag[:, LANES:]], axis=1),
            ],
            axis=0,
        )
        modes_out[step] = modes
        pre_a = jnp.dot(modes, wa_ref[...], preferred_element_type=F32) + ba_ref[...]
        hidden = gelu(pre_a).astype(BF)
        pre_b = jnp.dot(hidden, wb_ref[...], preferred_element_type=F32) + bb_ref[...]
        shrunk = (pre_b - shrink_level * jnp.tanh(pre_b * (1.0 / shrink_soft))).astype(BF)
        mixed = jnp.concatenate(
            [
                jnp.concatenate([shrunk[:LAT, :LANES], shrunk[LAT:, :LANES]], axis=1),
                jnp.concatenate([shrunk[:LAT, LANES:], shrunk[LAT:, LANES:]], axis=1),
            ],
            axis=0,
        )
        back = jnp.dot(back_ref[...], mixed, preferred_element_type=F32)
        for k in range(2):
            turn_out(turn_ref, back[:, k * LANES : (k + 1) * LANES], row + k, lats, rows, run)

    drain(turn_ref, own_out, other_out)


def row_sums(value):
    return jnp.sum(value.reshape(-1, 8, value.shape[1]), axis=0)


def mix_back_kernel(
    own_ref, other_ref, modes_ref, lat_ref, back_ref, wa_ref, ba_ref, wb_ref, bb_ref,
    *refs,
):
    own_out, other_out, grad_ref, turn_ref = refs[-4:]
    lats, rows = own_ref.shape[1], own_ref.shape[0]
    run = rows // 2
    grad_ref[...] = refs[0][...] if len(refs) > 4 else jnp.zeros_like(grad_ref)
    wide = wa_ref.shape[0]
    gwa_ref, gwb_ref = grad_ref.at[:wide], grad_ref.at[wide : 2 * wide]
    gba_ref, gbb_ref = grad_ref.at[2 * wide : 2 * wide + 8], grad_ref.at[2 * wide + 8 :]

    @pl.loop(0, run // 2, unroll=UNROLL)
    def _(step):
        row = 2 * step
        cells = jnp.concatenate(
            [latitudes(own_ref, other_ref, row + k, run) for k in range(2)], axis=1
        )
        full = jnp.dot(lat_ref[...], cells, preferred_element_type=F32)
        real, imag = full[:LAT], full[LAT:]
        grad = jnp.concatenate(
            [
                jnp.concatenate([real[:, :LANES], imag[:, :LANES]], axis=1),
                jnp.concatenate([real[:, LANES:], imag[:, LANES:]], axis=1),
            ],
            axis=0,
        )
        modes = modes_ref[step]
        pre_a = jnp.dot(modes, wa_ref[...], preferred_element_type=F32) + ba_ref[...]
        squash_a = gelu_parts(pre_a)
        hidden = (0.5 * pre_a * (1.0 + squash_a)).astype(BF)
        pre_b = jnp.dot(hidden, wb_ref[...], preferred_element_type=F32) + bb_ref[...]
        squash_b = jnp.tanh(pre_b * (1.0 / shrink_soft))
        factor = 1.0 - shrink_level / shrink_soft * (1.0 - squash_b * squash_b)
        grad_b = factor * grad
        gbb_ref[...] += row_sums(grad_b)
        grad_b = grad_b.astype(BF)
        grad_hidden = lax.dot_general(grad_b, wb_ref[...], ACROSS, preferred_element_type=F32)
        gwb_ref[...] += lax.dot_general(hidden, grad_b, OUTER, preferred_element_type=F32)
        grad_a = gelu_slope(pre_a, squash_a) * grad_hidden
        gba_ref[...] += row_sums(grad_a)
        grad_a = grad_a.astype(BF)
        grad_modes = lax.dot_general(
            grad_a, wa_ref[...], ACROSS, preferred_element_type=F32
        ).astype(BF)
        gwa_ref[...] += lax.dot_general(modes, grad_a, OUTER, preferred_element_type=F32)
        mixed = jnp.concatenate(
            [
                jnp.concatenate([grad_modes[:LAT, :LANES], grad_modes[LAT:, :LANES]], axis=1),
                jnp.concatenate([grad_modes[:LAT, LANES:], grad_modes[LAT:, LANES:]], axis=1),
            ],
            axis=0,
        )
        back = jnp.dot(back_ref[...], mixed, preferred_element_type=F32)
        for k in range(2):
            turn_out(turn_ref, back[:, k * LANES : (k + 1) * LANES], row + k, lats, rows, run)

    drain(turn_ref, own_out, other_out)


def per_device(
    inputs, valid_mask, cotangent, first_gain, first_shift, mix_weight_a, mix_bias_a,
    mix_weight_b, mix_bias_b, second_gain, second_shift, expand_weight, expand_bias,
    reduce_weight, reduce_bias,
):
    row_devs = lax.axis_size("rows")
    col_devs = lax.axis_size("cols")
    rows_here, cols_here, channels = inputs.shape
    block = channels // BLOCKS
    lon_size = cols_here * col_devs
    cols_pad = up_to(cols_here, 16)
    row_group = LAT // rows_here
    members = row_group * col_devs
    share = rows_here // CORES
    groups = share // PACK
    slots = (lon_size // 2 + 2) // 2
    slots_pad = up_to(slots, 16)
    lats = share * row_group
    half_rows = 2 * slots_pad
    all_rows = CORES * half_rows
    assert members == CORES * BLOCKS and block * PACK == 3 * LANES
    assert col_devs * cols_pad == all_rows and CORES * lats == LAT

    row_at, col_at = lax.axis_index("rows"), lax.axis_index("cols")
    core = col_at % CORES
    mine = (row_at % row_group) * (col_devs // CORES) + col_at // CORES

    def pick(table):
        return lax.dynamic_index_in_dim(jnp.asarray(table, BF), core, 0, keepdims=False)

    plain_np, weighted_np = lon_table(
        lon_size, col_devs, cols_here, cols_pad, slots, slots_pad
    )
    lat_np = lat_table(rows_here, row_group)
    lon_fwd, lon_wfwd = pick(plain_np), pick(weighted_np)
    lon_inv, lon_winv = (
        pick(np.swapaxes(plain_np, 1, 2)), pick(np.swapaxes(weighted_np, 1, 2))
    )
    lat_fwd, lat_inv = pick(lat_np), pick(np.swapaxes(lat_np, 1, 2))

    snap_groups = [
        [(s * row_group + r) * col_devs + c for r in range(row_group) for c in range(col_devs)]
        for s in range(row_devs // row_group)
    ]
    core_pairs = [
        (r * col_devs + c, r * col_devs + c ^ 1) for r in range(row_devs) for c in range(col_devs)
    ]

    def exchange(x):
        return lax.all_to_all(x, AXES, 0, 0, axis_index_groups=snap_groups, tiled=True)

    def swap(x):
        return lax.ppermute(x, AXES, core_pairs)

    def fold(x):
        return x.reshape((CORES, groups, PACK) + x.shape[1:])

    def row(v):
        return v.reshape(1, -1)

    x5, cot5 = fold(inputs), fold(cotangent)

    def lat_spec(cols, width):
        return pl.BlockSpec(
            (1, 1, PACK, cols, width), lambda i: (i // groups, i % groups, 0, 0, 0)
        )

    def both_spec(cols, width):
        return pl.BlockSpec((CORES, 1, PACK, cols, width), lambda i: (0, i, 0, 0, 0))

    packed_spec = pl.BlockSpec(
        (BLOCKS, 1, 1, cols_pad, 3 * LANES), lambda i: (0, i // groups, i % groups, 0, 0)
    )
    lat_steps = CORES * groups
    row_spec = pl.BlockSpec((1, channels), lambda i: (0, 0))
    here_spec, pad_spec = lat_spec(cols_here, channels), lat_spec(cols_pad, channels)
    mask, mask_spec = valid_mask, pl.BlockSpec((rows_here, cols_here), lambda i: (0, 0))
    packed_shape = (BLOCKS, CORES, groups, cols_pad, 3 * LANES)
    flat_shape = (members, groups, cols_pad, 3 * LANES)
    pad_shape = (CORES, groups, PACK, cols_pad, channels)
    here_shape = (CORES, groups, PACK, cols_here, channels)

    def shape(s, d):
        return jax.ShapeDtypeStruct(s, d)

    index = row_at * col_devs + col_at
    devices = row_devs * col_devs
    all_bits = [2**k for k in range(16) if 2**k < devices]
    cube, outer_bits = all_bits[1:4], all_bits[4:]
    core_line = core.astype(jnp.int32).reshape(1)

    def bit(mask_bit):
        return (index // mask_bit) % 2

    def partner(x, flip):
        return lax.ppermute(x, AXES, [(d, d ^ flip) for d in range(devices)])


    orders = [[cube[(p + k) % 3] for k in range(3)] for p in range(3)]

    def bits(level):
        return jnp.stack([bit(o[level]) for o in orders]).astype(jnp.int32)

    def zipped(kept, got):
        return [x for pair in zip(kept, got) for x in pair]

    def merge(own, got, which, single, after):
        n, (r, c) = len(own), own[0].shape
        out = [shape((n, 2 * r, c), BF)] * 2 if single else [shape((2 * r, c), BF)] * (2 * n)
        return call(
            lambda *refs: merge_kernel(n, single, *refs), zipped(own, got), out, 2.0,
            after=after, prefetch=[which], vmem=34 if single else 12, name="merge",
        )

    class Sum:
        def __init__(self, kept, got):
            self.kept, self.got, self.level = kept, got, 0

        def send(self, arrays):
            self.got = [partner(x, o[self.level]) for x, o in zip(arrays, orders)]

        def halve(self, after=()):
            first, n = self.level == 0, len(orders)
            rows, wide = self.kept[0].shape
            half = rows // n if first else rows // 2
            tiles = 2 if first else 1
            t = half // tiles
            args, specs = [], []
            if first:
                for chunk in range(2 * n):
                    grad, at = divmod(chunk, n)
                    args += [self.kept[grad], self.got[grad]]
                    specs += [pl.BlockSpec((t, wide), lambda i, b, at=at: (at * tiles + i, 0))] * 2
            else:
                for p in range(n):
                    stay = lambda i, b, p=p: (b[p] * tiles + i, 0)
                    leave = lambda i, b, p=p: ((1 - b[p]) * tiles + i, 0)
                    args += [self.kept[p], self.got[p]] * 2
                    specs += [pl.BlockSpec((t, wide), m) for m in (stay, stay, leave, leave)]
            res = call(
                halve_first_kernel if first else halve_kernel,
                args, [shape((half, wide), BF)] * (2 * n), 3.0,
                after=after, prefetch=[bits(self.level)], grid=(tiles,), in_specs=specs,
                out_specs=[pl.BlockSpec((t, wide), lambda i, b: (i, 0))] * (2 * n), vmem=20 if first else 12, name="halve",
            )
            self.kept = res[0::2]
            self.send(res[1::2])
            self.level += 1
            return self.kept[0]

        def settle(self, after=()):
            n = len(orders)
            self.kept = call(
                lambda *refs: settle_kernel(n, *refs), zipped(self.kept, self.got),
                [shape(x.shape, BF) for x in self.kept], 1.0, after=after, name="settle",
            )
            return self.kept[0]

        def join(self, stay, got, after=()):
            n, (r, c) = len(orders), self.kept[0].shape
            self.kept, sent = call(
                lambda *refs: join_kernel(n, *refs), self.kept + [stay, got],
                [shape((n * (r + EXTRA), c), BF)] * 2, 1.5, after=after, name="join",
            )
            self.got = partner(sent, outer_bits[0])
            for m in outer_bits[1:]:
                self.kept, sent = add(self.kept, self.got, BF)
                self.got = partner(sent, m)
            return self.kept

        def part(self, after=()):
            n, (r, c) = len(orders), self.kept.shape
            res = call(
                part_kernel, [self.kept, self.got], [shape((r // n, c), BF)] * (2 * n), 1.5,
                after=after, name="part",
            )
            self.kept = res[:n]
            self.level = len(cube) - 1
            self.send(res[n:])
            return self.kept[0]

        def double(self, after=()):
            n, (r, c), single = len(orders), self.kept[0].shape, self.level == 0
            res = merge(self.kept, self.got, bits(self.level), single, after)
            self.level -= 1
            if not single:
                self.kept = res[:n]
                self.send(res[n:])
                return self.kept[0]
            self.kept, sent = (x.reshape(2 * n * r, c) for x in res)
            self.got = partner(sent, 1)
            return self.kept

        def widen(self, done, after=()):
            rows, c = self.kept.shape
            chunk = rows // (len(orders) * BLOCKS)
            t = 2 * (chunk - EXTRA)
            steps = rows // chunk // 4
            full_rows = CORES * steps * t
            x = self.got if done else self.kept
            full = [shape((full_rows, c), F32), shape((c, full_rows), F32)]
            extra = [shape((2 * steps, EXTRA, c), BF)] * 2
            at = lambda i, h: (1 - h[0] if done else h[0]) * steps + i
            return call(
                widen_kernel, [x, x] + done[:2], full + extra, 5.0, after=after,
                prefetch=[core_line], grid=(steps,),
                in_specs=[
                    pl.BlockSpec((2 * chunk, c), lambda i, h: (i, 0)),
                    pl.BlockSpec((2 * chunk, c), lambda i, h: (steps + i, 0)),
                ] + [pl.BlockSpec(memory_space=pl.ANY)] * len(done[:2]),
                out_specs=[
                    pl.BlockSpec((t, c), lambda i, h: (at(i, h), 0)),
                    pl.BlockSpec((c, t), lambda i, h: (0, at(i, h))),
                ] + [pl.BlockSpec((2, EXTRA, c), lambda i, h: (i, 0, 0))] * 2,
                input_output_aliases={3: 0, 4: 1} if done else {}, name="widen",
            )

    def add(x, y, dtype, after=()):
        return call(add_kernel, [x, y], [shape(x.shape, dtype)] * 2, 1.0, after=after, name="add")

    class Tail:
        def __init__(self, x):
            self.bits = list(all_bits)
            self.x, self.got = x[0], partner(x[1], self.bits[0])

        def step(self, after=()):
            self.x, sent = add(self.x, self.got, F32, after)
            self.bits.pop(0)
            if self.bits:
                self.got = partner(sent, self.bits[0])
            return self.x


    turned_shape = shape((cols_here, rows_here, channels), F32)
    turned_spec = pl.BlockSpec(turned_shape.shape, lambda i: (0, 0, 0))

    def turn_back(x):
        return x.swapaxes(0, 1)

    def lon_forward(cells, table, after=()):
        return call(
            lambda *refs: lon_kernel(col_devs, row_group, *refs),
            [cells.reshape(flat_shape), table],
            [shape((half_rows, lats, LANES), BF)] * 2, 5.5, after=after,
            scratch_shapes=[pltpu.VMEM((all_rows * lats, LANES), F32)],
            vmem=24, name="lon_forward",
        )

    def lon_backward(pieces, table, after=()):
        return call(
            lambda *refs: lon_back_kernel(
                col_devs, row_group, len(pieces), refs[len(pieces)], *refs[: len(pieces)], refs[-1]
            ),
            [*pieces, table], shape(flat_shape, BF), 3.5, after=after, vmem=16, name="lon_backward",
        )

    def big_weight(w):
        w = lax.dynamic_index_in_dim(w, mine, 1, keepdims=False)
        gap = LANES - block
        w = jnp.pad(w, ((0, 0), (0, gap), (0, gap)))
        return jnp.concatenate(
            [jnp.concatenate([w[0], w[1]], 1), jnp.concatenate([-w[1], w[0]], 1)], 0
        )

    def big_bias(b):
        b = lax.dynamic_index_in_dim(b.reshape(2, BLOCKS, block), mine, 1, keepdims=False)
        return jnp.pad(b, ((0, 0), (0, LANES - block))).reshape(1, 2 * LANES)

    wa, wb = big_weight(mix_weight_a), big_weight(mix_weight_b)
    ba, bb = big_bias(mix_bias_a), big_bias(mix_bias_b)

    normed, send = call(
        first_kernel, [x5, mask, row(first_gain), row(first_shift)],
        [shape(pad_shape, BF), shape(packed_shape, BF)], 6.0,
        grid=(lat_steps,), in_specs=[here_spec, mask_spec, row_spec, row_spec],
        out_specs=[pad_spec, packed_spec], vmem=16, name="first_norm",
    )
    cells = exchange(send.reshape(flat_shape))

    own, other = lon_forward(cells, lon_fwd)
    other = swap(other)
    own, other, modes = call(
        mix_kernel, [own, other, lat_fwd, lat_inv, wa, ba, wb, bb],
        [shape((lats, half_rows, LANES), BF)] * 2
        + [shape((slots_pad // 2, 2 * LAT, 2 * LANES), BF)], 22.0,
        scratch_shapes=[pltpu.VMEM((2 * lats * half_rows, LANES), F32)], vmem=32, name="mix",
    )
    other = swap(other)
    got = exchange(lon_backward([own, other], lon_winv))

    resid, tokens, cot_pad = call(
        second_kernel,
        [x5, normed, mask, cot5, got.reshape(packed_shape), row(second_gain), row(second_shift)],
        [shape(pad_shape, F32), shape(pad_shape, BF), shape(pad_shape, BF)], 8.5,
        grid=(lat_steps,),
        in_specs=[here_spec, pad_spec, mask_spec, here_spec, packed_spec, row_spec, row_spec],
        out_specs=[pad_spec, pad_spec, pad_spec], vmem=56, name="second_norm",
    )
    tokens2, cot2 = tokens.reshape(-1, channels), cot_pad.reshape(-1, channels)
    count, hidden = tokens2.shape[0], expand_weight.shape[1]
    tile = hidden // 6
    all_tok = pl.BlockSpec((count, channels), lambda i: (0, 0))
    by_col = lambda n: pl.BlockSpec((n, tile), lambda i: (0, i))
    by_row = pl.BlockSpec((tile, channels), lambda i: (i, 0))
    act, gpre, gtok, g_ebias = call(
        chain_kernel,
        [tokens2, cot2, expand_weight, row(expand_bias), reduce_weight],
        [
            shape((count, hidden), BF), shape((count, hidden), BF),
            shape((count, channels), F32), shape((1, hidden), F32),
        ],
        25.0, grid=(6,),
        in_specs=[all_tok, all_tok, by_col(channels), by_col(1), by_row],
        out_specs=[by_col(count), by_col(count), all_tok, by_col(1)], vmem=46, name="mlp_chain",
    )

    halves = 3
    assert halves * CORES * tile == hidden

    def weight_grad(left, right, own, after, name):
        at = lambda i, c: (c[0] if own else 1 - c[0]) * halves + i
        return call(
            weight_grad_kernel, [left, right], shape((halves * tile, channels), BF), 5.0,
            after=after, prefetch=[core_line], grid=(halves,),
            in_specs=[
                pl.BlockSpec((count, tile), lambda i, c: (0, at(i, c))),
                pl.BlockSpec((count, channels), lambda i, c: (0, 0)),
            ],
            out_specs=[pl.BlockSpec((tile, channels), lambda i, c: (i, 0))], vmem=20, name=name,
        )

    one_row = shape((1, channels), F32)
    grad_resid, send, g_gain2, g_shift2, g_rbias = call(
        third_kernel,
        [resid, gtok.reshape(pad_shape), cot_pad, mask, row(second_gain)],
        [shape(pad_shape, F32), shape(packed_shape, BF)] + [one_row] * 3, 9.0,
        grid=(lat_steps,), in_specs=[pad_spec, pad_spec, pad_spec, mask_spec, row_spec],
        out_specs=[pad_spec, packed_spec, row_spec, row_spec, row_spec], vmem=56, name="second_back",
    )
    cells = exchange(send.reshape(flat_shape))

    sent_r = weight_grad(act, cot2, False, [send], "reduce_grad")
    sent_e = weight_grad(gpre, tokens2, False, [sent_r], "expand_grad")
    kept_r = weight_grad(act, cot2, True, [sent_e], "reduce_grad")
    kept_e = weight_grad(gpre, tokens2, True, [kept_r], "expand_grad")
    sums = Sum([kept_r, kept_e], [partner(sent_r, 1), partner(sent_e, 1)])

    own, other = lon_forward(cells, lon_wfwd, after=[kept_e])
    other = swap(other)
    token = sums.halve(after=[own])
    run = half_rows // SPLIT
    pieces, grads = [], []
    grad_shape = shape((4 * LANES + 16, 2 * LANES), F32)
    for k in range(SPLIT):
        here = pl.BlockSpec((run, lats, LANES), lambda i, k=k: (k, 0, 0))
        steps = modes.shape[0] // SPLIT
        const = lambda x: pl.BlockSpec(x.shape, lambda i: (0, 0))
        o, t, g = call(
            mix_back_kernel, [own, other, modes, lat_fwd, lat_inv, wa, ba, wb, bb] + grads,
            [shape((lats, run, LANES), BF)] * 2 + [grad_shape], 13.0,
            after=[token],
            in_specs=[
                here, here, pl.BlockSpec((steps,) + modes.shape[1:], lambda i, k=k: (k, 0, 0)),
            ] + [const(x) for x in (lat_fwd, lat_inv, wa, ba, wb, bb, *grads)],
            scratch_shapes=[pltpu.VMEM((2 * lats * run, LANES), F32)], name="mix_back",
        )
        pieces.append((o, swap(t)))
        grads = [g]
        token = sums.halve(after=[o])
    token = sums.settle(after=[token])
    send = lon_backward(
        [p[0] for p in pieces] + [p[1] for p in pieces], lon_inv, after=[token]
    )
    got = exchange(send)
    stay, leave = call(
        lambda *refs: collect_kernel(block, *refs), grads,
        [shape((3 * EXTRA, channels), F32)] * 2, 1.5, after=[send], prefetch=[core_line],
        name="collect",
    )
    token = sums.join(stay, partner(leave, 1))

    touched = call(
        touch_kernel, [], shape((8, LANES), F32), 0.5, after=[got, token], name="touch"
    )
    token = sums.part(after=[touched])
    token = sums.double(after=[token])

    grad_inputs, g_gain1, g_shift1 = call(
        last_kernel, [x5, grad_resid, mask, got.reshape(packed_shape), row(first_gain)],
        [turned_shape] + [one_row] * 2, 9.0, after=[token],
        grid=(lat_steps,), in_specs=[here_spec, pad_spec, mask_spec, packed_spec, row_spec],
        out_specs=[turned_spec, row_spec, row_spec], vmem=56, name="first_back",
    )
    tail_sum = Tail(
        call(
            tail_kernel, [g_gain1, g_shift1, g_gain2, g_shift2, g_rbias, g_ebias],
            [shape((1, 5 * channels + hidden), F32)] * 2, 1.0, name="tail",
        )
    )
    token = sums.double(after=[tail_sum.x])
    token = tail_sum.step(after=[token])
    outputs = call(
        branch_kernel,
        [act.reshape(CORES, groups, PACK, cols_pad, hidden), reduce_weight, resid, row(reduce_bias)],
        turned_shape, 10.0, after=[token], grid=(groups,),
        in_specs=[
            both_spec(cols_pad, hidden), pl.BlockSpec((hidden, channels), lambda i: (0, 0)),
            both_spec(cols_pad, channels), row_spec,
        ],
        out_specs=[turned_spec], vmem=32, name="branch",
    )

    token = tail_sum.step(after=[outputs])
    token = sums.double(after=[token])
    token = tail_sum.step(after=[token])
    own_done = sums.widen([], after=[token])
    token = tail_sum.step(after=[own_done[0]])
    g_reduce, g_expand, *got_extra = sums.widen(own_done, after=[token])
    token = got_extra[0]
    while tail_sum.bits:
        token = tail_sum.step(after=[token])
    weight_out, bias_out = shape(mix_weight_a.shape, F32), shape(mix_bias_a.shape, F32)
    g_wa, g_wb, g_ba, g_bb = call(
        lambda *refs: spread_kernel(block, *refs), own_done[2:] + got_extra,
        [weight_out, weight_out, bias_out, bias_out], 3.0, prefetch=[core_line], name="spread",
    )

    tail = tail_sum.x
    g_gain1, g_shift1, g_gain2, g_shift2, g_rbias = (
        tail[0, k * channels : (k + 1) * channels] for k in range(5)
    )
    g_ebias = tail[0, 5 * channels :]

    def flat(v):
        return v.reshape(-1)

    return (
        turn_back(outputs), turn_back(grad_inputs),
        flat(g_gain1), flat(g_shift1), g_wa, g_ba, g_wb, g_bb, flat(g_gain2), flat(g_shift2),
        g_expand, g_ebias, g_reduce, flat(g_rbias),
    )


def solution(mesh):
    grid = P("rows", "cols", None)
    placed = (grid, P("rows", "cols"), grid) + (P(),) * 12
    return jax.shard_map(
        per_device,
        mesh=mesh,
        in_specs=placed,
        out_specs=(grid, grid) + (P(),) * 12,
        check_vma=False,
    )
```

```python
import math

import jax
import jax.numpy as jnp
import numpy as np
from jax import lax
from jax.experimental import pallas as pl
from jax.experimental.pallas import tpu as pltpu
from jax.sharding import PartitionSpec as P

BLOCKS = 8
LAT = 96
CORES = 2
PACK = 4
LANES = 128

shrink_level = 0.01
shrink_soft = 0.1
norm_eps = 1e-05
gelu_root = math.sqrt(2.0 / math.pi)
gelu_cube = 0.044715

BF = jnp.bfloat16
F32 = jnp.float32
AXES = ("rows", "cols")


def up_to(value, step):
    return (value + step - 1) // step * step


def call(kernel, args, out_shape, us, after=(), in_specs=None, prefetch=(), vmem=12, hbm=(), pin=False, **kw):
    outs = out_shape if isinstance(out_shape, (list, tuple)) else [out_shape]
    lead, n_in, n_after = len(prefetch), len(args), len(after)

    def body(*refs):
        kernel(*refs[: lead + n_in], *refs[lead + n_in + n_after :])

    if pin:
        args = [pltpu.with_memory_space_constraint(x, pltpu.HBM) for x in args]
    grid = kw.pop("grid", (1,))
    whole = lambda x: pl.BlockSpec(x.shape, lambda *_, n=len(x.shape): (0,) * n)
    specs = list(in_specs) if in_specs is not None else [whole(a) for a in args]
    specs += [pl.BlockSpec(memory_space=pl.ANY)] * n_after
    out_specs = kw.pop("out_specs", None) or [whole(o) for o in outs]
    got = pl.pallas_call(
        body,
        grid_spec=pltpu.PrefetchScalarGridSpec(
            num_scalar_prefetch=lead,
            grid=grid,
            in_specs=specs,
            out_specs=out_specs,
            scratch_shapes=kw.pop("scratch_shapes", ()),
        ),
        out_shape=[pltpu.HBM(o.shape, o.dtype) if k in hbm else o for k, o in enumerate(outs)],
        compiler_params=pltpu.CompilerParams(vmem_limit_bytes=vmem * 1024 * 1024),
        cost_estimate=pl.CostEstimate(
            flops=0, bytes_accessed=int(us * 1e5), transcendentals=0
        ),
        **kw,
    )(*prefetch, *args, *after)
    return list(got) if isinstance(out_shape, (list, tuple)) else got[0]


SPLIT = 2
UNROLL = 1
WIDE = 12


def lon_table(lon_size, col_devs, cols_here, cols_pad, slots, slots_pad):
    modes = lon_size // 2 + 1
    table = np.zeros((CORES, 2, slots_pad, col_devs, cols_pad), np.float64)
    weights = np.zeros((CORES, slots_pad), np.float64)
    place = np.arange(lon_size).reshape(col_devs, cols_here)
    for half in range(CORES):
        for slot in range(slots):
            mode = half * slots + slot
            if mode >= modes:
                continue
            angle = (place * mode % lon_size) * (2.0 * math.pi / lon_size)
            table[half, 0, slot, :, :cols_here] = np.cos(angle) / math.sqrt(lon_size)
            edge = mode == 0 or 2 * mode == lon_size
            if not edge:
                table[half, 1, slot, :, :cols_here] = np.sin(angle) / math.sqrt(lon_size)
            weights[half, slot] = 1.0 if edge else 2.0
    weighted = table * weights[:, None, :, None, None]
    rows = 2 * slots_pad
    flat = [
        a.reshape(CORES, 2, SPLIT, slots_pad // SPLIT, col_devs, cols_pad)
        .swapaxes(1, 2)
        .reshape(CORES, rows, col_devs * cols_pad)
        for a in (table, weighted)
    ]
    return [
        np.stack([np.concatenate([a[h], a[1 - h]], 0) for h in range(CORES)]) for a in flat
    ]


def lat_table(rows_here, row_group):
    share = rows_here // CORES
    out = []
    for h in range(CORES):
        own = [
            rows_here * r + share * h + i for r in range(row_group) for i in range(share)
        ]
        other = [
            rows_here * r + share * (1 - h) + i for r in range(row_group) for i in range(share)
        ]
        angle = np.outer(np.arange(LAT), np.array(own + other)) % LAT * (2.0 * math.pi / LAT)
        cos, sin = np.cos(angle) / math.sqrt(LAT), np.sin(angle) / math.sqrt(LAT)
        out.append(np.block([[cos, -sin], [-sin, -cos]]))
    return np.stack(out)


def pack_lanes(tiles):
    a, b, c, d = tiles
    lane = lax.broadcasted_iota(jnp.int32, a.shape, a.ndim - 1)
    axis = a.ndim - 1
    b, c, d = pltpu.roll(b, 96, axis), pltpu.roll(c, 64, axis), pltpu.roll(d, 32, axis)
    return [
        jnp.where(lane < 96, a, b),
        jnp.where(lane < 64, b, c),
        jnp.where(lane < 32, c, d),
    ]


def unpack_lanes(tiles):
    a, b, c = tiles
    lane = lax.broadcasted_iota(jnp.int32, a.shape, a.ndim - 1)
    axis = a.ndim - 1
    return [
        a,
        pltpu.roll(jnp.where(lane >= 96, a, b), 32, axis),
        pltpu.roll(jnp.where(lane >= 64, b, c), 64, axis),
        pltpu.roll(c, 96, axis),
    ]


def tiles_of(value):
    return [value[:, LANES * i : LANES * (i + 1)] for i in range(value.shape[1] // LANES)]


def split_blocks(value):
    tiles = tiles_of(value)
    out = []
    for i in range(0, len(tiles), 3):
        out += unpack_lanes(tiles[i : i + 3])
    return out


def join_blocks(tiles):
    out = []
    for i in range(0, len(tiles), 4):
        out += pack_lanes(tiles[i : i + 4])
    return jnp.concatenate(out, axis=1)


def pad_rows(value, rows):
    return jnp.concatenate(
        [value, jnp.zeros((rows - value.shape[0], value.shape[1]), value.dtype)], axis=0
    )


def store_packed(ref, half, per_lat):
    split = [split_blocks(v) for v in per_lat]
    for q in range(BLOCKS):
        packed = pack_lanes([split[j][q] for j in range(PACK)])
        ref[q, half, 0] = jnp.concatenate(packed, axis=1).astype(ref.dtype)


def load_packed(ref, half):
    by_lat = [[] for _ in range(PACK)]
    for q in range(BLOCKS):
        parts = unpack_lanes(tiles_of(ref[q, half, 0].astype(F32)))
        for j in range(PACK):
            by_lat[j].append(parts[j])
    return [join_blocks(tiles) for tiles in by_lat]


def stats(x):
    average = jnp.mean(x, axis=-1, keepdims=True)
    centred = x - average
    spread = jnp.mean(centred * centred, axis=-1, keepdims=True)
    inv = lax.rsqrt(spread + norm_eps)
    return centred * inv, inv


def norm_back(grad, xhat, inv, gain):
    scaled = grad * gain
    m1 = jnp.mean(scaled, axis=-1, keepdims=True)
    m2 = jnp.mean(scaled * xhat, axis=-1, keepdims=True)
    return inv * (scaled - m1 - xhat * m2)


def mask_column(mask_ref, lat, rows):
    line = mask_ref[pl.ds(lat, 1), :].astype(F32)
    shape = (rows, line.shape[1])
    row, col = (lax.broadcasted_iota(jnp.int32, shape, k) for k in range(2))
    return jnp.sum(jnp.where(row == col, line, 0.0), axis=1, keepdims=True)


def first_kernel(x_ref, mask_ref, gain_ref, shift_ref, normed_ref, out_ref):
    rows = normed_ref.shape[3]
    half, first = 0, pl.program_id(0) * PACK
    lats = []
    for j in range(PACK):
        x = pad_rows(x_ref[half, 0, j].astype(F32), rows)
        xhat, _ = stats(x)
        y = mask_column(mask_ref, first + j, rows) * (xhat * gain_ref[...][None] + shift_ref[...][None])
        normed_ref[half, 0, j] = y.astype(BF)
        lats.append(y)
    store_packed(out_ref, half, lats)


def pad_kernel(x_ref, out_ref):
    rows = out_ref.shape[3]
    for j in range(PACK):
        out_ref[0, 0, j] = pad_rows(x_ref[0, 0, j].astype(F32), rows).astype(BF)


def second_kernel(
    x_ref, normed_ref, mask_ref, got_ref, gain_ref, shift_ref, resid_ref, tok_ref
):
    rows = normed_ref.shape[3]
    half, first = 0, pl.program_id(0) * PACK
    spatial = load_packed(got_ref, half)
    for j in range(PACK):
        x = pad_rows(x_ref[half, 0, j].astype(F32), rows)
        resid = x + normed_ref[half, 0, j].astype(F32)
        resid = resid + mask_column(mask_ref, first + j, rows) * spatial[j]
        resid_ref[half, 0, j] = resid
        xhat, _ = stats(resid)
        tok_ref[half, 0, j] = (xhat * gain_ref[...] + shift_ref[...]).astype(BF)


def third_kernel(
    resid_ref, gtok_ref, cot_ref, mask_ref, gain_ref,
    gresid_ref, send_ref, ggain_ref, gshift_ref, gbias_ref,
):
    @pl.when(pl.program_id(0) == 0)
    def _():
        ggain_ref[...] = jnp.zeros_like(ggain_ref)
        gshift_ref[...] = jnp.zeros_like(gshift_ref)
        gbias_ref[...] = jnp.zeros_like(gbias_ref)

    half, first = 0, pl.program_id(0) * PACK
    lats = []
    for j in range(PACK):
        xhat, inv = stats(resid_ref[half, 0, j])
        gtok = gtok_ref[half, 0, j].astype(F32)
        cot = cot_ref[half, 0, j].astype(F32)
        ggain_ref[...] += jnp.sum(gtok * xhat, axis=0, keepdims=True)
        gshift_ref[...] += jnp.sum(gtok, axis=0, keepdims=True)
        gbias_ref[...] += jnp.sum(cot, axis=0, keepdims=True)
        gres = cot + norm_back(gtok, xhat, inv, gain_ref[...])
        gresid_ref[half, 0, j] = gres.astype(gresid_ref.dtype)
        lats.append(mask_column(mask_ref, first + j, gres.shape[0]) * gres)
    store_packed(send_ref, half, lats)


def store_lat(out_ref, lat, value):
    out_ref[:, lat, :] = value[: out_ref.shape[0]]


def last_kernel(
    x_ref, gresid_ref, mask_ref, got_ref, gain_ref, out_ref, ggain_ref, gshift_ref
):
    @pl.when(pl.program_id(0) == 0)
    def _():
        ggain_ref[...] = jnp.zeros_like(ggain_ref)
        gshift_ref[...] = jnp.zeros_like(gshift_ref)

    rows = gresid_ref.shape[3]
    half, first = 0, pl.program_id(0) * PACK
    got = load_packed(got_ref, half)
    for j in range(PACK):
        x = pad_rows(x_ref[half, 0, j].astype(F32), rows)
        xhat, inv = stats(x)
        gres = gresid_ref[half, 0, j].astype(F32)
        grad = mask_column(mask_ref, first + j, rows) * (gres + got[j])
        ggain_ref[...] += jnp.sum(grad * xhat, axis=0, keepdims=True)
        gshift_ref[...] += jnp.sum(grad, axis=0, keepdims=True)
        store_lat(out_ref, first + j, gres + norm_back(grad, xhat, inv, gain_ref[...]))


OUTER = (((0,), (0,)), ((), ()))
ACROSS = (((1,), (1,)), ((), ()))


def chain_kernel(
    tok_ref, cot_ref, up_ref, bias_ref, down_ref, act_ref, gpre_ref, gtok_ref, gbias_ref, sum_ref
):
    @pl.when(pl.program_id(0) == 0)
    def _():
        sum_ref[...] = jnp.zeros_like(sum_ref)

    pre = jnp.dot(tok_ref[...], up_ref[...], preferred_element_type=F32) + bias_ref[...]
    gate = gelu_gate(pre)
    act_ref[...] = (pre * gate).astype(BF)
    gact = lax.dot_general(cot_ref[...], down_ref[...], ACROSS, preferred_element_type=F32)
    gpre = gelu_slope(pre, gate) * gact
    gbias_ref[...] = jnp.sum(gpre, axis=0, keepdims=True)
    gpre = gpre.astype(BF)
    gpre_ref[...] = gpre
    sum_ref[...] += lax.dot_general(gpre, up_ref[...], ACROSS, preferred_element_type=F32)

    @pl.when(pl.program_id(0) == pl.num_programs(0) - 1)
    def _():
        gtok_ref[...] = sum_ref[...].astype(gtok_ref.dtype)


def weight_grad_kernel(core_ref, left_ref, right_ref, out_ref, token_ref):
    token_ref[...] = jnp.zeros_like(token_ref)
    out_ref[...] = lax.dot_general(
        left_ref[...], right_ref[...], OUTER, preferred_element_type=F32
    ).astype(BF)


def branch_kernel(act_ref, down_ref, resid_ref, bias_ref, out_ref, token_ref):
    token_ref[...] = jnp.zeros_like(token_ref)
    cols = resid_ref.shape[3]
    rows = CORES * PACK * cols
    act = act_ref[...].reshape(rows, act_ref.shape[-1])
    branch = jnp.dot(act, down_ref[...], preferred_element_type=F32) + bias_ref[...]
    for half in range(CORES):
        for j in range(PACK):
            at = (half * PACK + j) * cols
            lat = (half * pl.num_programs(0) + pl.program_id(0)) * PACK + j
            store_lat(out_ref, lat, resid_ref[half, 0, j] + branch[at : at + cols])


def plus(left, right):
    return (left.astype(F32) + right.astype(F32)).astype(BF)


def halve_first_kernel(bits_ref, *refs):
    count = len(refs) // 6
    for p in range(count):
        a, b, c, d = refs[4 * p : 4 * p + 4]
        low, high = plus(a[...], b[...]), plus(c[...], d[...])
        first = bits_ref[p] == 0
        refs[4 * count + 2 * p][...] = jnp.where(first, low, high)
        refs[4 * count + 2 * p + 1][...] = jnp.where(first, high, low)


def halve_kernel(bits_ref, *refs):
    count = len(refs) // 6
    for k in range(2 * count):
        refs[4 * count + k][...] = plus(refs[2 * k][...], refs[2 * k + 1][...])


def join_kernel(count, *refs):
    stay, got = refs[count : count + 2]
    for p in range(count):
        n, m = refs[p].shape[0], stay.shape[0] // count
        value = refs[p][...]
        rows = slice(p * m, (p + 1) * m)
        extra = (stay[rows] + got[rows]).astype(BF)
        for out in refs[-2:]:
            out[p * (n + m) : p * (n + m) + n] = value
            out[p * (n + m) + n : (p + 1) * (n + m)] = extra


def settle_kernel(count, *refs):
    for p in range(count):
        refs[2 * count + p][...] = plus(refs[2 * p][...], refs[2 * p + 1][...])


def touch_kernel(out):
    out[...] = jnp.zeros_like(out)


def part_kernel(kept, got, *outs):
    n, count = outs[0].shape[0], len(outs) // 2
    for p in range(count):
        rows = slice(p * n, (p + 1) * n)
        value = plus(kept[rows], got[rows])
        outs[p][...] = value
        outs[count + p][...] = value


def add_kernel(left, right, *outs):
    value = left[...].astype(F32) + right[...].astype(F32)
    for out in outs:
        out[...] = value.astype(out.dtype)


def tail_kernel(*refs):
    for out in refs[-2:]:
        at = 0
        for ref in refs[:-2]:
            out[:, at : at + ref.shape[1]] = ref[...]
            at += ref.shape[1]


def merge_kernel(count, single, bits_ref, *refs):
    outs = refs[2 * count :]
    for p in range(count):
        own, got = refs[2 * p], refs[2 * p + 1]
        n = own.shape[0]
        for out in (outs[p::count] if not single else [o.at[p] for o in outs]):
            out[pl.ds(pl.multiple_of(bits_ref[p] * n, 16), n), :] = own[...]
            out[pl.ds(pl.multiple_of((1 - bits_ref[p]) * n, 16), n), :] = got[...]


def widen_kernel(core_ref, reduce_ref, expand_ref, *refs):
    reduce_out, expand_out, extra_r, extra_e = refs[-4:]
    n = reduce_out.shape[0] // 2
    for k in range(2):
        at = k * (n + EXTRA)
        reduce_out[k * n : (k + 1) * n] = reduce_ref[at : at + n].astype(F32)
        expand_out[:, k * n : (k + 1) * n] = expand_ref[at : at + n].astype(F32).T
        extra_r[k] = reduce_ref[at + n : at + n + EXTRA]
        extra_e[k] = expand_ref[at + n : at + n + EXTRA]


EXTRA = 16


def collect_kernel(block, core_ref, grad_ref, *refs):
    wide = 2 * LANES
    halves, lines = [], []
    for i in range(2):
        g = grad_ref[i * wide : (i + 1) * wide]
        at = 2 * wide + 8 * i
        line = jnp.sum(grad_ref[at : at + 8], axis=0, keepdims=True)
        top, low = g[:block], g[LANES : LANES + block]
        halves.append([top[:, :LANES] + low[:, LANES:], top[:, LANES:] - low[:, :LANES]])
        lines += [line[:, :LANES], line[:, LANES:]]
    rows = lax.broadcasted_iota(jnp.int32, (EXTRA, LANES), 0)
    bias = sum(jnp.where(rows == k, line, 0.0) for k, line in enumerate(lines))
    first = core_ref[0] == 0
    for k, out in enumerate(refs[-2:]):
        own = first if k == 0 else jnp.logical_not(first)
        out[...] = jnp.zeros_like(out)
        for p in range(2):
            value = jnp.where(own, halves[0][p], halves[1][p])
            for t in range(block // EXTRA):
                at = slice(t * LANES, (t + 1) * LANES)
                out[p * EXTRA : (p + 1) * EXTRA, at] = value[t * EXTRA : (t + 1) * EXTRA]
        out[2 * EXTRA : 3 * EXTRA, :LANES] = jnp.where(own, bias, 0.0)


def spread_kernel(block, core_ref, *refs):
    own, got = refs[:2], refs[2:4]
    wa_ref, wb_ref, ba_ref, bb_ref = refs[4:]
    first = core_ref[0] == 0
    per = own[0].shape[0]
    biases = [[] for _ in range(4)]
    for q in range(BLOCKS):
        for half in range(CORES):
            for p in range(3):
                if half == 1 and p == 2:
                    continue
                k = sum(((q >> ((p + j) % 3)) & 1) << (2 - j) for j in range(3))
                at = p * BLOCKS + k
                mine, other = (r[at // per][at % per].astype(F32) for r in (own, got))
                value = jnp.where(first, mine, other) if half == 0 else jnp.where(first, other, mine)
                if p == 2:
                    for i in range(4):
                        biases[i].append(value[i : i + 1, :LANES])
                    continue
                out = wb_ref if half else wa_ref
                for t in range(block // EXTRA):
                    out[p, q, t * EXTRA : (t + 1) * EXTRA, :] = value[
                        :, t * LANES : t * LANES + block
                    ]
    for i in range(4):
        (bb_ref if i > 1 else ba_ref)[i % 2 : i % 2 + 1, :] = join_blocks(biases[i])


def lon_kernel(col_devs, row_group, x_ref, table_ref, own_ref, other_ref, turn_ref):
    groups = x_ref.shape[1]
    rows = table_ref.shape[0]
    lats = own_ref.shape[1]
    slots = own_ref.shape[0]
    for r in range(row_group):
        for g in range(groups):
            cells = jnp.concatenate(
                [x_ref[r * col_devs + c, g] for c in range(col_devs)], axis=0
            )
            modes = jnp.dot(table_ref[...], cells, preferred_element_type=F32)
            for j, tile in enumerate(unpack_lanes(tiles_of(modes))):
                at = (r * groups + g) * PACK + j
                turn_ref[pl.ds(at, rows, stride=lats), :] = tile

    @pl.loop(0, slots, unroll=4)
    def _(s):
        own_ref[s] = turn_ref[pl.ds(pl.multiple_of(s * lats, 8), lats), :].astype(BF)
        other_ref[s] = turn_ref[
            pl.ds(pl.multiple_of((s + slots) * lats, 8), lats), :
        ].astype(BF)


def lon_back_kernel(col_devs, row_group, pieces, table_ref, *refs):
    out_ref = refs[pieces]
    groups = out_ref.shape[1]
    cols = out_ref.shape[2]
    for r in range(row_group):
        for g in range(groups):
            tiles = []
            for j in range(0, PACK, 2):
                pair = []
                for k in range(2):
                    at = (r * groups + g) * PACK + j + k
                    pair.append(jnp.concatenate([r_[at] for r_ in refs[:pieces]], axis=0))
                cells = jnp.dot(
                    table_ref[...], jnp.concatenate(pair, axis=1), preferred_element_type=F32
                )
                tiles += tiles_of(cells)
            packed = jnp.concatenate(pack_lanes(tiles), axis=1).astype(BF)
            for c in range(col_devs):
                out_ref[r * col_devs + c, g] = packed[c * cols : (c + 1) * cols]


def gelu_gate(v):
    inner = v * (gelu_root * gelu_cube * (v * v) + gelu_root)
    return 0.5 * jnp.tanh(inner) + 0.5


def gelu_slope(v, gate):
    inner = 6.0 * gelu_root * gelu_cube * (v * v) + 2.0 * gelu_root
    return gate + (v * gate) * (1.0 - gate) * inner


def slots_down(real, imag):
    return [
        jnp.concatenate([v[:, k * LANES : (k + 1) * LANES] for v in (real, imag)], axis=1)
        for k in range(WIDE)
    ]


def slots_across(value):
    rows = [value[k * LAT : (k + 1) * LAT] for k in range(WIDE)]
    parts = [
        jnp.concatenate([r[:, p * LANES : (p + 1) * LANES] for r in rows], axis=1)
        for p in range(2)
    ]
    return jnp.concatenate(parts, axis=0)


def latitudes(own_ref, other_ref, row, run):
    return jnp.concatenate(
        [own_ref[row], other_ref[row], own_ref[row + run], other_ref[row + run]], axis=0
    )


def turn_out(turn_ref, value, row, lats, rows, run):
    for part in range(2):
        for dest in range(2):
            piece = value[(2 * part + dest) * lats : (2 * part + dest + 1) * lats]
            start = dest * lats * rows + part * run + row
            turn_ref[pl.ds(start, lats, stride=rows), :] = piece


def drain(turn_ref, own_ref, other_ref):
    lats, rows = own_ref.shape[0], own_ref.shape[1]

    @pl.loop(0, lats, unroll=4)
    def _(at):
        own_ref[at] = turn_ref[pl.ds(pl.multiple_of(at * rows, 8), rows), :].astype(BF)
        other_ref[at] = turn_ref[
            pl.ds(pl.multiple_of((at + lats) * rows, 8), rows), :
        ].astype(BF)


def mix_kernel(
    own_ref, other_ref, lat_ref, back_ref, wa_ref, ba_ref, wb_ref, bb_ref,
    own_out, other_out, modes_out, turn_ref,
):
    lats, rows = own_ref.shape[1], own_ref.shape[0]
    run = rows // 2 // SPLIT

    @pl.loop(0, rows // 2 // WIDE, unroll=UNROLL)
    def _(step):
        slot = WIDE * step
        row = slot + slot // run * run
        cells = jnp.concatenate(
            [latitudes(own_ref, other_ref, row + k, run) for k in range(WIDE)], axis=1
        )
        full = jnp.dot(lat_ref[...], cells, preferred_element_type=F32).astype(BF)
        real, imag = full[:LAT], full[LAT:]
        modes = jnp.concatenate(slots_down(real, imag), axis=0)
        modes_out[step] = modes
        pre_a = jnp.dot(modes, wa_ref[...], preferred_element_type=F32) + ba_ref[...]
        hidden = (pre_a * gelu_gate(pre_a)).astype(BF)
        pre_b = jnp.dot(hidden, wb_ref[...], preferred_element_type=F32) + bb_ref[...]
        shrunk = (pre_b - shrink_level * jnp.tanh(pre_b * (1.0 / shrink_soft))).astype(BF)
        mixed = slots_across(shrunk)
        back = jnp.dot(back_ref[...], mixed, preferred_element_type=F32)
        for k in range(WIDE):
            turn_out(turn_ref, back[:, k * LANES : (k + 1) * LANES], row + k, lats, rows, run)

    drain(turn_ref, own_out, other_out)


def row_sums(value):
    return jnp.sum(value.reshape(-1, 8, value.shape[1]), axis=0)


def mix_back_kernel(
    own_ref, other_ref, modes_ref, lat_ref, back_ref, wa_ref, ba_ref, wb_ref, bb_ref,
    *refs,
):
    own_out, other_out, grad_ref, turn_ref = refs[-4:]
    lats, rows = own_ref.shape[1], own_ref.shape[0]
    run = rows // 2
    grad_ref[...] = refs[0][...] if len(refs) > 4 else jnp.zeros_like(grad_ref)
    wide = wa_ref.shape[0]
    gwa_ref, gwb_ref = grad_ref.at[:wide], grad_ref.at[wide : 2 * wide]
    gba_ref, gbb_ref = grad_ref.at[2 * wide : 2 * wide + 8], grad_ref.at[2 * wide + 8 :]

    @pl.loop(0, run // WIDE, unroll=UNROLL)
    def _(step):
        row = WIDE * step
        cells = jnp.concatenate(
            [latitudes(own_ref, other_ref, row + k, run) for k in range(WIDE)], axis=1
        )
        full = jnp.dot(lat_ref[...], cells, preferred_element_type=F32)
        real, imag = full[:LAT], full[LAT:]
        grad = jnp.concatenate(slots_down(real, imag), axis=0)
        modes = modes_ref[step]
        pre_a = jnp.dot(modes, wa_ref[...], preferred_element_type=F32) + ba_ref[...]
        gate_a = gelu_gate(pre_a)
        hidden = (pre_a * gate_a).astype(BF)
        pre_b = jnp.dot(hidden, wb_ref[...], preferred_element_type=F32) + bb_ref[...]
        squash_b = jnp.tanh(pre_b * (1.0 / shrink_soft))
        level = shrink_level / shrink_soft
        factor = level * (squash_b * squash_b) + (1.0 - level)
        grad_b = factor * grad
        gbb_ref[...] += row_sums(grad_b)
        grad_b = grad_b.astype(BF)
        grad_hidden = lax.dot_general(grad_b, wb_ref[...], ACROSS, preferred_element_type=F32)
        gwb_ref[...] += lax.dot_general(hidden, grad_b, OUTER, preferred_element_type=F32)
        grad_a = gelu_slope(pre_a, gate_a) * grad_hidden
        gba_ref[...] += row_sums(grad_a)
        grad_a = grad_a.astype(BF)
        grad_modes = lax.dot_general(
            grad_a, wa_ref[...], ACROSS, preferred_element_type=F32
        ).astype(BF)
        gwa_ref[...] += lax.dot_general(modes, grad_a, OUTER, preferred_element_type=F32)
        mixed = slots_across(grad_modes)
        back = jnp.dot(back_ref[...], mixed, preferred_element_type=F32)
        for k in range(WIDE):
            turn_out(turn_ref, back[:, k * LANES : (k + 1) * LANES], row + k, lats, rows, run)

    drain(turn_ref, own_out, other_out)


def per_device(
    inputs, valid_mask, cotangent, first_gain, first_shift, mix_weight_a, mix_bias_a,
    mix_weight_b, mix_bias_b, second_gain, second_shift, expand_weight, expand_bias,
    reduce_weight, reduce_bias,
):
    row_devs = lax.axis_size("rows")
    col_devs = lax.axis_size("cols")
    rows_here, cols_here, channels = inputs.shape
    block = channels // BLOCKS
    lon_size = cols_here * col_devs
    cols_pad = up_to(cols_here, 16)
    row_group = LAT // rows_here
    members = row_group * col_devs
    share = rows_here // CORES
    groups = share // PACK
    slots = (lon_size // 2 + 2) // 2
    slots_pad = up_to(slots, 16)
    lats = share * row_group
    half_rows = 2 * slots_pad
    all_rows = CORES * half_rows
    assert members == CORES * BLOCKS and block * PACK == 3 * LANES
    assert col_devs * cols_pad == all_rows and CORES * lats == LAT

    row_at, col_at = lax.axis_index("rows"), lax.axis_index("cols")
    core = col_at % CORES
    mine = (row_at % row_group) * (col_devs // CORES) + col_at // CORES

    def pick(table):
        return lax.dynamic_index_in_dim(jnp.asarray(table, BF), core, 0, keepdims=False)

    plain_np, weighted_np = lon_table(
        lon_size, col_devs, cols_here, cols_pad, slots, slots_pad
    )
    lat_np = lat_table(rows_here, row_group)
    lon_fwd, lon_wfwd = pick(plain_np), pick(weighted_np)
    lon_inv, lon_winv = (
        pick(np.swapaxes(plain_np, 1, 2)), pick(np.swapaxes(weighted_np, 1, 2))
    )
    lat_fwd, lat_inv = pick(lat_np), pick(np.swapaxes(lat_np, 1, 2))

    snap_groups = [
        [(s * row_group + r) * col_devs + c for r in range(row_group) for c in range(col_devs)]
        for s in range(row_devs // row_group)
    ]
    core_pairs = [
        (r * col_devs + c, r * col_devs + c ^ 1) for r in range(row_devs) for c in range(col_devs)
    ]

    def exchange(x):
        return lax.all_to_all(x, AXES, 0, 0, axis_index_groups=snap_groups, tiled=True)

    def swap(x):
        return lax.ppermute(x, AXES, core_pairs)

    def fold(x):
        return x.reshape((CORES, groups, PACK) + x.shape[1:])

    def row(v):
        return v.reshape(1, -1)

    x5, cot5 = fold(inputs), fold(cotangent)

    def lat_spec(cols, width):
        return pl.BlockSpec(
            (1, 1, PACK, cols, width), lambda i: (i // groups, i % groups, 0, 0, 0)
        )

    def both_spec(cols, width):
        return pl.BlockSpec((CORES, 1, PACK, cols, width), lambda i: (0, i, 0, 0, 0))

    packed_spec = pl.BlockSpec(
        (BLOCKS, 1, 1, cols_pad, 3 * LANES), lambda i: (0, i // groups, i % groups, 0, 0)
    )
    lat_steps = CORES * groups
    row_spec = pl.BlockSpec((1, channels), lambda i: (0, 0))
    line_spec = pl.BlockSpec((channels,), lambda i: (0,))
    here_spec, pad_spec = lat_spec(cols_here, channels), lat_spec(cols_pad, channels)
    mask, mask_spec = valid_mask, pl.BlockSpec((rows_here, cols_here), lambda i: (0, 0))
    packed_shape = (BLOCKS, CORES, groups, cols_pad, 3 * LANES)
    flat_shape = (members, groups, cols_pad, 3 * LANES)
    pad_shape = (CORES, groups, PACK, cols_pad, channels)
    here_shape = (CORES, groups, PACK, cols_here, channels)

    def shape(s, d):
        return jax.ShapeDtypeStruct(s, d)

    index = row_at * col_devs + col_at
    devices = row_devs * col_devs
    all_bits = [2**k for k in range(16) if 2**k < devices]
    cube, outer_bits = all_bits[1:4], all_bits[4:]
    core_line = core.astype(jnp.int32).reshape(1)

    def bit(mask_bit):
        return (index // mask_bit) % 2

    def partner(x, flip):
        return lax.ppermute(x, AXES, [(d, d ^ flip) for d in range(devices)])


    orders = [[cube[(p + k) % 3] for k in range(3)] for p in range(3)]

    def bits(level):
        return jnp.stack([bit(o[level]) for o in orders]).astype(jnp.int32)

    def zipped(kept, got):
        return [x for pair in zip(kept, got) for x in pair]

    def merge(own, got, which, single, after):
        n, (r, c) = len(own), own[0].shape
        out = [shape((n, 2 * r, c), BF)] * 2 if single else [shape((2 * r, c), BF)] * (2 * n)
        return call(
            lambda *refs: merge_kernel(n, single, *refs), zipped(own, got), out, 2.0,
            after=after, prefetch=[which], vmem=34 if single else 12, name="merge",
        )

    class Sum:
        def __init__(self, kept, got):
            self.kept, self.got, self.level = kept, got, 0

        def send(self, arrays):
            self.got = [partner(x, o[self.level]) for x, o in zip(arrays, orders)]

        def halve(self, after=()):
            first, n = self.level == 0, len(orders)
            rows, wide = self.kept[0].shape
            half = rows // n if first else rows // 2
            tiles = 2 if first else 1
            t = half // tiles
            args, specs = [], []
            if first:
                for chunk in range(2 * n):
                    grad, at = divmod(chunk, n)
                    args += [self.kept[grad], self.got[grad]]
                    specs += [pl.BlockSpec((t, wide), lambda i, b, at=at: (at * tiles + i, 0))] * 2
            else:
                for p in range(n):
                    stay = lambda i, b, p=p: (b[p] * tiles + i, 0)
                    leave = lambda i, b, p=p: ((1 - b[p]) * tiles + i, 0)
                    args += [self.kept[p], self.got[p]] * 2
                    specs += [pl.BlockSpec((t, wide), m) for m in (stay, stay, leave, leave)]
            res = call(
                halve_first_kernel if first else halve_kernel,
                args, [shape((half, wide), BF)] * (2 * n), 3.0,
                after=after, prefetch=[bits(self.level)], grid=(tiles,), in_specs=specs,
                out_specs=[pl.BlockSpec((t, wide), lambda i, b: (i, 0))] * (2 * n), vmem=20 if first else 12, name="halve",
            )
            self.kept = res[0::2]
            self.send(res[1::2])
            self.level += 1
            return self.kept[0]

        def settle(self, after=()):
            n = len(orders)
            self.kept = call(
                lambda *refs: settle_kernel(n, *refs), zipped(self.kept, self.got),
                [shape(x.shape, BF) for x in self.kept], 1.0, after=after, name="settle",
            )
            return self.kept[0]

        def join(self, stay, got, after=()):
            n, (r, c) = len(orders), self.kept[0].shape
            self.kept, sent = call(
                lambda *refs: join_kernel(n, *refs), self.kept + [stay, got],
                [shape((n * (r + EXTRA), c), BF)] * 2, 1.5, after=after, name="join",
            )
            self.got = partner(sent, outer_bits[0])
            for m in outer_bits[1:]:
                self.kept, sent = add(self.kept, self.got, BF)
                self.got = partner(sent, m)
            return self.kept

        def part(self, after=()):
            n, (r, c) = len(orders), self.kept.shape
            res = call(
                part_kernel, [self.kept, self.got], [shape((r // n, c), BF)] * (2 * n), 1.5,
                after=after, name="part",
            )
            self.kept = res[:n]
            self.level = len(cube) - 1
            self.send(res[n:])
            return self.kept[0]

        def double(self, after=()):
            n, (r, c), single = len(orders), self.kept[0].shape, self.level == 0
            res = merge(self.kept, self.got, bits(self.level), single, after)
            self.level -= 1
            if not single:
                self.kept = res[:n]
                self.send(res[n:])
                return self.kept[0]
            self.kept, sent = (x.reshape(2 * n * r, c) for x in res)
            self.got = partner(sent, 1)
            return self.kept

        def widen(self, done, after=()):
            rows, c = self.kept.shape
            chunk = rows // (len(orders) * BLOCKS)
            t = 2 * (chunk - EXTRA)
            steps = rows // chunk // 4
            full_rows = CORES * steps * t
            x = self.got if done else self.kept
            full = [shape((full_rows, c), F32), shape((c, full_rows), F32)]
            extra = [shape((2 * steps, EXTRA, c), BF)] * 2
            at = lambda i, h: (1 - h[0] if done else h[0]) * steps + i
            return call(
                widen_kernel, [x, x] + done[:2], full + extra, 5.0, after=after,
                prefetch=[core_line], grid=(steps,),
                in_specs=[
                    pl.BlockSpec((2 * chunk, c), lambda i, h: (i, 0)),
                    pl.BlockSpec((2 * chunk, c), lambda i, h: (steps + i, 0)),
                ] + [pl.BlockSpec(memory_space=pl.ANY)] * len(done[:2]),
                out_specs=[
                    pl.BlockSpec((t, c), lambda i, h: (at(i, h), 0)),
                    pl.BlockSpec((c, t), lambda i, h: (0, at(i, h))),
                ] + [pl.BlockSpec((2, EXTRA, c), lambda i, h: (i, 0, 0))] * 2,
                input_output_aliases={3: 0, 4: 1} if done else {}, hbm=(0, 1), name="widen",
            )

    def add(x, y, dtype, after=()):
        return call(add_kernel, [x, y], [shape(x.shape, dtype)] * 2, 1.0, after=after, name="add")

    class Tail:
        def __init__(self, x):
            self.bits = list(all_bits)
            self.x, self.got = x[0], partner(x[1], self.bits[0])

        def step(self, after=()):
            self.x, sent = add(self.x, self.got, F32, after)
            self.bits.pop(0)
            if self.bits:
                self.got = partner(sent, self.bits[0])
            return self.x


    turned_shape = shape((cols_here, rows_here, channels), F32)
    turned_spec = pl.BlockSpec(turned_shape.shape, lambda i: (0, 0, 0))

    def turn_back(x):
        return x.swapaxes(0, 1)

    def lon_forward(cells, table, after=()):
        return call(
            lambda *refs: lon_kernel(col_devs, row_group, *refs),
            [cells.reshape(flat_shape), table],
            [shape((half_rows, lats, LANES), BF)] * 2, 5.5, after=after,
            scratch_shapes=[pltpu.VMEM((all_rows * lats, LANES), F32)],
            vmem=24, name="lon_forward",
        )

    def lon_backward(pieces, table, after=()):
        return call(
            lambda *refs: lon_back_kernel(
                col_devs, row_group, len(pieces), refs[len(pieces)], *refs[: len(pieces)], refs[-1]
            ),
            [*pieces, table], shape(flat_shape, BF), 3.5, after=after, vmem=16, name="lon_backward",
        )

    def big_weight(w):
        w = lax.dynamic_index_in_dim(w, mine, 1, keepdims=False)
        gap = LANES - block
        w = jnp.pad(w, ((0, 0), (0, gap), (0, gap)))
        return jnp.concatenate(
            [jnp.concatenate([w[0], w[1]], 1), jnp.concatenate([-w[1], w[0]], 1)], 0
        )

    def big_bias(b):
        b = lax.dynamic_index_in_dim(b.reshape(2, BLOCKS, block), mine, 1, keepdims=False)
        return jnp.pad(b, ((0, 0), (0, LANES - block))).reshape(1, 2 * LANES)

    wa, wb = big_weight(mix_weight_a), big_weight(mix_weight_b)
    ba, bb = big_bias(mix_bias_a), big_bias(mix_bias_b)

    normed, send = call(
        first_kernel, [x5, mask, first_gain, first_shift],
        [shape(pad_shape, BF), shape(packed_shape, BF)], 6.0, hbm=(0, 1),
        grid=(lat_steps,), in_specs=[here_spec, mask_spec, line_spec, line_spec],
        out_specs=[pad_spec, packed_spec], vmem=16, name="first_norm",
    )
    cells = exchange(send.reshape(flat_shape))

    own, other = lon_forward(cells, lon_fwd)
    other = swap(other)
    own, other, modes = call(
        mix_kernel, [own, other, lat_fwd, lat_inv, wa, ba, wb, bb],
        [shape((lats, half_rows, LANES), BF)] * 2
        + [shape((slots_pad // WIDE, WIDE * LAT, 2 * LANES), BF)], 22.0,
        scratch_shapes=[pltpu.VMEM((2 * lats * half_rows, LANES), F32)], vmem=32, hbm=(2,), name="mix",
    )
    other = swap(other)
    lon_out = lon_backward([own, other], lon_winv)
    got = exchange(lon_out)

    cot_pad = call(
        pad_kernel, [cot5], shape(pad_shape, BF), 2.0, after=[lon_out], grid=(lat_steps,),
        in_specs=[here_spec], out_specs=[pad_spec], name="pad",
    )

    resid, tokens = call(
        second_kernel,
        [x5, normed, mask, got.reshape(packed_shape), row(second_gain), row(second_shift)],
        [shape(pad_shape, F32), shape(pad_shape, BF)], 8.5, after=[cot_pad],
        grid=(lat_steps,),
        in_specs=[here_spec, pad_spec, mask_spec, packed_spec, row_spec, row_spec],
        out_specs=[pad_spec, pad_spec], vmem=56, name="second_norm",
    )
    tokens2, cot2 = tokens.reshape(-1, channels), cot_pad.reshape(-1, channels)
    count, hidden = tokens2.shape[0], expand_weight.shape[1]
    tile = hidden // 6
    all_tok = pl.BlockSpec((count, channels), lambda i: (0, 0))
    by_col = lambda n: pl.BlockSpec((n, tile), lambda i: (0, i))
    by_row = pl.BlockSpec((tile, channels), lambda i: (i, 0))
    act, gpre, gtok, g_ebias = call(
        chain_kernel,
        [tokens2, cot2, expand_weight, row(expand_bias), reduce_weight],
        [
            shape((count, hidden), BF), shape((count, hidden), BF),
            shape((count, channels), BF), shape((1, hidden), F32),
        ],
        25.0, grid=(6,),
        in_specs=[all_tok, all_tok, by_col(channels), by_col(1), by_row],
        out_specs=[by_col(count), by_col(count), all_tok, by_col(1)], scratch_shapes=[pltpu.VMEM((count, channels), F32)], vmem=46, hbm=(0, 1, 2), pin=True, name="mlp_chain",
    )

    halves = 3
    assert halves * CORES * tile == hidden

    def weight_grad(left, right, own, after, name):
        at = lambda i, c: (c[0] if own else 1 - c[0]) * halves + i
        return call(
            weight_grad_kernel, [left, right],
            [shape((halves * tile, channels), BF), shape((8, LANES), F32)], 5.0,
            after=after, prefetch=[core_line], grid=(halves,),
            in_specs=[
                pl.BlockSpec((count, tile), lambda i, c: (0, at(i, c))),
                pl.BlockSpec((count, channels), lambda i, c: (0, 0)),
            ],
            out_specs=[
                pl.BlockSpec((tile, channels), lambda i, c: (i, 0)),
                pl.BlockSpec((8, LANES), lambda i, c: (0, 0)),
            ],
            vmem=20, name=name,
        )

    one_row = shape((1, channels), F32)
    grad_resid, send, g_gain2, g_shift2, g_rbias = call(
        third_kernel,
        [resid, gtok.reshape(pad_shape), cot_pad, mask, row(second_gain)],
        [shape(pad_shape, BF), shape(packed_shape, BF)] + [one_row] * 3, 9.0,
        grid=(lat_steps,), in_specs=[pad_spec, pad_spec, pad_spec, mask_spec, row_spec],
        out_specs=[pad_spec, packed_spec, row_spec, row_spec, row_spec], vmem=56, name="second_back",
    )
    cells = exchange(send.reshape(flat_shape))

    sent_r, token = weight_grad(act, cot2, False, [g_gain2], "reduce_grad")
    sent_e, token = weight_grad(gpre, tokens2, False, [token], "expand_grad")
    kept_r, token = weight_grad(act, cot2, True, [token], "reduce_grad")
    kept_e, token = weight_grad(gpre, tokens2, True, [token], "expand_grad")
    sums = Sum([kept_r, kept_e], [partner(sent_r, 1), partner(sent_e, 1)])

    own, other = lon_forward(cells, lon_wfwd, after=[token])
    other = swap(other)
    token = sums.halve(after=[own])
    run = half_rows // SPLIT
    pieces, grads = [], []
    grad_shape = shape((4 * LANES + 16, 2 * LANES), F32)
    for k in range(SPLIT):
        here = pl.BlockSpec((run, lats, LANES), lambda i, k=k: (k, 0, 0))
        steps = modes.shape[0] // SPLIT
        const = lambda x: pl.BlockSpec(x.shape, lambda i: (0, 0))
        o, t, g = call(
            mix_back_kernel, [own, other, modes, lat_fwd, lat_inv, wa, ba, wb, bb] + grads,
            [shape((lats, run, LANES), BF)] * 2 + [grad_shape], 13.0,
            after=[token],
            in_specs=[
                here, here, pl.BlockSpec((steps,) + modes.shape[1:], lambda i, k=k: (k, 0, 0)),
            ] + [const(x) for x in (lat_fwd, lat_inv, wa, ba, wb, bb, *grads)],
            scratch_shapes=[pltpu.VMEM((2 * lats * run, LANES), F32)], name="mix_back",
        )
        pieces.append((o, swap(t)))
        grads = [g]
        token = sums.halve(after=[o])
    token = sums.settle(after=[token])
    send = lon_backward(
        [p[0] for p in pieces] + [p[1] for p in pieces], lon_inv, after=[token]
    )
    got = exchange(send)
    stay, leave = call(
        lambda *refs: collect_kernel(block, *refs), grads,
        [shape((3 * EXTRA, channels), F32)] * 2, 1.5, after=[send], prefetch=[core_line],
        name="collect",
    )
    token = sums.join(stay, partner(leave, 1))

    outputs, token = call(
        branch_kernel,
        [act.reshape(CORES, groups, PACK, cols_pad, hidden), reduce_weight, resid, row(reduce_bias)],
        [turned_shape, shape((8, LANES), F32)], 10.0, after=[token], grid=(groups,),
        in_specs=[
            both_spec(cols_pad, hidden), pl.BlockSpec((hidden, channels), lambda i: (0, 0)),
            both_spec(cols_pad, channels), row_spec,
        ],
        out_specs=[turned_spec, pl.BlockSpec((8, LANES), lambda i: (0, 0))], vmem=32, name="branch",
    )

    touched = call(
        touch_kernel, [], shape((8, LANES), F32), 0.5, after=[got, token], name="touch"
    )
    token = sums.part(after=[touched])
    token = sums.double(after=[token])
    token = sums.double(after=[token])

    grad_inputs, g_gain1, g_shift1 = call(
        last_kernel, [x5, grad_resid, mask, got.reshape(packed_shape), row(first_gain)],
        [turned_shape] + [one_row] * 2, 9.0, after=[token],
        grid=(lat_steps,), in_specs=[here_spec, pad_spec, mask_spec, packed_spec, row_spec],
        out_specs=[turned_spec, row_spec, row_spec], vmem=56, name="first_back",
    )
    tail_sum = Tail(
        call(
            tail_kernel, [g_gain1, g_shift1, g_gain2, g_shift2, g_rbias, g_ebias],
            [shape((1, 5 * channels + hidden), F32)] * 2, 1.0, name="tail",
        )
    )
    token = tail_sum.step()
    token = sums.double(after=[token])
    token = tail_sum.step(after=[token])
    own_done = sums.widen([], after=[token])
    token = tail_sum.step(after=[own_done[2]])
    g_reduce, g_expand, *got_extra = sums.widen(own_done, after=[token])
    token = got_extra[0]
    while tail_sum.bits:
        token = tail_sum.step(after=[token])
    weight_out, bias_out = shape(mix_weight_a.shape, F32), shape(mix_bias_a.shape, F32)
    g_wa, g_wb, g_ba, g_bb = call(
        lambda *refs: spread_kernel(block, *refs), own_done[2:] + got_extra,
        [weight_out, weight_out, bias_out, bias_out], 3.0, prefetch=[core_line], name="spread",
    )

    tail = tail_sum.x
    g_gain1, g_shift1, g_gain2, g_shift2, g_rbias = (
        tail[0, k * channels : (k + 1) * channels] for k in range(5)
    )
    g_ebias = tail[0, 5 * channels :]

    def flat(v):
        return v.reshape(-1)

    return (
        turn_back(outputs), turn_back(grad_inputs),
        flat(g_gain1), flat(g_shift1), g_wa, g_ba, g_wb, g_bb, flat(g_gain2), flat(g_shift2),
        g_expand, g_ebias, g_reduce, flat(g_rbias),
    )


def solution(mesh):
    grid = P("rows", "cols", None)
    placed = (grid, P("rows", "cols"), grid) + (P(),) * 12
    return jax.shard_map(
        per_device,
        mesh=mesh,
        in_specs=placed,
        out_specs=(grid, grid) + (P(),) * 12,
        check_vma=False,
    )
```

```python
import math

import jax
import jax.numpy as jnp
import numpy as np
from jax import lax
from jax.experimental import pallas as pl
from jax.experimental.pallas import tpu as pltpu
from jax.sharding import PartitionSpec as P

BLOCKS = 8
LAT = 96
CORES = 2
PACK = 4
LANES = 128

shrink_level = 0.01
shrink_soft = 0.1
norm_eps = 1e-05
gelu_root = math.sqrt(2.0 / math.pi)
gelu_cube = 0.044715

BF = jnp.bfloat16
F32 = jnp.float32
AXES = ("rows", "cols")


def up_to(value, step):
    return (value + step - 1) // step * step


def call(kernel, args, out_shape, us, after=(), in_specs=None, prefetch=(), vmem=12, hbm=(), pin=False, **kw):
    outs = out_shape if isinstance(out_shape, (list, tuple)) else [out_shape]
    lead, n_in, n_after = len(prefetch), len(args), len(after)

    def body(*refs):
        kernel(*refs[: lead + n_in], *refs[lead + n_in + n_after :])

    if pin:
        at = range(len(args)) if pin is True else pin
        args = [
            pltpu.with_memory_space_constraint(x, pltpu.HBM) if k in at else x
            for k, x in enumerate(args)
        ]
    grid = kw.pop("grid", (1,))
    whole = lambda x: pl.BlockSpec(x.shape, lambda *_, n=len(x.shape): (0,) * n)
    specs = list(in_specs) if in_specs is not None else [whole(a) for a in args]
    specs += [pl.BlockSpec(memory_space=pl.ANY)] * n_after
    out_specs = kw.pop("out_specs", None) or [whole(o) for o in outs]
    got = pl.pallas_call(
        body,
        grid_spec=pltpu.PrefetchScalarGridSpec(
            num_scalar_prefetch=lead,
            grid=grid,
            in_specs=specs,
            out_specs=out_specs,
            scratch_shapes=kw.pop("scratch_shapes", ()),
        ),
        out_shape=[pltpu.HBM(o.shape, o.dtype) if k in hbm else o for k, o in enumerate(outs)],
        compiler_params=pltpu.CompilerParams(vmem_limit_bytes=vmem * 1024 * 1024),
        cost_estimate=pl.CostEstimate(
            flops=0, bytes_accessed=int(us * 1e5), transcendentals=0
        ),
        **kw,
    )(*prefetch, *args, *after)
    return list(got) if isinstance(out_shape, (list, tuple)) else got[0]


SPLIT = 1
UNROLL = 1
WIDE = 12


def lon_table(lon_size, col_devs, cols_here, cols_pad, slots, slots_pad):
    modes = lon_size // 2 + 1
    table = np.zeros((CORES, 2, slots_pad, col_devs, cols_pad), np.float64)
    weights = np.zeros((CORES, slots_pad), np.float64)
    place = np.arange(lon_size).reshape(col_devs, cols_here)
    for half in range(CORES):
        for slot in range(slots):
            mode = half * slots + slot
            if mode >= modes:
                continue
            angle = (place * mode % lon_size) * (2.0 * math.pi / lon_size)
            table[half, 0, slot, :, :cols_here] = np.cos(angle) / math.sqrt(lon_size)
            edge = mode == 0 or 2 * mode == lon_size
            if not edge:
                table[half, 1, slot, :, :cols_here] = np.sin(angle) / math.sqrt(lon_size)
            weights[half, slot] = 1.0 if edge else 2.0
    weighted = table * weights[:, None, :, None, None]
    rows = 2 * slots_pad
    flat = [
        a.reshape(CORES, 2, SPLIT, slots_pad // SPLIT, col_devs, cols_pad)
        .swapaxes(1, 2)
        .reshape(CORES, rows, col_devs * cols_pad)
        for a in (table, weighted)
    ]
    return [
        np.stack([np.concatenate([a[h], a[1 - h]], 0) for h in range(CORES)]) for a in flat
    ]


def lat_table(rows_here, row_group):
    share = rows_here // CORES
    out = []
    for h in range(CORES):
        own = [
            rows_here * r + share * h + i for r in range(row_group) for i in range(share)
        ]
        other = [
            rows_here * r + share * (1 - h) + i for r in range(row_group) for i in range(share)
        ]
        angle = np.outer(np.arange(LAT), np.array(own + other)) % LAT * (2.0 * math.pi / LAT)
        cos, sin = np.cos(angle) / math.sqrt(LAT), np.sin(angle) / math.sqrt(LAT)
        out.append(np.block([[cos, -sin], [-sin, -cos]]))
    return np.stack(out)


def pack_lanes(tiles):
    a, b, c, d = tiles
    lane = lax.broadcasted_iota(jnp.int32, a.shape, a.ndim - 1)
    axis = a.ndim - 1
    b, c, d = pltpu.roll(b, 96, axis), pltpu.roll(c, 64, axis), pltpu.roll(d, 32, axis)
    return [
        jnp.where(lane < 96, a, b),
        jnp.where(lane < 64, b, c),
        jnp.where(lane < 32, c, d),
    ]


def unpack_lanes(tiles):
    a, b, c = tiles
    lane = lax.broadcasted_iota(jnp.int32, a.shape, a.ndim - 1)
    axis = a.ndim - 1
    return [
        a,
        pltpu.roll(jnp.where(lane >= 96, a, b), 32, axis),
        pltpu.roll(jnp.where(lane >= 64, b, c), 64, axis),
        pltpu.roll(c, 96, axis),
    ]


def tiles_of(value):
    return [value[:, LANES * i : LANES * (i + 1)] for i in range(value.shape[1] // LANES)]


def split_blocks(value):
    tiles = tiles_of(value)
    out = []
    for i in range(0, len(tiles), 3):
        out += unpack_lanes(tiles[i : i + 3])
    return out


def join_blocks(tiles):
    out = []
    for i in range(0, len(tiles), 4):
        out += pack_lanes(tiles[i : i + 4])
    return jnp.concatenate(out, axis=1)


def pad_rows(value, rows):
    return jnp.concatenate(
        [value, jnp.zeros((rows - value.shape[0], value.shape[1]), value.dtype)], axis=0
    )


def store_packed(ref, half, per_lat):
    split = [split_blocks(v) for v in per_lat]
    for q in range(BLOCKS):
        packed = pack_lanes([split[j][q] for j in range(PACK)])
        ref[q, half, 0] = jnp.concatenate(packed, axis=1).astype(ref.dtype)


def load_packed(ref, half):
    by_lat = [[] for _ in range(PACK)]
    for q in range(BLOCKS):
        parts = unpack_lanes(tiles_of(ref[q, half, 0].astype(F32)))
        for j in range(PACK):
            by_lat[j].append(parts[j])
    return [join_blocks(tiles) for tiles in by_lat]


def stats(x):
    average = jnp.mean(x, axis=-1, keepdims=True)
    centred = x - average
    spread = jnp.mean(centred * centred, axis=-1, keepdims=True)
    inv = lax.rsqrt(spread + norm_eps)
    return centred * inv, inv


def norm_back(grad, xhat, inv, gain):
    scaled = grad * gain
    m1 = jnp.mean(scaled, axis=-1, keepdims=True)
    m2 = jnp.mean(scaled * xhat, axis=-1, keepdims=True)
    return inv * (scaled - m1 - xhat * m2)


def mask_column(mask_ref, lat, rows):
    line = mask_ref[pl.ds(lat, 1), :].astype(F32)
    shape = (rows, line.shape[1])
    row, col = (lax.broadcasted_iota(jnp.int32, shape, k) for k in range(2))
    return jnp.sum(jnp.where(row == col, line, 0.0), axis=1, keepdims=True)


def first_kernel(x_ref, mask_ref, gain_ref, shift_ref, normed_ref, out_ref):
    rows = normed_ref.shape[3]
    half, first = 0, pl.program_id(0) * PACK
    lats = []
    for j in range(PACK):
        x = pad_rows(x_ref[half, 0, j].astype(F32), rows)
        xhat, _ = stats(x)
        y = mask_column(mask_ref, first + j, rows) * (xhat * gain_ref[...][None] + shift_ref[...][None])
        normed_ref[half, 0, j] = y.astype(BF)
        lats.append(y)
    store_packed(out_ref, half, lats)


def pad_kernel(x_ref, out_ref):
    rows = out_ref.shape[3]
    for j in range(PACK):
        out_ref[0, 0, j] = pad_rows(x_ref[0, 0, j].astype(F32), rows).astype(BF)


def second_kernel(
    x_ref, normed_ref, mask_ref, got_ref, gain_ref, shift_ref, resid_ref, tok_ref
):
    rows = normed_ref.shape[3]
    half, first = 0, pl.program_id(0) * PACK
    spatial = load_packed(got_ref, half)
    for j in range(PACK):
        x = pad_rows(x_ref[half, 0, j].astype(F32), rows)
        resid = x + normed_ref[half, 0, j].astype(F32)
        resid = resid + mask_column(mask_ref, first + j, rows) * spatial[j]
        resid_ref[half, 0, j] = resid
        xhat, _ = stats(resid)
        tok_ref[half, 0, j] = (xhat * gain_ref[...] + shift_ref[...]).astype(BF)


def third_kernel(
    resid_ref, gtok_ref, cot_ref, mask_ref, gain_ref,
    gresid_ref, send_ref, ggain_ref, gshift_ref, gbias_ref,
):
    @pl.when(pl.program_id(0) == 0)
    def _():
        ggain_ref[...] = jnp.zeros_like(ggain_ref)
        gshift_ref[...] = jnp.zeros_like(gshift_ref)
        gbias_ref[...] = jnp.zeros_like(gbias_ref)

    half, first = 0, pl.program_id(0) * PACK
    lats = []
    for j in range(PACK):
        xhat, inv = stats(resid_ref[half, 0, j])
        gtok = gtok_ref[half, 0, j].astype(F32)
        cot = cot_ref[half, 0, j].astype(F32)
        ggain_ref[...] += jnp.sum(gtok * xhat, axis=0, keepdims=True)
        gshift_ref[...] += jnp.sum(gtok, axis=0, keepdims=True)
        gbias_ref[...] += jnp.sum(cot, axis=0, keepdims=True)
        gres = cot + norm_back(gtok, xhat, inv, gain_ref[...])
        gresid_ref[half, 0, j] = gres.astype(gresid_ref.dtype)
        lats.append(mask_column(mask_ref, first + j, gres.shape[0]) * gres)
    store_packed(send_ref, half, lats)


def store_lat(out_ref, lat, value):
    out_ref[:, lat, :] = value[: out_ref.shape[0]]


def last_kernel(
    x_ref, gresid_ref, mask_ref, got_ref, gain_ref, out_ref, ggain_ref, gshift_ref
):
    @pl.when(pl.program_id(0) == 0)
    def _():
        ggain_ref[...] = jnp.zeros_like(ggain_ref)
        gshift_ref[...] = jnp.zeros_like(gshift_ref)

    rows = gresid_ref.shape[3]
    half, first = 0, pl.program_id(0) * PACK
    got = load_packed(got_ref, half)
    for j in range(PACK):
        x = pad_rows(x_ref[half, 0, j].astype(F32), rows)
        xhat, inv = stats(x)
        gres = gresid_ref[half, 0, j].astype(F32)
        grad = mask_column(mask_ref, first + j, rows) * (gres + got[j])
        ggain_ref[...] += jnp.sum(grad * xhat, axis=0, keepdims=True)
        gshift_ref[...] += jnp.sum(grad, axis=0, keepdims=True)
        store_lat(out_ref, first + j, gres + norm_back(grad, xhat, inv, gain_ref[...]))


OUTER = (((0,), (0,)), ((), ()))
ACROSS = (((1,), (1,)), ((), ()))


def chain_kernel(
    tok_ref, cot_ref, up_ref, bias_ref, down_ref, act_ref, gpre_ref, gtok_ref, gbias_ref, sum_ref
):
    @pl.when(pl.program_id(0) == 0)
    def _():
        sum_ref[...] = jnp.zeros_like(sum_ref)

    pre = jnp.dot(tok_ref[...], up_ref[...], preferred_element_type=F32) + bias_ref[...]
    gate = gelu_gate(pre)
    act_ref[...] = (pre * gate).astype(BF)
    gact = lax.dot_general(cot_ref[...], down_ref[...], ACROSS, preferred_element_type=F32)
    gpre = gelu_slope(pre, gate) * gact
    gbias_ref[...] = jnp.sum(gpre, axis=0, keepdims=True)
    gpre = gpre.astype(BF)
    gpre_ref[...] = gpre
    sum_ref[...] += lax.dot_general(gpre, up_ref[...], ACROSS, preferred_element_type=F32)

    @pl.when(pl.program_id(0) == pl.num_programs(0) - 1)
    def _():
        gtok_ref[...] = sum_ref[...].astype(gtok_ref.dtype)


def weight_grad_kernel(core_ref, left_ref, right_ref, out_ref, token_ref):
    token_ref[...] = jnp.zeros_like(token_ref)
    out_ref[...] = lax.dot_general(
        left_ref[...], right_ref[...], OUTER, preferred_element_type=F32
    ).astype(BF)


def branch_kernel(act_ref, down_ref, resid_ref, bias_ref, out_ref, token_ref):
    token_ref[...] = jnp.zeros_like(token_ref)
    cols = resid_ref.shape[3]
    rows = CORES * PACK * cols
    act = act_ref[...].reshape(rows, act_ref.shape[-1])
    branch = jnp.dot(act, down_ref[...], preferred_element_type=F32) + bias_ref[...]
    for half in range(CORES):
        for j in range(PACK):
            at = (half * PACK + j) * cols
            lat = (half * pl.num_programs(0) + pl.program_id(0)) * PACK + j
            store_lat(out_ref, lat, resid_ref[half, 0, j] + branch[at : at + cols])


def plus(left, right):
    return (left.astype(F32) + right.astype(F32)).astype(BF)


def halve_first_kernel(bits_ref, *refs):
    count = len(refs) // 6
    for p in range(count):
        a, b, c, d = refs[4 * p : 4 * p + 4]
        low, high = plus(a[...], b[...]), plus(c[...], d[...])
        first = bits_ref[p] == 0
        refs[4 * count + 2 * p][...] = jnp.where(first, low, high)
        refs[4 * count + 2 * p + 1][...] = jnp.where(first, high, low)


def halve_kernel(bits_ref, *refs):
    count = len(refs) // 6
    for k in range(2 * count):
        refs[4 * count + k][...] = plus(refs[2 * k][...], refs[2 * k + 1][...])


def join_kernel(count, *refs):
    stay, got = refs[count : count + 2]
    for p in range(count):
        n, m = refs[p].shape[0], stay.shape[0] // count
        value = refs[p][...]
        rows = slice(p * m, (p + 1) * m)
        extra = (stay[rows] + got[rows]).astype(BF)
        for out in refs[-2:]:
            out[p * (n + m) : p * (n + m) + n] = value
            out[p * (n + m) + n : (p + 1) * (n + m)] = extra


def settle_kernel(count, *refs):
    for p in range(count):
        refs[2 * count + p][...] = plus(refs[2 * p][...], refs[2 * p + 1][...])


def touch_kernel(out):
    out[...] = jnp.zeros_like(out)


def part_kernel(kept, got, *outs):
    n, count = outs[0].shape[0], len(outs) // 2
    for p in range(count):
        rows = slice(p * n, (p + 1) * n)
        value = plus(kept[rows], got[rows])
        outs[p][...] = value
        outs[count + p][...] = value


def add_kernel(left, right, *outs):
    value = left[...].astype(F32) + right[...].astype(F32)
    for out in outs:
        out[...] = value.astype(out.dtype)


def tail_kernel(*refs):
    for out in refs[-2:]:
        at = 0
        for ref in refs[:-2]:
            out[:, at : at + ref.shape[1]] = ref[...]
            at += ref.shape[1]


def merge_kernel(count, single, bits_ref, *refs):
    outs = refs[2 * count :]
    for p in range(count):
        own, got = refs[2 * p], refs[2 * p + 1]
        n = own.shape[0]
        for out in (outs[p::count] if not single else [o.at[p] for o in outs]):
            out[pl.ds(pl.multiple_of(bits_ref[p] * n, 16), n), :] = own[...]
            out[pl.ds(pl.multiple_of((1 - bits_ref[p]) * n, 16), n), :] = got[...]


def widen_kernel(core_ref, reduce_ref, expand_ref, *refs):
    reduce_out, expand_out, extra_r, extra_e = refs[-4:]
    n = reduce_out.shape[0] // 2
    for k in range(2):
        at = k * (n + EXTRA)
        reduce_out[k * n : (k + 1) * n] = reduce_ref[at : at + n].astype(F32)
        expand_out[:, k * n : (k + 1) * n] = expand_ref[at : at + n].astype(F32).T
        extra_r[k] = reduce_ref[at + n : at + n + EXTRA]
        extra_e[k] = expand_ref[at + n : at + n + EXTRA]


EXTRA = 16


def collect_kernel(block, core_ref, grad_ref, *refs):
    wide = 2 * LANES
    halves, lines = [], []
    for i in range(2):
        g = grad_ref[i * wide : (i + 1) * wide]
        at = 2 * wide + 8 * i
        line = jnp.sum(grad_ref[at : at + 8], axis=0, keepdims=True)
        top, low = g[:block], g[LANES : LANES + block]
        halves.append([top[:, :LANES] + low[:, LANES:], top[:, LANES:] - low[:, :LANES]])
        lines += [line[:, :LANES], line[:, LANES:]]
    rows = lax.broadcasted_iota(jnp.int32, (EXTRA, LANES), 0)
    bias = sum(jnp.where(rows == k, line, 0.0) for k, line in enumerate(lines))
    first = core_ref[0] == 0
    for k, out in enumerate(refs[-2:]):
        own = first if k == 0 else jnp.logical_not(first)
        out[...] = jnp.zeros_like(out)
        for p in range(2):
            value = jnp.where(own, halves[0][p], halves[1][p])
            for t in range(block // EXTRA):
                at = slice(t * LANES, (t + 1) * LANES)
                out[p * EXTRA : (p + 1) * EXTRA, at] = value[t * EXTRA : (t + 1) * EXTRA]
        out[2 * EXTRA : 3 * EXTRA, :LANES] = jnp.where(own, bias, 0.0)


def spread_kernel(block, core_ref, *refs):
    own, got = refs[:2], refs[2:4]
    wa_ref, wb_ref, ba_ref, bb_ref = refs[4:]
    first = core_ref[0] == 0
    per = own[0].shape[0]
    biases = [[] for _ in range(4)]
    for q in range(BLOCKS):
        for half in range(CORES):
            for p in range(3):
                if half == 1 and p == 2:
                    continue
                k = sum(((q >> ((p + j) % 3)) & 1) << (2 - j) for j in range(3))
                at = p * BLOCKS + k
                mine, other = (r[at // per][at % per].astype(F32) for r in (own, got))
                value = jnp.where(first, mine, other) if half == 0 else jnp.where(first, other, mine)
                if p == 2:
                    for i in range(4):
                        biases[i].append(value[i : i + 1, :LANES])
                    continue
                out = wb_ref if half else wa_ref
                for t in range(block // EXTRA):
                    out[p, q, t * EXTRA : (t + 1) * EXTRA, :] = value[
                        :, t * LANES : t * LANES + block
                    ]
    for i in range(4):
        (bb_ref if i > 1 else ba_ref)[i % 2 : i % 2 + 1, :] = join_blocks(biases[i])


def lon_kernel(col_devs, row_group, x_ref, table_ref, own_ref, other_ref, turn_ref):
    groups = x_ref.shape[1]
    rows = table_ref.shape[0]
    lats = own_ref.shape[1]
    slots = own_ref.shape[0]
    for r in range(row_group):
        for g in range(groups):
            cells = jnp.concatenate(
                [x_ref[r * col_devs + c, g] for c in range(col_devs)], axis=0
            )
            modes = jnp.dot(table_ref[...], cells, preferred_element_type=F32)
            for j, tile in enumerate(unpack_lanes(tiles_of(modes))):
                at = (r * groups + g) * PACK + j
                turn_ref[pl.ds(at, rows, stride=lats), :] = tile

    @pl.loop(0, slots, unroll=4)
    def _(s):
        own_ref[s] = turn_ref[pl.ds(pl.multiple_of(s * lats, 8), lats), :].astype(BF)
        other_ref[s] = turn_ref[
            pl.ds(pl.multiple_of((s + slots) * lats, 8), lats), :
        ].astype(BF)


def lon_back_kernel(col_devs, row_group, pieces, table_ref, *refs):
    out_ref = refs[pieces]
    groups = out_ref.shape[1]
    cols = out_ref.shape[2]
    for r in range(row_group):
        for g in range(groups):
            tiles = []
            for j in range(0, PACK, 2):
                pair = []
                for k in range(2):
                    at = (r * groups + g) * PACK + j + k
                    pair.append(jnp.concatenate([r_[at] for r_ in refs[:pieces]], axis=0))
                cells = jnp.dot(
                    table_ref[...], jnp.concatenate(pair, axis=1), preferred_element_type=F32
                )
                tiles += tiles_of(cells)
            packed = jnp.concatenate(pack_lanes(tiles), axis=1).astype(BF)
            for c in range(col_devs):
                out_ref[r * col_devs + c, g] = packed[c * cols : (c + 1) * cols]


def gelu_gate(v):
    inner = v * (gelu_root * gelu_cube * (v * v) + gelu_root)
    return 0.5 * jnp.tanh(inner) + 0.5


def gelu_slope(v, gate):
    inner = 6.0 * gelu_root * gelu_cube * (v * v) + 2.0 * gelu_root
    return gate + (v * gate) * (1.0 - gate) * inner


def slots_down(real, imag):
    return [
        jnp.concatenate([v[:, k * LANES : (k + 1) * LANES] for v in (real, imag)], axis=1)
        for k in range(WIDE)
    ]


def slots_across(value):
    rows = [value[k * LAT : (k + 1) * LAT] for k in range(WIDE)]
    parts = [
        jnp.concatenate([r[:, p * LANES : (p + 1) * LANES] for r in rows], axis=1)
        for p in range(2)
    ]
    return jnp.concatenate(parts, axis=0)


def latitudes(own_ref, other_ref, row, run):
    return jnp.concatenate(
        [own_ref[row], other_ref[row], own_ref[row + run], other_ref[row + run]], axis=0
    )


def turn_out(turn_ref, value, row, lats, rows, run):
    for part in range(2):
        for dest in range(2):
            piece = value[(2 * part + dest) * lats : (2 * part + dest + 1) * lats]
            start = dest * lats * rows + part * run + row
            turn_ref[pl.ds(start, lats, stride=rows), :] = piece


def drain(turn_ref, own_ref, other_ref):
    lats, rows = own_ref.shape[0], own_ref.shape[1]

    @pl.loop(0, lats, unroll=4)
    def _(at):
        own_ref[at] = turn_ref[pl.ds(pl.multiple_of(at * rows, 8), rows), :].astype(BF)
        other_ref[at] = turn_ref[
            pl.ds(pl.multiple_of((at + lats) * rows, 8), rows), :
        ].astype(BF)


def mix_kernel(
    own_ref, other_ref, lat_ref, back_ref, wa_ref, ba_ref, wb_ref, bb_ref,
    own_out, other_out, modes_out, turn_ref,
):
    lats, rows = own_ref.shape[1], own_ref.shape[0]
    run = rows // 2 // SPLIT

    @pl.loop(0, rows // 2 // WIDE, unroll=UNROLL)
    def _(step):
        slot = WIDE * step
        row = slot + slot // run * run
        cells = jnp.concatenate(
            [latitudes(own_ref, other_ref, row + k, run) for k in range(WIDE)], axis=1
        )
        full = jnp.dot(lat_ref[...], cells, preferred_element_type=F32).astype(BF)
        real, imag = full[:LAT], full[LAT:]
        modes = jnp.concatenate(slots_down(real, imag), axis=0)
        modes_out[step] = modes
        pre_a = jnp.dot(modes, wa_ref[...], preferred_element_type=F32) + ba_ref[...]
        hidden = (pre_a * gelu_gate(pre_a)).astype(BF)
        pre_b = jnp.dot(hidden, wb_ref[...], preferred_element_type=F32) + bb_ref[...]
        shrunk = (pre_b - shrink_level * jnp.tanh(pre_b * (1.0 / shrink_soft))).astype(BF)
        mixed = slots_across(shrunk)
        back = jnp.dot(back_ref[...], mixed, preferred_element_type=F32)
        for k in range(WIDE):
            turn_out(turn_ref, back[:, k * LANES : (k + 1) * LANES], row + k, lats, rows, run)

    drain(turn_ref, own_out, other_out)


def row_sums(value):
    return jnp.sum(value.reshape(-1, 8, value.shape[1]), axis=0)


def mix_back_kernel(
    own_ref, other_ref, modes_ref, lat_ref, back_ref, wa_ref, ba_ref, wb_ref, bb_ref,
    *refs,
):
    own_out, other_out, grad_ref, turn_ref = refs[-4:]
    lats, rows = own_ref.shape[1], own_ref.shape[0]
    run = rows // 2
    grad_ref[...] = refs[0][...] if len(refs) > 4 else jnp.zeros_like(grad_ref)
    wide = wa_ref.shape[0]
    gwa_ref, gwb_ref = grad_ref.at[:wide], grad_ref.at[wide : 2 * wide]
    gba_ref, gbb_ref = grad_ref.at[2 * wide : 2 * wide + 8], grad_ref.at[2 * wide + 8 :]

    @pl.loop(0, run // WIDE, unroll=UNROLL)
    def _(step):
        row = WIDE * step
        cells = jnp.concatenate(
            [latitudes(own_ref, other_ref, row + k, run) for k in range(WIDE)], axis=1
        )
        full = jnp.dot(lat_ref[...], cells, preferred_element_type=F32)
        real, imag = full[:LAT], full[LAT:]
        grad = jnp.concatenate(slots_down(real, imag), axis=0)
        modes = modes_ref[step]
        pre_a = jnp.dot(modes, wa_ref[...], preferred_element_type=F32) + ba_ref[...]
        gate_a = gelu_gate(pre_a)
        hidden = (pre_a * gate_a).astype(BF)
        pre_b = jnp.dot(hidden, wb_ref[...], preferred_element_type=F32) + bb_ref[...]
        squash_b = jnp.tanh(pre_b * (1.0 / shrink_soft))
        level = shrink_level / shrink_soft
        factor = level * (squash_b * squash_b) + (1.0 - level)
        grad_b = factor * grad
        gbb_ref[...] += row_sums(grad_b)
        grad_b = grad_b.astype(BF)
        grad_hidden = lax.dot_general(grad_b, wb_ref[...], ACROSS, preferred_element_type=F32)
        gwb_ref[...] += lax.dot_general(hidden, grad_b, OUTER, preferred_element_type=F32)
        grad_a = gelu_slope(pre_a, gate_a) * grad_hidden
        gba_ref[...] += row_sums(grad_a)
        grad_a = grad_a.astype(BF)
        grad_modes = lax.dot_general(
            grad_a, wa_ref[...], ACROSS, preferred_element_type=F32
        ).astype(BF)
        gwa_ref[...] += lax.dot_general(modes, grad_a, OUTER, preferred_element_type=F32)
        mixed = slots_across(grad_modes)
        back = jnp.dot(back_ref[...], mixed, preferred_element_type=F32)
        for k in range(WIDE):
            turn_out(turn_ref, back[:, k * LANES : (k + 1) * LANES], row + k, lats, rows, run)

    drain(turn_ref, own_out, other_out)


def per_device(
    inputs, valid_mask, cotangent, first_gain, first_shift, mix_weight_a, mix_bias_a,
    mix_weight_b, mix_bias_b, second_gain, second_shift, expand_weight, expand_bias,
    reduce_weight, reduce_bias,
):
    row_devs = lax.axis_size("rows")
    col_devs = lax.axis_size("cols")
    rows_here, cols_here, channels = inputs.shape
    block = channels // BLOCKS
    lon_size = cols_here * col_devs
    cols_pad = up_to(cols_here, 16)
    row_group = LAT // rows_here
    members = row_group * col_devs
    share = rows_here // CORES
    groups = share // PACK
    slots = (lon_size // 2 + 2) // 2
    slots_pad = up_to(slots, 16)
    lats = share * row_group
    half_rows = 2 * slots_pad
    all_rows = CORES * half_rows
    assert members == CORES * BLOCKS and block * PACK == 3 * LANES
    assert col_devs * cols_pad == all_rows and CORES * lats == LAT

    row_at, col_at = lax.axis_index("rows"), lax.axis_index("cols")
    core = col_at % CORES
    mine = (row_at % row_group) * (col_devs // CORES) + col_at // CORES

    def pick(table):
        return lax.dynamic_index_in_dim(jnp.asarray(table, BF), core, 0, keepdims=False)

    plain_np, weighted_np = lon_table(
        lon_size, col_devs, cols_here, cols_pad, slots, slots_pad
    )
    lat_np = lat_table(rows_here, row_group)
    lon_fwd, lon_wfwd = pick(plain_np), pick(weighted_np)
    lon_inv, lon_winv = (
        pick(np.swapaxes(plain_np, 1, 2)), pick(np.swapaxes(weighted_np, 1, 2))
    )
    lat_fwd, lat_inv = pick(lat_np), pick(np.swapaxes(lat_np, 1, 2))

    snap_groups = [
        [(s * row_group + r) * col_devs + c for r in range(row_group) for c in range(col_devs)]
        for s in range(row_devs // row_group)
    ]
    core_pairs = [
        (r * col_devs + c, r * col_devs + c ^ 1) for r in range(row_devs) for c in range(col_devs)
    ]

    def exchange(x):
        return lax.all_to_all(x, AXES, 0, 0, axis_index_groups=snap_groups, tiled=True)

    def swap(x):
        return lax.ppermute(x, AXES, core_pairs)

    def fold(x):
        return x.reshape((CORES, groups, PACK) + x.shape[1:])

    def row(v):
        return v.reshape(1, -1)

    x5, cot5 = fold(inputs), fold(cotangent)

    def lat_spec(cols, width):
        return pl.BlockSpec(
            (1, 1, PACK, cols, width), lambda i: (i // groups, i % groups, 0, 0, 0)
        )

    def both_spec(cols, width):
        return pl.BlockSpec((CORES, 1, PACK, cols, width), lambda i: (0, i, 0, 0, 0))

    packed_spec = pl.BlockSpec(
        (BLOCKS, 1, 1, cols_pad, 3 * LANES), lambda i: (0, i // groups, i % groups, 0, 0)
    )
    lat_steps = CORES * groups
    row_spec = pl.BlockSpec((1, channels), lambda i: (0, 0))
    line_spec = pl.BlockSpec((channels,), lambda i: (0,))
    here_spec, pad_spec = lat_spec(cols_here, channels), lat_spec(cols_pad, channels)
    mask, mask_spec = valid_mask, pl.BlockSpec((rows_here, cols_here), lambda i: (0, 0))
    packed_shape = (BLOCKS, CORES, groups, cols_pad, 3 * LANES)
    flat_shape = (members, groups, cols_pad, 3 * LANES)
    pad_shape = (CORES, groups, PACK, cols_pad, channels)
    here_shape = (CORES, groups, PACK, cols_here, channels)

    def shape(s, d):
        return jax.ShapeDtypeStruct(s, d)

    index = row_at * col_devs + col_at
    devices = row_devs * col_devs
    all_bits = [2**k for k in range(16) if 2**k < devices]
    cube, outer_bits = all_bits[1:4], all_bits[4:]
    core_line = core.astype(jnp.int32).reshape(1)

    def bit(mask_bit):
        return (index // mask_bit) % 2

    def partner(x, flip):
        return lax.ppermute(x, AXES, [(d, d ^ flip) for d in range(devices)])


    orders = [[cube[(p + k) % 3] for k in range(3)] for p in range(3)]

    def bits(level):
        return jnp.stack([bit(o[level]) for o in orders]).astype(jnp.int32)

    def zipped(kept, got):
        return [x for pair in zip(kept, got) for x in pair]

    def merge(own, got, which, single, after):
        n, (r, c) = len(own), own[0].shape
        out = [shape((n, 2 * r, c), BF)] * 2 if single else [shape((2 * r, c), BF)] * (2 * n)
        return call(
            lambda *refs: merge_kernel(n, single, *refs), zipped(own, got), out, 2.0,
            after=after, prefetch=[which], vmem=34 if single else 12, name="merge",
        )

    class Sum:
        def __init__(self, kept, got):
            self.kept, self.got, self.level = kept, got, 0

        def send(self, arrays):
            self.got = [partner(x, o[self.level]) for x, o in zip(arrays, orders)]

        def halve(self, after=()):
            first, n = self.level == 0, len(orders)
            rows, wide = self.kept[0].shape
            half = rows // n if first else rows // 2
            tiles = 2 if first else 1
            t = half // tiles
            args, specs = [], []
            if first:
                for chunk in range(2 * n):
                    grad, at = divmod(chunk, n)
                    args += [self.kept[grad], self.got[grad]]
                    specs += [pl.BlockSpec((t, wide), lambda i, b, at=at: (at * tiles + i, 0))] * 2
            else:
                for p in range(n):
                    stay = lambda i, b, p=p: (b[p] * tiles + i, 0)
                    leave = lambda i, b, p=p: ((1 - b[p]) * tiles + i, 0)
                    args += [self.kept[p], self.got[p]] * 2
                    specs += [pl.BlockSpec((t, wide), m) for m in (stay, stay, leave, leave)]
            res = call(
                halve_first_kernel if first else halve_kernel,
                args, [shape((half, wide), BF)] * (2 * n), 3.0,
                after=after, prefetch=[bits(self.level)], grid=(tiles,), in_specs=specs,
                out_specs=[pl.BlockSpec((t, wide), lambda i, b: (i, 0))] * (2 * n), vmem=20 if first else 12, name="halve",
            )
            self.kept = res[0::2]
            self.send(res[1::2])
            self.level += 1
            return self.kept[0]

        def settle(self, after=()):
            n = len(orders)
            self.kept = call(
                lambda *refs: settle_kernel(n, *refs), zipped(self.kept, self.got),
                [shape(x.shape, BF) for x in self.kept], 1.0, after=after, name="settle",
            )
            return self.kept[0]

        def join(self, stay, got, after=()):
            n, (r, c) = len(orders), self.kept[0].shape
            self.kept, sent = call(
                lambda *refs: join_kernel(n, *refs), self.kept + [stay, got],
                [shape((n * (r + EXTRA), c), BF)] * 2, 1.5, after=after, name="join",
            )
            self.got = partner(sent, outer_bits[0])
            for m in outer_bits[1:]:
                self.kept, sent = add(self.kept, self.got, BF)
                self.got = partner(sent, m)
            return self.kept

        def part(self, after=()):
            n, (r, c) = len(orders), self.kept.shape
            res = call(
                part_kernel, [self.kept, self.got], [shape((r // n, c), BF)] * (2 * n), 1.5,
                after=after, name="part",
            )
            self.kept = res[:n]
            self.level = len(cube) - 1
            self.send(res[n:])
            return self.kept[0]

        def double(self, after=()):
            n, (r, c), single = len(orders), self.kept[0].shape, self.level == 0
            res = merge(self.kept, self.got, bits(self.level), single, after)
            self.level -= 1
            if not single:
                self.kept = res[:n]
                self.send(res[n:])
                return self.kept[0]
            self.kept, sent = (x.reshape(2 * n * r, c) for x in res)
            self.got = partner(sent, 1)
            return self.kept

        def widen(self, done, after=()):
            rows, c = self.kept.shape
            chunk = rows // (len(orders) * BLOCKS)
            t = 2 * (chunk - EXTRA)
            steps = rows // chunk // 4
            full_rows = CORES * steps * t
            x = self.got if done else self.kept
            full = [shape((full_rows, c), F32), shape((c, full_rows), F32)]
            extra = [shape((2 * steps, EXTRA, c), BF)] * 2
            at = lambda i, h: (1 - h[0] if done else h[0]) * steps + i
            return call(
                widen_kernel, [x, x] + done[:2], full + extra, 5.0, after=after,
                prefetch=[core_line], grid=(steps,),
                in_specs=[
                    pl.BlockSpec((2 * chunk, c), lambda i, h: (i, 0)),
                    pl.BlockSpec((2 * chunk, c), lambda i, h: (steps + i, 0)),
                ] + [pl.BlockSpec(memory_space=pl.ANY)] * len(done[:2]),
                out_specs=[
                    pl.BlockSpec((t, c), lambda i, h: (at(i, h), 0)),
                    pl.BlockSpec((c, t), lambda i, h: (0, at(i, h))),
                ] + [pl.BlockSpec((2, EXTRA, c), lambda i, h: (i, 0, 0))] * 2,
                input_output_aliases={3: 0, 4: 1} if done else {}, hbm=(0, 1), name="widen",
            )

    def add(x, y, dtype, after=()):
        return call(add_kernel, [x, y], [shape(x.shape, dtype)] * 2, 1.0, after=after, name="add")

    class Tail:
        def __init__(self, x):
            self.bits = list(all_bits)
            self.x, self.got = x[0], partner(x[1], self.bits[0])

        def step(self, after=()):
            self.x, sent = add(self.x, self.got, F32, after)
            self.bits.pop(0)
            if self.bits:
                self.got = partner(sent, self.bits[0])
            return self.x


    turned_shape = shape((cols_here, rows_here, channels), F32)
    turned_spec = pl.BlockSpec(turned_shape.shape, lambda i: (0, 0, 0))

    def turn_back(x):
        return x.swapaxes(0, 1)

    def lon_forward(cells, table, after=()):
        return call(
            lambda *refs: lon_kernel(col_devs, row_group, *refs),
            [cells.reshape(flat_shape), table],
            [shape((half_rows, lats, LANES), BF)] * 2, 5.5, after=after,
            scratch_shapes=[pltpu.VMEM((all_rows * lats, LANES), F32)],
            vmem=24, name="lon_forward",
        )

    def lon_backward(pieces, table, after=()):
        return call(
            lambda *refs: lon_back_kernel(
                col_devs, row_group, len(pieces), refs[len(pieces)], *refs[: len(pieces)], refs[-1]
            ),
            [*pieces, table], shape(flat_shape, BF), 3.5, after=after, vmem=16, name="lon_backward",
        )

    def big_weight(w):
        w = lax.dynamic_index_in_dim(w, mine, 1, keepdims=False)
        gap = LANES - block
        w = jnp.pad(w, ((0, 0), (0, gap), (0, gap)))
        return jnp.concatenate(
            [jnp.concatenate([w[0], w[1]], 1), jnp.concatenate([-w[1], w[0]], 1)], 0
        )

    def big_bias(b):
        b = lax.dynamic_index_in_dim(b.reshape(2, BLOCKS, block), mine, 1, keepdims=False)
        return jnp.pad(b, ((0, 0), (0, LANES - block))).reshape(1, 2 * LANES)

    wa, wb = big_weight(mix_weight_a), big_weight(mix_weight_b)
    ba, bb = big_bias(mix_bias_a), big_bias(mix_bias_b)

    normed, send = call(
        first_kernel, [x5, mask, first_gain, first_shift],
        [shape(pad_shape, BF), shape(packed_shape, BF)], 6.0, hbm=(0, 1),
        grid=(lat_steps,), in_specs=[here_spec, mask_spec, line_spec, line_spec],
        out_specs=[pad_spec, packed_spec], vmem=16, name="first_norm",
    )
    cells = exchange(send.reshape(flat_shape))

    own, other = lon_forward(cells, lon_fwd)
    other = swap(other)
    own, other, modes = call(
        mix_kernel, [own, other, lat_fwd, lat_inv, wa, ba, wb, bb],
        [shape((lats, half_rows, LANES), BF)] * 2
        + [shape((slots_pad // WIDE, WIDE * LAT, 2 * LANES), BF)], 22.0,
        scratch_shapes=[pltpu.VMEM((2 * lats * half_rows, LANES), F32)], vmem=32, hbm=(2,), name="mix",
    )
    other = swap(other)
    lon_out = lon_backward([own, other], lon_winv)
    got = exchange(lon_out)

    cot_pad = call(
        pad_kernel, [cot5], shape(pad_shape, BF), 2.0, after=[lon_out], grid=(lat_steps,),
        in_specs=[here_spec], out_specs=[pad_spec], name="pad",
    )

    resid, tokens = call(
        second_kernel,
        [x5, normed, mask, got.reshape(packed_shape), row(second_gain), row(second_shift)],
        [shape(pad_shape, F32), shape(pad_shape, BF)], 8.5, after=[cot_pad],
        grid=(lat_steps,),
        in_specs=[here_spec, pad_spec, mask_spec, packed_spec, row_spec, row_spec],
        out_specs=[pad_spec, pad_spec], vmem=40, pin=(0, 1), name="second_norm",
    )
    tokens2, cot2 = tokens.reshape(-1, channels), cot_pad.reshape(-1, channels)
    count, hidden = tokens2.shape[0], expand_weight.shape[1]
    tile = hidden // 6
    all_tok = pl.BlockSpec((count, channels), lambda i: (0, 0))
    by_col = lambda n: pl.BlockSpec((n, tile), lambda i: (0, i))
    by_row = pl.BlockSpec((tile, channels), lambda i: (i, 0))
    act, gpre, gtok, g_ebias = call(
        chain_kernel,
        [tokens2, cot2, expand_weight, row(expand_bias), reduce_weight],
        [
            shape((count, hidden), BF), shape((count, hidden), BF),
            shape((count, channels), BF), shape((1, hidden), F32),
        ],
        25.0, grid=(6,),
        in_specs=[all_tok, all_tok, by_col(channels), by_col(1), by_row],
        out_specs=[by_col(count), by_col(count), all_tok, by_col(1)], scratch_shapes=[pltpu.VMEM((count, channels), F32)], vmem=46, hbm=(0, 1, 2), pin=True, name="mlp_chain",
    )

    halves = 3
    assert halves * CORES * tile == hidden

    def weight_grad(left, right, own, after, name):
        at = lambda i, c: (c[0] if own else 1 - c[0]) * halves + i
        return call(
            weight_grad_kernel, [left, right],
            [shape((halves * tile, channels), BF), shape((8, LANES), F32)], 5.0,
            after=after, prefetch=[core_line], grid=(halves,),
            in_specs=[
                pl.BlockSpec((count, tile), lambda i, c: (0, at(i, c))),
                pl.BlockSpec((count, channels), lambda i, c: (0, 0)),
            ],
            out_specs=[
                pl.BlockSpec((tile, channels), lambda i, c: (i, 0)),
                pl.BlockSpec((8, LANES), lambda i, c: (0, 0)),
            ],
            vmem=20, name=name,
        )

    one_row = shape((1, channels), F32)
    grad_resid, send, g_gain2, g_shift2, g_rbias = call(
        third_kernel,
        [resid, gtok.reshape(pad_shape), cot_pad, mask, row(second_gain)],
        [shape(pad_shape, BF), shape(packed_shape, BF)] + [one_row] * 3, 9.0,
        grid=(lat_steps,), in_specs=[pad_spec, pad_spec, pad_spec, mask_spec, row_spec],
        out_specs=[pad_spec, packed_spec, row_spec, row_spec, row_spec], vmem=56, name="second_back",
    )
    cells = exchange(send.reshape(flat_shape))

    sent_r, token = weight_grad(act, cot2, False, [g_gain2], "reduce_grad")
    sent_e, token = weight_grad(gpre, tokens2, False, [token], "expand_grad")
    kept_r, token = weight_grad(act, cot2, True, [token], "reduce_grad")
    kept_e, token = weight_grad(gpre, tokens2, True, [token], "expand_grad")
    sums = Sum([kept_r, kept_e], [partner(sent_r, 1), partner(sent_e, 1)])

    own, other = lon_forward(cells, lon_wfwd, after=[token])
    other = swap(other)
    token = sums.halve(after=[own])
    run = half_rows // SPLIT
    pieces, grads = [], []
    grad_shape = shape((4 * LANES + 16, 2 * LANES), F32)
    for k in range(SPLIT):
        here = pl.BlockSpec((run, lats, LANES), lambda i, k=k: (k, 0, 0))
        steps = modes.shape[0] // SPLIT
        const = lambda x: pl.BlockSpec(x.shape, lambda i: (0, 0))
        o, t, g = call(
            mix_back_kernel, [own, other, modes, lat_fwd, lat_inv, wa, ba, wb, bb] + grads,
            [shape((lats, run, LANES), BF)] * 2 + [grad_shape], 13.0,
            after=[token],
            in_specs=[
                here, here, pl.BlockSpec((steps,) + modes.shape[1:], lambda i, k=k: (k, 0, 0)),
            ] + [const(x) for x in (lat_fwd, lat_inv, wa, ba, wb, bb, *grads)],
            scratch_shapes=[pltpu.VMEM((2 * lats * run, LANES), F32)], vmem=34, name="mix_back",
        )
        pieces.append((o, swap(t)))
        grads = [g]
        token = sums.halve(after=[o])
    token = sums.halve(after=[token])
    token = sums.settle(after=[token])
    send = lon_backward(
        [p[0] for p in pieces] + [p[1] for p in pieces], lon_inv, after=[token]
    )
    got = exchange(send)
    stay, leave = call(
        lambda *refs: collect_kernel(block, *refs), grads,
        [shape((3 * EXTRA, channels), F32)] * 2, 1.5, after=[send], prefetch=[core_line],
        name="collect",
    )
    token = sums.join(stay, partner(leave, 1))

    outputs, token = call(
        branch_kernel,
        [act.reshape(CORES, groups, PACK, cols_pad, hidden), reduce_weight, resid, row(reduce_bias)],
        [turned_shape, shape((8, LANES), F32)], 10.0, after=[token], grid=(groups,),
        in_specs=[
            both_spec(cols_pad, hidden), pl.BlockSpec((hidden, channels), lambda i: (0, 0)),
            both_spec(cols_pad, channels), row_spec,
        ],
        out_specs=[turned_spec, pl.BlockSpec((8, LANES), lambda i: (0, 0))], vmem=32, name="branch",
    )

    touched = call(
        touch_kernel, [], shape((8, LANES), F32), 0.5, after=[got, token], name="touch"
    )
    token = sums.part(after=[touched])
    token = sums.double(after=[token])
    token = sums.double(after=[token])

    grad_inputs, g_gain1, g_shift1 = call(
        last_kernel, [x5, grad_resid, mask, got.reshape(packed_shape), row(first_gain)],
        [turned_shape] + [one_row] * 2, 9.0, after=[token],
        grid=(lat_steps,), in_specs=[here_spec, pad_spec, mask_spec, packed_spec, row_spec],
        out_specs=[turned_spec, row_spec, row_spec], vmem=36, pin=(0, 1), name="first_back",
    )
    tail_sum = Tail(
        call(
            tail_kernel, [g_gain1, g_shift1, g_gain2, g_shift2, g_rbias, g_ebias],
            [shape((1, 5 * channels + hidden), F32)] * 2, 1.0, name="tail",
        )
    )
    token = tail_sum.step()
    token = sums.double(after=[token])
    token = tail_sum.step(after=[token])
    own_done = sums.widen([], after=[token])
    token = tail_sum.step(after=[own_done[2]])
    g_reduce, g_expand, *got_extra = sums.widen(own_done, after=[token])
    token = got_extra[0]
    while tail_sum.bits:
        token = tail_sum.step(after=[token])
    weight_out, bias_out = shape(mix_weight_a.shape, F32), shape(mix_bias_a.shape, F32)
    g_wa, g_wb, g_ba, g_bb = call(
        lambda *refs: spread_kernel(block, *refs), own_done[2:] + got_extra,
        [weight_out, weight_out, bias_out, bias_out], 3.0, prefetch=[core_line], name="spread",
    )

    tail = tail_sum.x
    g_gain1, g_shift1, g_gain2, g_shift2, g_rbias = (
        tail[0, k * channels : (k + 1) * channels] for k in range(5)
    )
    g_ebias = tail[0, 5 * channels :]

    def flat(v):
        return v.reshape(-1)

    return (
        turn_back(outputs), turn_back(grad_inputs),
        flat(g_gain1), flat(g_shift1), g_wa, g_ba, g_wb, g_bb, flat(g_gain2), flat(g_shift2),
        g_expand, g_ebias, g_reduce, flat(g_rbias),
    )


def solution(mesh):
    grid = P("rows", "cols", None)
    placed = (grid, P("rows", "cols"), grid) + (P(),) * 12
    return jax.shard_map(
        per_device,
        mesh=mesh,
        in_specs=placed,
        out_specs=(grid, grid) + (P(),) * 12,
        check_vma=False,
    )
```

```python
import math

import jax
import jax.numpy as jnp
import numpy as np
from jax import lax
from jax.experimental import pallas as pl
from jax.experimental.pallas import tpu as pltpu
from jax.sharding import PartitionSpec as P

BLOCKS = 8
LAT = 96
CORES = 2
PACK = 4
LANES = 128

shrink_level = 0.01
shrink_soft = 0.1
norm_eps = 1e-05
gelu_root = math.sqrt(2.0 / math.pi)
gelu_cube = 0.044715

BF = jnp.bfloat16
F32 = jnp.float32
AXES = ("rows", "cols")


def up_to(value, step):
    return (value + step - 1) // step * step


def call(kernel, args, out_shape, us, after=(), in_specs=None, prefetch=(), vmem=12, hbm=(), pin=False, **kw):
    outs = out_shape if isinstance(out_shape, (list, tuple)) else [out_shape]
    lead, n_in, n_after = len(prefetch), len(args), len(after)

    def body(*refs):
        kernel(*refs[: lead + n_in], *refs[lead + n_in + n_after :])

    if pin:
        at = range(len(args)) if pin is True else pin
        args = [
            pltpu.with_memory_space_constraint(x, pltpu.HBM) if k in at else x
            for k, x in enumerate(args)
        ]
    grid = kw.pop("grid", (1,))
    whole = lambda x: pl.BlockSpec(x.shape, lambda *_, n=len(x.shape): (0,) * n)
    specs = list(in_specs) if in_specs is not None else [whole(a) for a in args]
    specs += [pl.BlockSpec(memory_space=pl.ANY)] * n_after
    out_specs = kw.pop("out_specs", None) or [whole(o) for o in outs]
    got = pl.pallas_call(
        body,
        grid_spec=pltpu.PrefetchScalarGridSpec(
            num_scalar_prefetch=lead,
            grid=grid,
            in_specs=specs,
            out_specs=out_specs,
            scratch_shapes=kw.pop("scratch_shapes", ()),
        ),
        out_shape=[pltpu.HBM(o.shape, o.dtype) if k in hbm else o for k, o in enumerate(outs)],
        compiler_params=pltpu.CompilerParams(vmem_limit_bytes=vmem * 1024 * 1024),
        cost_estimate=pl.CostEstimate(
            flops=0, bytes_accessed=int(us * 1e5), transcendentals=0
        ),
        **kw,
    )(*prefetch, *args, *after)
    return list(got) if isinstance(out_shape, (list, tuple)) else got[0]


SPLIT = 1
UNROLL = 1
WIDE = 12


def lon_table(lon_size, col_devs, cols_here, cols_pad, slots, slots_pad):
    modes = lon_size // 2 + 1
    table = np.zeros((CORES, 2, slots_pad, col_devs, cols_pad), np.float64)
    weights = np.zeros((CORES, slots_pad), np.float64)
    place = np.arange(lon_size).reshape(col_devs, cols_here)
    for half in range(CORES):
        for slot in range(slots):
            mode = half * slots + slot
            if mode >= modes:
                continue
            angle = (place * mode % lon_size) * (2.0 * math.pi / lon_size)
            table[half, 0, slot, :, :cols_here] = np.cos(angle) / math.sqrt(lon_size)
            edge = mode == 0 or 2 * mode == lon_size
            if not edge:
                table[half, 1, slot, :, :cols_here] = np.sin(angle) / math.sqrt(lon_size)
            weights[half, slot] = 1.0 if edge else 2.0
    weighted = table * weights[:, None, :, None, None]
    rows = 2 * slots_pad
    flat = [
        a.reshape(CORES, 2, SPLIT, slots_pad // SPLIT, col_devs, cols_pad)
        .swapaxes(1, 2)
        .reshape(CORES, rows, col_devs * cols_pad)
        for a in (table, weighted)
    ]
    return [
        np.stack([np.concatenate([a[h], a[1 - h]], 0) for h in range(CORES)]) for a in flat
    ]


def lat_table(rows_here, row_group):
    share = rows_here // CORES
    out = []
    for h in range(CORES):
        own = [
            rows_here * r + share * h + i for r in range(row_group) for i in range(share)
        ]
        other = [
            rows_here * r + share * (1 - h) + i for r in range(row_group) for i in range(share)
        ]
        angle = np.outer(np.arange(LAT), np.array(own + other)) % LAT * (2.0 * math.pi / LAT)
        cos, sin = np.cos(angle) / math.sqrt(LAT), np.sin(angle) / math.sqrt(LAT)
        out.append(np.block([[cos, -sin], [-sin, -cos]]))
    return np.stack(out)


def pack_lanes(tiles):
    a, b, c, d = tiles
    lane = lax.broadcasted_iota(jnp.int32, a.shape, a.ndim - 1)
    axis = a.ndim - 1
    b, c, d = pltpu.roll(b, 96, axis), pltpu.roll(c, 64, axis), pltpu.roll(d, 32, axis)
    return [
        jnp.where(lane < 96, a, b),
        jnp.where(lane < 64, b, c),
        jnp.where(lane < 32, c, d),
    ]


def unpack_lanes(tiles):
    a, b, c = tiles
    lane = lax.broadcasted_iota(jnp.int32, a.shape, a.ndim - 1)
    axis = a.ndim - 1
    return [
        a,
        pltpu.roll(jnp.where(lane >= 96, a, b), 32, axis),
        pltpu.roll(jnp.where(lane >= 64, b, c), 64, axis),
        pltpu.roll(c, 96, axis),
    ]


def tiles_of(value):
    return [value[:, LANES * i : LANES * (i + 1)] for i in range(value.shape[1] // LANES)]


def split_blocks(value):
    tiles = tiles_of(value)
    out = []
    for i in range(0, len(tiles), 3):
        out += unpack_lanes(tiles[i : i + 3])
    return out


def join_blocks(tiles):
    out = []
    for i in range(0, len(tiles), 4):
        out += pack_lanes(tiles[i : i + 4])
    return jnp.concatenate(out, axis=1)


def pad_rows(value, rows):
    return jnp.concatenate(
        [value, jnp.zeros((rows - value.shape[0], value.shape[1]), value.dtype)], axis=0
    )


def store_packed(ref, half, per_lat):
    split = [split_blocks(v) for v in per_lat]
    for q in range(BLOCKS):
        packed = pack_lanes([split[j][q] for j in range(PACK)])
        ref[q, half, 0] = jnp.concatenate(packed, axis=1).astype(ref.dtype)


def load_packed(ref, half):
    by_lat = [[] for _ in range(PACK)]
    for q in range(BLOCKS):
        parts = unpack_lanes(tiles_of(ref[q, half, 0].astype(F32)))
        for j in range(PACK):
            by_lat[j].append(parts[j])
    return [join_blocks(tiles) for tiles in by_lat]


def stats(x):
    average = jnp.mean(x, axis=-1, keepdims=True)
    centred = x - average
    spread = jnp.mean(centred * centred, axis=-1, keepdims=True)
    inv = lax.rsqrt(spread + norm_eps)
    return centred * inv, inv


def norm_back(grad, xhat, inv, gain):
    scaled = grad * gain
    m1 = jnp.mean(scaled, axis=-1, keepdims=True)
    m2 = jnp.mean(scaled * xhat, axis=-1, keepdims=True)
    return inv * (scaled - m1 - xhat * m2)


def mask_column(mask_ref, lat, rows):
    line = mask_ref[pl.ds(lat, 1), :].astype(F32)
    shape = (rows, line.shape[1])
    row, col = (lax.broadcasted_iota(jnp.int32, shape, k) for k in range(2))
    return jnp.sum(jnp.where(row == col, line, 0.0), axis=1, keepdims=True)


def first_kernel(x_ref, mask_ref, gain_ref, shift_ref, normed_ref, out_ref):
    rows = normed_ref.shape[3]
    half, first = 0, pl.program_id(0) * PACK
    lats = []
    for j in range(PACK):
        x = pad_rows(x_ref[half, 0, j].astype(F32), rows)
        xhat, _ = stats(x)
        y = mask_column(mask_ref, first + j, rows) * (xhat * gain_ref[...][None] + shift_ref[...][None])
        normed_ref[half, 0, j] = y.astype(BF)
        lats.append(y)
    store_packed(out_ref, half, lats)


def pad_kernel(x_ref, out_ref):
    rows = out_ref.shape[3]
    for j in range(PACK):
        out_ref[0, 0, j] = pad_rows(x_ref[0, 0, j].astype(F32), rows).astype(BF)


def second_kernel(
    x_ref, normed_ref, mask_ref, got_ref, gain_ref, shift_ref, resid_ref, tok_ref
):
    rows = normed_ref.shape[3]
    half, first = 0, pl.program_id(0) * PACK
    spatial = load_packed(got_ref, half)
    for j in range(PACK):
        x = pad_rows(x_ref[half, 0, j].astype(F32), rows)
        resid = x + normed_ref[half, 0, j].astype(F32)
        resid = resid + mask_column(mask_ref, first + j, rows) * spatial[j]
        resid_ref[half, 0, j] = resid
        xhat, _ = stats(resid)
        tok_ref[half, 0, j] = (xhat * gain_ref[...] + shift_ref[...]).astype(BF)


def third_kernel(
    resid_ref, gtok_ref, cot_ref, mask_ref, gain_ref,
    gresid_ref, send_ref, ggain_ref, gshift_ref, gbias_ref,
):
    @pl.when(pl.program_id(0) == 0)
    def _():
        ggain_ref[...] = jnp.zeros_like(ggain_ref)
        gshift_ref[...] = jnp.zeros_like(gshift_ref)
        gbias_ref[...] = jnp.zeros_like(gbias_ref)

    half, first = 0, pl.program_id(0) * PACK
    lats = []
    for j in range(PACK):
        xhat, inv = stats(resid_ref[half, 0, j])
        gtok = gtok_ref[half, 0, j].astype(F32)
        cot = cot_ref[half, 0, j].astype(F32)
        ggain_ref[...] += jnp.sum(gtok * xhat, axis=0, keepdims=True)
        gshift_ref[...] += jnp.sum(gtok, axis=0, keepdims=True)
        gbias_ref[...] += jnp.sum(cot, axis=0, keepdims=True)
        gres = cot + norm_back(gtok, xhat, inv, gain_ref[...])
        gresid_ref[half, 0, j] = gres.astype(gresid_ref.dtype)
        lats.append(mask_column(mask_ref, first + j, gres.shape[0]) * gres)
    store_packed(send_ref, half, lats)


def store_lat(out_ref, lat, value):
    out_ref[:, lat, :] = value[: out_ref.shape[0]]


def last_kernel(
    x_ref, gresid_ref, mask_ref, got_ref, gain_ref, out_ref, ggain_ref, gshift_ref
):
    @pl.when(pl.program_id(0) == 0)
    def _():
        ggain_ref[...] = jnp.zeros_like(ggain_ref)
        gshift_ref[...] = jnp.zeros_like(gshift_ref)

    rows = gresid_ref.shape[3]
    half, first = 0, pl.program_id(0) * PACK
    got = load_packed(got_ref, half)
    for j in range(PACK):
        x = pad_rows(x_ref[half, 0, j].astype(F32), rows)
        xhat, inv = stats(x)
        gres = gresid_ref[half, 0, j].astype(F32)
        grad = mask_column(mask_ref, first + j, rows) * (gres + got[j])
        ggain_ref[...] += jnp.sum(grad * xhat, axis=0, keepdims=True)
        gshift_ref[...] += jnp.sum(grad, axis=0, keepdims=True)
        store_lat(out_ref, first + j, gres + norm_back(grad, xhat, inv, gain_ref[...]))


OUTER = (((0,), (0,)), ((), ()))
ACROSS = (((1,), (1,)), ((), ()))


def chain_kernel(
    tok_ref, cot_ref, up_ref, bias_ref, down_ref, act_ref, gpre_ref, gtok_ref, gbias_ref, sum_ref
):
    @pl.when(pl.program_id(0) == 0)
    def _():
        sum_ref[...] = jnp.zeros_like(sum_ref)

    pre = jnp.dot(tok_ref[...], up_ref[...], preferred_element_type=F32) + bias_ref[...]
    gate = gelu_gate(pre)
    act_ref[...] = (pre * gate).astype(BF)
    gact = lax.dot_general(cot_ref[...], down_ref[...], ACROSS, preferred_element_type=F32)
    gpre = gelu_slope(pre, gate) * gact
    gbias_ref[...] = jnp.sum(gpre, axis=0, keepdims=True)
    gpre = gpre.astype(BF)
    gpre_ref[...] = gpre
    sum_ref[...] += lax.dot_general(gpre, up_ref[...], ACROSS, preferred_element_type=F32)

    @pl.when(pl.program_id(0) == pl.num_programs(0) - 1)
    def _():
        gtok_ref[...] = sum_ref[...].astype(gtok_ref.dtype)


def weight_grad_kernel(core_ref, left_ref, right_ref, out_ref, token_ref):
    token_ref[...] = jnp.zeros_like(token_ref)
    out_ref[...] = lax.dot_general(
        left_ref[...], right_ref[...], OUTER, preferred_element_type=F32
    ).astype(BF)


def branch_kernel(act_ref, down_ref, resid_ref, bias_ref, out_ref, token_ref):
    token_ref[...] = jnp.zeros_like(token_ref)
    cols = resid_ref.shape[3]
    rows = CORES * PACK * cols
    act = act_ref[...].reshape(rows, act_ref.shape[-1])
    branch = jnp.dot(act, down_ref[...], preferred_element_type=F32) + bias_ref[...]
    for half in range(CORES):
        for j in range(PACK):
            at = (half * PACK + j) * cols
            lat = (half * pl.num_programs(0) + pl.program_id(0)) * PACK + j
            store_lat(out_ref, lat, resid_ref[half, 0, j] + branch[at : at + cols])


def plus(left, right):
    return (left.astype(F32) + right.astype(F32)).astype(BF)


def halve_first_kernel(bits_ref, *refs):
    count = len(refs) // 6
    for p in range(count):
        a, b, c, d = refs[4 * p : 4 * p + 4]
        low, high = plus(a[...], b[...]), plus(c[...], d[...])
        first = bits_ref[p] == 0
        refs[4 * count + 2 * p][...] = jnp.where(first, low, high)
        refs[4 * count + 2 * p + 1][...] = jnp.where(first, high, low)


def halve_kernel(bits_ref, *refs):
    count = len(refs) // 6
    for k in range(2 * count):
        refs[4 * count + k][...] = plus(refs[2 * k][...], refs[2 * k + 1][...])


def join_kernel(count, *refs):
    stay, got = refs[count : count + 2]
    for p in range(count):
        n, m = refs[p].shape[0], stay.shape[0] // count
        value = refs[p][...]
        rows = slice(p * m, (p + 1) * m)
        extra = (stay[rows] + got[rows]).astype(BF)
        for out in refs[-2:]:
            out[p * (n + m) : p * (n + m) + n] = value
            out[p * (n + m) + n : (p + 1) * (n + m)] = extra


def settle_kernel(count, *refs):
    for p in range(count):
        refs[2 * count + p][...] = plus(refs[2 * p][...], refs[2 * p + 1][...])


def touch_kernel(out):
    out[...] = jnp.zeros_like(out)


def part_kernel(kept, got, *outs):
    n, count = outs[0].shape[0], len(outs) // 2
    for p in range(count):
        rows = slice(p * n, (p + 1) * n)
        value = plus(kept[rows], got[rows])
        outs[p][...] = value
        outs[count + p][...] = value


def add_kernel(left, right, *outs):
    value = left[...].astype(F32) + right[...].astype(F32)
    for out in outs:
        out[...] = value.astype(out.dtype)


def tail_kernel(*refs):
    for out in refs[-2:]:
        at = 0
        for ref in refs[:-2]:
            out[:, at : at + ref.shape[1]] = ref[...]
            at += ref.shape[1]


def merge_kernel(count, single, bits_ref, *refs):
    outs = refs[2 * count :]
    for p in range(count):
        own, got = refs[2 * p], refs[2 * p + 1]
        n = own.shape[0]
        for out in (outs[p::count] if not single else [o.at[p] for o in outs]):
            out[pl.ds(pl.multiple_of(bits_ref[p] * n, 16), n), :] = own[...]
            out[pl.ds(pl.multiple_of((1 - bits_ref[p]) * n, 16), n), :] = got[...]


def widen_kernel(core_ref, reduce_ref, expand_ref, *refs):
    reduce_out, expand_out, extra_r, extra_e = refs[-4:]
    n = reduce_out.shape[0] // 2
    for k in range(2):
        at = k * (n + EXTRA)
        reduce_out[k * n : (k + 1) * n] = reduce_ref[at : at + n].astype(F32)
        expand_out[:, k * n : (k + 1) * n] = expand_ref[at : at + n].astype(F32).T
        extra_r[k] = reduce_ref[at + n : at + n + EXTRA]
        extra_e[k] = expand_ref[at + n : at + n + EXTRA]


EXTRA = 16


def collect_kernel(block, core_ref, grad_ref, *refs):
    wide = 2 * LANES
    halves, lines = [], []
    for i in range(2):
        g = grad_ref[i * wide : (i + 1) * wide]
        at = 2 * wide + 8 * i
        line = jnp.sum(grad_ref[at : at + 8], axis=0, keepdims=True)
        top, low = g[:block], g[LANES : LANES + block]
        halves.append([top[:, :LANES] + low[:, LANES:], top[:, LANES:] - low[:, :LANES]])
        lines += [line[:, :LANES], line[:, LANES:]]
    rows = lax.broadcasted_iota(jnp.int32, (EXTRA, LANES), 0)
    bias = sum(jnp.where(rows == k, line, 0.0) for k, line in enumerate(lines))
    first = core_ref[0] == 0
    for k, out in enumerate(refs[-2:]):
        own = first if k == 0 else jnp.logical_not(first)
        out[...] = jnp.zeros_like(out)
        for p in range(2):
            value = jnp.where(own, halves[0][p], halves[1][p])
            for t in range(block // EXTRA):
                at = slice(t * LANES, (t + 1) * LANES)
                out[p * EXTRA : (p + 1) * EXTRA, at] = value[t * EXTRA : (t + 1) * EXTRA]
        out[2 * EXTRA : 3 * EXTRA, :LANES] = jnp.where(own, bias, 0.0)


def spread_kernel(block, core_ref, *refs):
    own, got = refs[:2], refs[2:4]
    wa_ref, wb_ref, ba_ref, bb_ref = refs[4:]
    first = core_ref[0] == 0
    per = own[0].shape[0]
    biases = [[] for _ in range(4)]
    for q in range(BLOCKS):
        for half in range(CORES):
            for p in range(3):
                if half == 1 and p == 2:
                    continue
                k = sum(((q >> ((p + j) % 3)) & 1) << (2 - j) for j in range(3))
                at = p * BLOCKS + k
                mine, other = (r[at // per][at % per].astype(F32) for r in (own, got))
                value = jnp.where(first, mine, other) if half == 0 else jnp.where(first, other, mine)
                if p == 2:
                    for i in range(4):
                        biases[i].append(value[i : i + 1, :LANES])
                    continue
                out = wb_ref if half else wa_ref
                for t in range(block // EXTRA):
                    out[p, q, t * EXTRA : (t + 1) * EXTRA, :] = value[
                        :, t * LANES : t * LANES + block
                    ]
    for i in range(4):
        (bb_ref if i > 1 else ba_ref)[i % 2 : i % 2 + 1, :] = join_blocks(biases[i])


def lon_kernel(col_devs, row_group, x_ref, table_ref, own_ref, other_ref, turn_ref):
    groups = x_ref.shape[1]
    rows = table_ref.shape[0]
    lats = own_ref.shape[1]
    slots = own_ref.shape[0]
    for r in range(row_group):
        for g in range(groups):
            cells = jnp.concatenate(
                [x_ref[r * col_devs + c, g] for c in range(col_devs)], axis=0
            )
            modes = jnp.dot(table_ref[...], cells, preferred_element_type=F32)
            for j, tile in enumerate(unpack_lanes(tiles_of(modes))):
                at = (r * groups + g) * PACK + j
                turn_ref[pl.ds(at, rows, stride=lats), :] = tile

    @pl.loop(0, slots, unroll=4)
    def _(s):
        own_ref[s] = turn_ref[pl.ds(pl.multiple_of(s * lats, 8), lats), :].astype(BF)
        other_ref[s] = turn_ref[
            pl.ds(pl.multiple_of((s + slots) * lats, 8), lats), :
        ].astype(BF)


def lon_back_kernel(col_devs, row_group, pieces, table_ref, *refs):
    out_ref = refs[pieces]
    groups = out_ref.shape[1]
    cols = out_ref.shape[2]
    for r in range(row_group):
        for g in range(groups):
            tiles = []
            for j in range(0, PACK, 2):
                pair = []
                for k in range(2):
                    at = (r * groups + g) * PACK + j + k
                    pair.append(jnp.concatenate([r_[at] for r_ in refs[:pieces]], axis=0))
                cells = jnp.dot(
                    table_ref[...], jnp.concatenate(pair, axis=1), preferred_element_type=F32
                )
                tiles += tiles_of(cells)
            packed = jnp.concatenate(pack_lanes(tiles), axis=1).astype(BF)
            for c in range(col_devs):
                out_ref[r * col_devs + c, g] = packed[c * cols : (c + 1) * cols]


def gelu_gate(v):
    inner = v * (gelu_root * gelu_cube * (v * v) + gelu_root)
    return 0.5 * jnp.tanh(inner) + 0.5


def gelu_slope(v, gate):
    inner = 6.0 * gelu_root * gelu_cube * (v * v) + 2.0 * gelu_root
    return gate + (v * gate) * (1.0 - gate) * inner


def slots_down(real, imag):
    return [
        jnp.concatenate([v[:, k * LANES : (k + 1) * LANES] for v in (real, imag)], axis=1)
        for k in range(WIDE)
    ]


def slots_across(value):
    rows = [value[k * LAT : (k + 1) * LAT] for k in range(WIDE)]
    parts = [
        jnp.concatenate([r[:, p * LANES : (p + 1) * LANES] for r in rows], axis=1)
        for p in range(2)
    ]
    return jnp.concatenate(parts, axis=0)


def latitudes(own_ref, other_ref, row, run):
    return jnp.concatenate(
        [own_ref[row], other_ref[row], own_ref[row + run], other_ref[row + run]], axis=0
    )


def turn_out(turn_ref, value, row, lats, rows, run):
    for part in range(2):
        for dest in range(2):
            piece = value[(2 * part + dest) * lats : (2 * part + dest + 1) * lats]
            start = dest * lats * rows + part * run + row
            turn_ref[pl.ds(start, lats, stride=rows), :] = piece


def drain(turn_ref, own_ref, other_ref):
    lats, rows = own_ref.shape[0], own_ref.shape[1]

    @pl.loop(0, lats, unroll=4)
    def _(at):
        own_ref[at] = turn_ref[pl.ds(pl.multiple_of(at * rows, 8), rows), :].astype(BF)
        other_ref[at] = turn_ref[
            pl.ds(pl.multiple_of((at + lats) * rows, 8), rows), :
        ].astype(BF)


def mix_kernel(
    own_ref, other_ref, lat_ref, back_ref, wa_ref, ba_ref, wb_ref, bb_ref,
    own_out, other_out, modes_out, turn_ref,
):
    lats, rows = own_ref.shape[1], own_ref.shape[0]
    run = rows // 2 // SPLIT

    @pl.loop(0, rows // 2 // WIDE, unroll=UNROLL)
    def _(step):
        slot = WIDE * step
        row = slot + slot // run * run
        cells = jnp.concatenate(
            [latitudes(own_ref, other_ref, row + k, run) for k in range(WIDE)], axis=1
        )
        full = jnp.dot(lat_ref[...], cells, preferred_element_type=F32).astype(BF)
        real, imag = full[:LAT], full[LAT:]
        modes = jnp.concatenate(slots_down(real, imag), axis=0)
        modes_out[step] = modes
        pre_a = jnp.dot(modes, wa_ref[...], preferred_element_type=F32) + ba_ref[...]
        hidden = (pre_a * gelu_gate(pre_a)).astype(BF)
        pre_b = jnp.dot(hidden, wb_ref[...], preferred_element_type=F32) + bb_ref[...]
        shrunk = (pre_b - shrink_level * jnp.tanh(pre_b * (1.0 / shrink_soft))).astype(BF)
        mixed = slots_across(shrunk)
        back = jnp.dot(back_ref[...], mixed, preferred_element_type=F32)
        for k in range(WIDE):
            turn_out(turn_ref, back[:, k * LANES : (k + 1) * LANES], row + k, lats, rows, run)

    drain(turn_ref, own_out, other_out)


def row_sums(value):
    return jnp.sum(value.reshape(-1, 8, value.shape[1]), axis=0)


def mix_back_kernel(
    own_ref, other_ref, modes_ref, lat_ref, back_ref, wa_ref, ba_ref, wb_ref, bb_ref,
    *refs,
):
    own_out, other_out, grad_ref, turn_ref = refs[-4:]
    lats, rows = own_ref.shape[1], own_ref.shape[0]
    run = rows // 2
    grad_ref[...] = refs[0][...] if len(refs) > 4 else jnp.zeros_like(grad_ref)
    wide = wa_ref.shape[0]
    gwa_ref, gwb_ref = grad_ref.at[:wide], grad_ref.at[wide : 2 * wide]
    gba_ref, gbb_ref = grad_ref.at[2 * wide : 2 * wide + 8], grad_ref.at[2 * wide + 8 :]

    @pl.loop(0, run // WIDE, unroll=UNROLL)
    def _(step):
        row = WIDE * step
        cells = jnp.concatenate(
            [latitudes(own_ref, other_ref, row + k, run) for k in range(WIDE)], axis=1
        )
        full = jnp.dot(lat_ref[...], cells, preferred_element_type=F32)
        real, imag = full[:LAT], full[LAT:]
        grad = jnp.concatenate(slots_down(real, imag), axis=0)
        modes = modes_ref[step]
        pre_a = jnp.dot(modes, wa_ref[...], preferred_element_type=F32) + ba_ref[...]
        gate_a = gelu_gate(pre_a)
        hidden = (pre_a * gate_a).astype(BF)
        pre_b = jnp.dot(hidden, wb_ref[...], preferred_element_type=F32) + bb_ref[...]
        squash_b = jnp.tanh(pre_b * (1.0 / shrink_soft))
        level = shrink_level / shrink_soft
        factor = level * (squash_b * squash_b) + (1.0 - level)
        grad_b = factor * grad
        gbb_ref[...] += row_sums(grad_b)
        grad_b = grad_b.astype(BF)
        grad_hidden = lax.dot_general(grad_b, wb_ref[...], ACROSS, preferred_element_type=F32)
        gwb_ref[...] += lax.dot_general(hidden, grad_b, OUTER, preferred_element_type=F32)
        grad_a = gelu_slope(pre_a, gate_a) * grad_hidden
        gba_ref[...] += row_sums(grad_a)
        grad_a = grad_a.astype(BF)
        grad_modes = lax.dot_general(
            grad_a, wa_ref[...], ACROSS, preferred_element_type=F32
        ).astype(BF)
        gwa_ref[...] += lax.dot_general(modes, grad_a, OUTER, preferred_element_type=F32)
        mixed = slots_across(grad_modes)
        back = jnp.dot(back_ref[...], mixed, preferred_element_type=F32)
        for k in range(WIDE):
            turn_out(turn_ref, back[:, k * LANES : (k + 1) * LANES], row + k, lats, rows, run)

    drain(turn_ref, own_out, other_out)


def per_device(
    inputs, valid_mask, cotangent, first_gain, first_shift, mix_weight_a, mix_bias_a,
    mix_weight_b, mix_bias_b, second_gain, second_shift, expand_weight, expand_bias,
    reduce_weight, reduce_bias,
):
    row_devs = lax.axis_size("rows")
    col_devs = lax.axis_size("cols")
    rows_here, cols_here, channels = inputs.shape
    block = channels // BLOCKS
    lon_size = cols_here * col_devs
    cols_pad = up_to(cols_here, 16)
    row_group = LAT // rows_here
    members = row_group * col_devs
    share = rows_here // CORES
    groups = share // PACK
    slots = (lon_size // 2 + 2) // 2
    slots_pad = up_to(slots, 16)
    lats = share * row_group
    half_rows = 2 * slots_pad
    all_rows = CORES * half_rows
    assert members == CORES * BLOCKS and block * PACK == 3 * LANES
    assert col_devs * cols_pad == all_rows and CORES * lats == LAT

    row_at, col_at = lax.axis_index("rows"), lax.axis_index("cols")
    core = col_at % CORES
    mine = (row_at % row_group) * (col_devs // CORES) + col_at // CORES

    def pick(table):
        return lax.dynamic_index_in_dim(jnp.asarray(table, BF), core, 0, keepdims=False)

    plain_np, weighted_np = lon_table(
        lon_size, col_devs, cols_here, cols_pad, slots, slots_pad
    )
    lat_np = lat_table(rows_here, row_group)
    lon_fwd, lon_wfwd = pick(plain_np), pick(weighted_np)
    lon_inv, lon_winv = (
        pick(np.swapaxes(plain_np, 1, 2)), pick(np.swapaxes(weighted_np, 1, 2))
    )
    lat_fwd, lat_inv = pick(lat_np), pick(np.swapaxes(lat_np, 1, 2))

    snap_groups = [
        [(s * row_group + r) * col_devs + c for r in range(row_group) for c in range(col_devs)]
        for s in range(row_devs // row_group)
    ]
    core_pairs = [
        (r * col_devs + c, r * col_devs + c ^ 1) for r in range(row_devs) for c in range(col_devs)
    ]

    def exchange(x):
        return lax.all_to_all(x, AXES, 0, 0, axis_index_groups=snap_groups, tiled=True)

    def swap(x):
        return lax.ppermute(x, AXES, core_pairs)

    def fold(x):
        return x.reshape((CORES, groups, PACK) + x.shape[1:])

    def row(v):
        return v.reshape(1, -1)

    x5, cot5 = fold(inputs), fold(cotangent)

    def lat_spec(cols, width):
        return pl.BlockSpec(
            (1, 1, PACK, cols, width), lambda i: (i // groups, i % groups, 0, 0, 0)
        )

    def both_spec(cols, width):
        return pl.BlockSpec((CORES, 1, PACK, cols, width), lambda i: (0, i, 0, 0, 0))

    packed_spec = pl.BlockSpec(
        (BLOCKS, 1, 1, cols_pad, 3 * LANES), lambda i: (0, i // groups, i % groups, 0, 0)
    )
    lat_steps = CORES * groups
    row_spec = pl.BlockSpec((1, channels), lambda i: (0, 0))
    line_spec = pl.BlockSpec((channels,), lambda i: (0,))
    here_spec, pad_spec = lat_spec(cols_here, channels), lat_spec(cols_pad, channels)
    mask, mask_spec = valid_mask, pl.BlockSpec((rows_here, cols_here), lambda i: (0, 0))
    packed_shape = (BLOCKS, CORES, groups, cols_pad, 3 * LANES)
    flat_shape = (members, groups, cols_pad, 3 * LANES)
    pad_shape = (CORES, groups, PACK, cols_pad, channels)
    here_shape = (CORES, groups, PACK, cols_here, channels)

    def shape(s, d):
        return jax.ShapeDtypeStruct(s, d)

    index = row_at * col_devs + col_at
    devices = row_devs * col_devs
    all_bits = [2**k for k in range(16) if 2**k < devices]
    cube, outer_bits = all_bits[1:4], all_bits[4:]
    core_line = core.astype(jnp.int32).reshape(1)

    def bit(mask_bit):
        return (index // mask_bit) % 2

    def partner(x, flip):
        return lax.ppermute(x, AXES, [(d, d ^ flip) for d in range(devices)])


    orders = [[cube[(p + k) % 3] for k in range(3)] for p in range(3)]

    def bits(level):
        return jnp.stack([bit(o[level]) for o in orders]).astype(jnp.int32)

    def zipped(kept, got):
        return [x for pair in zip(kept, got) for x in pair]

    def merge(own, got, which, single, after):
        n, (r, c) = len(own), own[0].shape
        out = [shape((n, 2 * r, c), BF)] * 2 if single else [shape((2 * r, c), BF)] * (2 * n)
        return call(
            lambda *refs: merge_kernel(n, single, *refs), zipped(own, got), out, 2.0,
            after=after, prefetch=[which], vmem=34 if single else 12, name="merge",
        )

    class Sum:
        def __init__(self, kept, got):
            self.kept, self.got, self.level = kept, got, 0

        def send(self, arrays):
            self.got = [partner(x, o[self.level]) for x, o in zip(arrays, orders)]

        def halve(self, after=()):
            first, n = self.level == 0, len(orders)
            rows, wide = self.kept[0].shape
            half = rows // n if first else rows // 2
            tiles = 2 if first else 1
            t = half // tiles
            args, specs = [], []
            if first:
                for chunk in range(2 * n):
                    grad, at = divmod(chunk, n)
                    args += [self.kept[grad], self.got[grad]]
                    specs += [pl.BlockSpec((t, wide), lambda i, b, at=at: (at * tiles + i, 0))] * 2
            else:
                for p in range(n):
                    stay = lambda i, b, p=p: (b[p] * tiles + i, 0)
                    leave = lambda i, b, p=p: ((1 - b[p]) * tiles + i, 0)
                    args += [self.kept[p], self.got[p]] * 2
                    specs += [pl.BlockSpec((t, wide), m) for m in (stay, stay, leave, leave)]
            res = call(
                halve_first_kernel if first else halve_kernel,
                args, [shape((half, wide), BF)] * (2 * n), 3.0,
                after=after, prefetch=[bits(self.level)], grid=(tiles,), in_specs=specs,
                out_specs=[pl.BlockSpec((t, wide), lambda i, b: (i, 0))] * (2 * n), vmem=20 if first else 12, name="halve",
            )
            self.kept = res[0::2]
            self.send(res[1::2])
            self.level += 1
            return self.kept[0]

        def settle(self, after=()):
            n = len(orders)
            self.kept = call(
                lambda *refs: settle_kernel(n, *refs), zipped(self.kept, self.got),
                [shape(x.shape, BF) for x in self.kept], 1.0, after=after, name="settle",
            )
            return self.kept[0]

        def join(self, stay, got, after=()):
            n, (r, c) = len(orders), self.kept[0].shape
            self.kept, sent = call(
                lambda *refs: join_kernel(n, *refs), self.kept + [stay, got],
                [shape((n * (r + EXTRA), c), BF)] * 2, 1.5, after=after, name="join",
            )
            self.got = partner(sent, outer_bits[0])
            for m in outer_bits[1:]:
                self.kept, sent = add(self.kept, self.got, BF)
                self.got = partner(sent, m)
            return self.kept

        def part(self, after=()):
            n, (r, c) = len(orders), self.kept.shape
            res = call(
                part_kernel, [self.kept, self.got], [shape((r // n, c), BF)] * (2 * n), 1.5,
                after=after, name="part",
            )
            self.kept = res[:n]
            self.level = len(cube) - 1
            self.send(res[n:])
            return self.kept[0]

        def double(self, after=()):
            n, (r, c), single = len(orders), self.kept[0].shape, self.level == 0
            res = merge(self.kept, self.got, bits(self.level), single, after)
            self.level -= 1
            if not single:
                self.kept = res[:n]
                self.send(res[n:])
                return self.kept[0]
            self.kept, sent = (x.reshape(2 * n * r, c) for x in res)
            self.got = partner(sent, 1)
            return self.kept

        def widen(self, done, after=()):
            rows, c = self.kept.shape
            chunk = rows // (len(orders) * BLOCKS)
            t = 2 * (chunk - EXTRA)
            steps = rows // chunk // 4
            full_rows = CORES * steps * t
            x = self.got if done else self.kept
            full = [shape((full_rows, c), F32), shape((c, full_rows), F32)]
            extra = [shape((2 * steps, EXTRA, c), BF)] * 2
            at = lambda i, h: (1 - h[0] if done else h[0]) * steps + i
            return call(
                widen_kernel, [x, x] + done[:2], full + extra, 5.0, after=after,
                prefetch=[core_line], grid=(steps,),
                in_specs=[
                    pl.BlockSpec((2 * chunk, c), lambda i, h: (i, 0)),
                    pl.BlockSpec((2 * chunk, c), lambda i, h: (steps + i, 0)),
                ] + [pl.BlockSpec(memory_space=pl.ANY)] * len(done[:2]),
                out_specs=[
                    pl.BlockSpec((t, c), lambda i, h: (at(i, h), 0)),
                    pl.BlockSpec((c, t), lambda i, h: (0, at(i, h))),
                ] + [pl.BlockSpec((2, EXTRA, c), lambda i, h: (i, 0, 0))] * 2,
                input_output_aliases={3: 0, 4: 1} if done else {}, hbm=(0, 1), name="widen",
            )

    def add(x, y, dtype, after=()):
        return call(add_kernel, [x, y], [shape(x.shape, dtype)] * 2, 1.0, after=after, name="add")

    class Tail:
        def __init__(self, x):
            self.bits = list(all_bits)
            self.x, self.got = x[0], partner(x[1], self.bits[0])

        def step(self, after=()):
            self.x, sent = add(self.x, self.got, F32, after)
            self.bits.pop(0)
            if self.bits:
                self.got = partner(sent, self.bits[0])
            return self.x


    turned_shape = shape((cols_here, rows_here, channels), F32)
    turned_spec = pl.BlockSpec(turned_shape.shape, lambda i: (0, 0, 0))

    def turn_back(x):
        return x.swapaxes(0, 1)

    def lon_forward(cells, table, after=()):
        return call(
            lambda *refs: lon_kernel(col_devs, row_group, *refs),
            [cells.reshape(flat_shape), table],
            [shape((half_rows, lats, LANES), BF)] * 2, 5.5, after=after,
            scratch_shapes=[pltpu.VMEM((all_rows * lats, LANES), F32)],
            vmem=24, name="lon_forward",
        )

    def lon_backward(pieces, table, after=()):
        return call(
            lambda *refs: lon_back_kernel(
                col_devs, row_group, len(pieces), refs[len(pieces)], *refs[: len(pieces)], refs[-1]
            ),
            [*pieces, table], shape(flat_shape, BF), 3.5, after=after, vmem=16, name="lon_backward",
        )

    def big_weight(w):
        w = lax.dynamic_index_in_dim(w, mine, 1, keepdims=False)
        gap = LANES - block
        w = jnp.pad(w, ((0, 0), (0, gap), (0, gap)))
        return jnp.concatenate(
            [jnp.concatenate([w[0], w[1]], 1), jnp.concatenate([-w[1], w[0]], 1)], 0
        )

    def big_bias(b):
        b = lax.dynamic_index_in_dim(b.reshape(2, BLOCKS, block), mine, 1, keepdims=False)
        return jnp.pad(b, ((0, 0), (0, LANES - block))).reshape(1, 2 * LANES)

    wa, wb = big_weight(mix_weight_a), big_weight(mix_weight_b)
    ba, bb = big_bias(mix_bias_a), big_bias(mix_bias_b)

    normed, send = call(
        first_kernel, [x5, mask, first_gain, first_shift],
        [shape(pad_shape, BF), shape(packed_shape, BF)], 6.0, hbm=(0, 1),
        grid=(lat_steps,), in_specs=[here_spec, mask_spec, line_spec, line_spec],
        out_specs=[pad_spec, packed_spec], vmem=16, name="first_norm",
    )
    cells = exchange(send.reshape(flat_shape))

    own, other = lon_forward(cells, lon_fwd)
    other = swap(other)
    own, other, modes = call(
        mix_kernel, [own, other, lat_fwd, lat_inv, wa, ba, wb, bb],
        [shape((lats, half_rows, LANES), BF)] * 2
        + [shape((slots_pad // WIDE, WIDE * LAT, 2 * LANES), BF)], 22.0,
        scratch_shapes=[pltpu.VMEM((2 * lats * half_rows, LANES), F32)], vmem=32, hbm=(2,), name="mix",
    )
    other = swap(other)
    lon_out = lon_backward([own, other], lon_winv)
    got = exchange(lon_out)

    cot_pad = call(
        pad_kernel, [cot5], shape(pad_shape, BF), 2.0, after=[lon_out], grid=(lat_steps,),
        in_specs=[here_spec], out_specs=[pad_spec], name="pad",
    )

    resid, tokens = call(
        second_kernel,
        [x5, normed, mask, got.reshape(packed_shape), row(second_gain), row(second_shift)],
        [shape(pad_shape, F32), shape(pad_shape, BF)], 8.5, after=[cot_pad],
        grid=(lat_steps,),
        in_specs=[here_spec, pad_spec, mask_spec, packed_spec, row_spec, row_spec],
        out_specs=[pad_spec, pad_spec], vmem=40, pin=(0, 1), name="second_norm",
    )
    tokens2, cot2 = tokens.reshape(-1, channels), cot_pad.reshape(-1, channels)
    count, hidden = tokens2.shape[0], expand_weight.shape[1]
    tile = hidden // 6
    all_tok = pl.BlockSpec((count, channels), lambda i: (0, 0))
    by_col = lambda n: pl.BlockSpec((n, tile), lambda i: (0, i))
    by_row = pl.BlockSpec((tile, channels), lambda i: (i, 0))
    act, gpre, gtok, g_ebias = call(
        chain_kernel,
        [tokens2, cot2, expand_weight, row(expand_bias), reduce_weight],
        [
            shape((count, hidden), BF), shape((count, hidden), BF),
            shape((count, channels), BF), shape((1, hidden), F32),
        ],
        25.0, grid=(6,),
        in_specs=[all_tok, all_tok, by_col(channels), by_col(1), by_row],
        out_specs=[by_col(count), by_col(count), all_tok, by_col(1)], scratch_shapes=[pltpu.VMEM((count, channels), F32)], vmem=46, hbm=(0, 1, 2), pin=True, name="mlp_chain",
    )

    halves = 3
    assert halves * CORES * tile == hidden

    def weight_grad(left, right, own, after, name):
        at = lambda i, c: (c[0] if own else 1 - c[0]) * halves + i
        return call(
            weight_grad_kernel, [left, right],
            [shape((halves * tile, channels), BF), shape((8, LANES), F32)], 5.0,
            after=after, prefetch=[core_line], grid=(halves,),
            in_specs=[
                pl.BlockSpec((count, tile), lambda i, c: (0, at(i, c))),
                pl.BlockSpec((count, channels), lambda i, c: (0, 0)),
            ],
            out_specs=[
                pl.BlockSpec((tile, channels), lambda i, c: (i, 0)),
                pl.BlockSpec((8, LANES), lambda i, c: (0, 0)),
            ],
            vmem=20, hbm=(0,) if own else (), name=name,
        )

    one_row = shape((1, channels), F32)
    grad_resid, send, g_gain2, g_shift2, g_rbias = call(
        third_kernel,
        [resid, gtok.reshape(pad_shape), cot_pad, mask, row(second_gain)],
        [shape(pad_shape, BF), shape(packed_shape, BF)] + [one_row] * 3, 9.0,
        grid=(lat_steps,), in_specs=[pad_spec, pad_spec, pad_spec, mask_spec, row_spec],
        out_specs=[pad_spec, packed_spec, row_spec, row_spec, row_spec], vmem=56, name="second_back",
    )
    cells = exchange(send.reshape(flat_shape))

    sent_r, token = weight_grad(act, cot2, False, [g_gain2], "reduce_grad")
    sent_e, token = weight_grad(gpre, tokens2, False, [token], "expand_grad")
    kept_r, token = weight_grad(act, cot2, True, [token], "reduce_grad")
    kept_e, token = weight_grad(gpre, tokens2, True, [token], "expand_grad")
    sums = Sum([kept_r, kept_e], [partner(sent_r, 1), partner(sent_e, 1)])

    own, other = lon_forward(cells, lon_wfwd, after=[token])
    other = swap(other)
    token = sums.halve(after=[own])
    run = half_rows // SPLIT
    pieces, grads = [], []
    grad_shape = shape((4 * LANES + 16, 2 * LANES), F32)
    for k in range(SPLIT):
        here = pl.BlockSpec((run, lats, LANES), lambda i, k=k: (k, 0, 0))
        steps = modes.shape[0] // SPLIT
        const = lambda x: pl.BlockSpec(x.shape, lambda i: (0, 0))
        o, t, g = call(
            mix_back_kernel, [own, other, modes, lat_fwd, lat_inv, wa, ba, wb, bb] + grads,
            [shape((lats, run, LANES), BF)] * 2 + [grad_shape], 13.0,
            after=[token],
            in_specs=[
                here, here, pl.BlockSpec((steps,) + modes.shape[1:], lambda i, k=k: (k, 0, 0)),
            ] + [const(x) for x in (lat_fwd, lat_inv, wa, ba, wb, bb, *grads)],
            scratch_shapes=[pltpu.VMEM((2 * lats * run, LANES), F32)], vmem=34, name="mix_back",
        )
        pieces.append((o, swap(t)))
        grads = [g]
        token = sums.halve(after=[o])
    token = sums.halve(after=[token])
    token = sums.settle(after=[token])
    send = lon_backward(
        [p[0] for p in pieces] + [p[1] for p in pieces], lon_inv, after=[token]
    )
    got = exchange(send)
    stay, leave = call(
        lambda *refs: collect_kernel(block, *refs), grads,
        [shape((3 * EXTRA, channels), F32)] * 2, 1.5, after=[send], prefetch=[core_line],
        name="collect",
    )
    token = sums.join(stay, partner(leave, 1))

    outputs, token = call(
        branch_kernel,
        [act.reshape(CORES, groups, PACK, cols_pad, hidden), reduce_weight, resid, row(reduce_bias)],
        [turned_shape, shape((8, LANES), F32)], 10.0, after=[token], grid=(groups,),
        in_specs=[
            both_spec(cols_pad, hidden), pl.BlockSpec((hidden, channels), lambda i: (0, 0)),
            both_spec(cols_pad, channels), row_spec,
        ],
        out_specs=[turned_spec, pl.BlockSpec((8, LANES), lambda i: (0, 0))], vmem=32, name="branch",
    )

    touched = call(
        touch_kernel, [], shape((8, LANES), F32), 0.5, after=[got, token], name="touch"
    )
    token = sums.part(after=[touched])
    token = sums.double(after=[token])
    token = sums.double(after=[token])

    grad_inputs, g_gain1, g_shift1 = call(
        last_kernel, [x5, grad_resid, mask, got.reshape(packed_shape), row(first_gain)],
        [turned_shape] + [one_row] * 2, 9.0, after=[token],
        grid=(lat_steps,), in_specs=[here_spec, pad_spec, mask_spec, packed_spec, row_spec],
        out_specs=[turned_spec, row_spec, row_spec], vmem=36, pin=(0, 1), name="first_back",
    )
    tail_sum = Tail(
        call(
            tail_kernel, [g_gain1, g_shift1, g_gain2, g_shift2, g_rbias, g_ebias],
            [shape((1, 5 * channels + hidden), F32)] * 2, 1.0, name="tail",
        )
    )
    token = tail_sum.step()
    token = sums.double(after=[token])
    token = tail_sum.step(after=[token])
    own_done = sums.widen([], after=[token])
    token = tail_sum.step(after=[own_done[2]])
    g_reduce, g_expand, *got_extra = sums.widen(own_done, after=[token])
    token = got_extra[0]
    while tail_sum.bits:
        token = tail_sum.step(after=[token])
    weight_out, bias_out = shape(mix_weight_a.shape, F32), shape(mix_bias_a.shape, F32)
    g_wa, g_wb, g_ba, g_bb = call(
        lambda *refs: spread_kernel(block, *refs), own_done[2:] + got_extra,
        [weight_out, weight_out, bias_out, bias_out], 3.0, prefetch=[core_line], name="spread",
    )

    tail = tail_sum.x
    g_gain1, g_shift1, g_gain2, g_shift2, g_rbias = (
        tail[0, k * channels : (k + 1) * channels] for k in range(5)
    )
    g_ebias = tail[0, 5 * channels :]

    def flat(v):
        return v.reshape(-1)

    return (
        turn_back(outputs), turn_back(grad_inputs),
        flat(g_gain1), flat(g_shift1), g_wa, g_ba, g_wb, g_bb, flat(g_gain2), flat(g_shift2),
        g_expand, g_ebias, g_reduce, flat(g_rbias),
    )


def solution(mesh):
    grid = P("rows", "cols", None)
    placed = (grid, P("rows", "cols"), grid) + (P(),) * 12
    return jax.shard_map(
        per_device,
        mesh=mesh,
        in_specs=placed,
        out_specs=(grid, grid) + (P(),) * 12,
        check_vma=False,
    )
```
